32 devices in a mesh: dp: 4 (over z), fsdp: 8 (over y, x, core).
Axes of the slice: x: 2, y: 2, z: 4, core: 2. Of those that a mesh axis runs over, the one named last changes fastest.
Arguments:
- tokens: bfloat16 [32768, 768], P(('dp', 'fsdp')), may hold values from -12 to 12
- lengths: int32 [32], P(('dp', 'fsdp')), may hold values from 64 to 1024, as said below
- qkv_weight: bfloat16 [768, 2304], P('fsdp'), may hold values from -0.21875 to 0.21875
- qkv_bias: bfloat16 [2304], P('fsdp'), may hold values from -1.25 to 1.25
- out_weight: bfloat16 [768, 768], P('fsdp'), may hold values from -1.75 to 1.75
- out_bias: bfloat16 [768], P('fsdp'), may hold values from -1.25 to 1.25
- fc_weight: bfloat16 [768, 3072], P('fsdp'), may hold values from -0.21875 to 0.21875
- fc_bias: bfloat16 [3072], P('fsdp'), may hold values from -1.25 to 1.25
- proj_weight: bfloat16 [3072, 768], P('fsdp'), may hold values from -0.109375 to 0.109375
- proj_bias: bfloat16 [768], P('fsdp'), may hold values from -1.25 to 1.25
- norm1_gain: bfloat16 [768], P('fsdp'), may hold values from 0.5 to 1.5
- norm1_bias: bfloat16 [768], P('fsdp'), may hold values from -1.25 to 1.25
- norm2_gain: bfloat16 [768], P('fsdp'), may hold values from 0.5 to 1.5
- norm2_bias: bfloat16 [768], P('fsdp'), may hold values from -1.25 to 1.25
- feature_map: bfloat16 [768, 128], P('fsdp'), may hold values from -0.75 to 0.75
- cotangent: bfloat16 [32768, 768], P(('dp', 'fsdp')), may hold values from -6 to 6
Outputs:
- block_out: bfloat16 [32768, 768], P(('dp', 'fsdp'))
- input_grad: bfloat16 [32768, 768], P(('dp', 'fsdp'))
- qkvw_grad: float32 [768, 2304], P('fsdp')
- qkb_grad: float32 [1536], P('fsdp')
- vb_grad: float32 [768], P('fsdp')
- outw_grad: float32 [768, 768], P('fsdp')
- outb_grad: float32 [768], P('fsdp')
- fcw_grad: float32 [768, 3072], P('fsdp')
- fcb_grad: float32 [3072], P('fsdp')
- projw_grad: float32 [3072, 768], P('fsdp')
- projb_grad: float32 [768], P('fsdp')
- gain1_grad: float32 [768], P('fsdp')
- bias1_grad: float32 [768], P('fsdp')
- gain2_grad: float32 [768], P('fsdp')
- bias2_grad: float32 [768], P('fsdp')
- fmap_grad: float32 [768, 128], P('fsdp')
The draws below stay inside these ranges and needn't reach their ends.
Inputs may be any that keep to these rules, and one draw needn't show every extreme that they name: Sequence s has lengths[s] real tokens at the start of its 1024 rows; the rest is padding. Some sequence fills its rows and some has exactly 64.
All inputs are finite; a program needn't handle non-finite values.
Results may differ from the reference program's by a relative error of at most 0.03.
Values may be sent and summed in bfloat16 or wider, within the bound.
No kernel may reach another device: no remote copies, remote signals or barrier semaphores. Data moves between devices by JAX's collectives and lax.ppermute only.
A program may use at most 256 MiB of HBM per device.

```python
import jax
import jax.numpy as jnp
from jax import lax

D = 768
HEADS = 12
HD = 64
FF = 3072
SPAN = 64
TOK_DEV = 1024
SHORTEST = 64
SEQS = 32
TOKENS = 32768
N_FSDP = 8


def draw_lengths(key, part):
    key = jax.random.fold_in(key, 11)
    draw_key, pick_key = jax.random.split(key)
    counts = jax.random.randint(draw_key, (SEQS,), SHORTEST, TOK_DEV + 1, dtype=jnp.int32)
    chosen = jax.random.permutation(pick_key, SEQS)
    counts = counts.at[chosen[0]].set(TOK_DEV)
    counts = counts.at[chosen[1]].set(SHORTEST)
    return counts.astype(jnp.int32)


def strengthened(array, own_key, source, target, shards_of, factor):
    def block_of(axis_at):
        return (jnp.arange(array.shape[axis_at]) // (array.shape[axis_at] // shards_of)).reshape((-1,) + (1,) * (array.ndim - 1 - axis_at))

    first = jax.random.permutation(own_key, shards_of)[block_of(target)]
    other_side = (block_of(target) + shards_of // 2) % shards_of
    return jnp.where((block_of(source) == first) | (block_of(source) == other_side), factor * array, array)


def block_scale(stream_key, dims, shards, smallest, high):
    loudness = 1.0
    for dim, shards_of in shards:
        draws = jax.random.uniform(jax.random.fold_in(jax.random.fold_in(stream_key, 6), dim), (shards_of,), jnp.float32, smallest / len(shards), high / len(shards))
        loudness = loudness * jnp.repeat(jnp.exp(draws), dims[dim] // shards_of).reshape((-1,) + (1,) * (len(dims) - 1 - dim))
    return loudness


def gaussian(own_key, dims, scale, reach, shards=(), kind=jnp.bfloat16):
    values = scale * jax.random.normal(own_key, dims, jnp.float32)
    if shards:
        values = values * block_scale(own_key, dims, shards, -0.22, 0.18)
    return jnp.clip(values, -reach, reach).astype(kind)


def heavy_noise(stream_key, shape, deviation, limit, cuts, heavy, held_as=jnp.bfloat16):
    result = deviation * jax.random.normal(stream_key, shape, jnp.float32)
    if cuts:
        result = result * block_scale(stream_key, shape, cuts, -0.22, 0.18)
    return jnp.clip(strengthened(result, jax.random.fold_in(stream_key, 3), *heavy), -limit, limit).astype(held_as)


def setup_inputs(seed: int = 0) -> dict:
    splits = jax.random.split(jax.random.key(seed), 17)
    tokens = heavy_noise(splits[0], (TOKENS, D), 1.0, 12.0, ((0, 32),), (0, 1, 32, 2.75))
    lengths = draw_lengths(jax.random.fold_in(splits[16], 71), 0)
    qkv_weight = gaussian(splits[2], (D, 3 * D), D ** -0.5, 0.21875, ((0, 8),))
    qkv_bias = gaussian(splits[3], (3 * D,), 0.2, 1.25, ((0, 8),))
    out_weight = gaussian(splits[4], (D, D), (D // 64) ** -0.5, 1.75, ((0, 8),))
    out_bias = gaussian(splits[5], (D,), 0.2, 1.25, ((0, 8),))
    fc_weight = gaussian(splits[6], (D, FF), D ** -0.5, 0.21875, ((0, 8),))
    fc_bias = gaussian(splits[7], (FF,), 0.2, 1.25, ((0, 8),))
    proj_weight = gaussian(splits[8], (FF, D), FF ** -0.5, 0.109375, ((0, 8),))
    proj_bias = gaussian(splits[9], (D,), 0.2, 1.25, ((0, 8),))
    norm1_gain = jnp.clip(1.0 + 0.1 * jax.random.normal(splits[10], (D,), jnp.float32), 0.5, 1.5).astype(jnp.bfloat16)
    norm1_bias = gaussian(splits[11], (D,), 0.2, 1.25, ((0, 8),))
    norm2_gain = jnp.clip(1.0 + 0.1 * jax.random.normal(splits[12], (D,), jnp.float32), 0.5, 1.5).astype(jnp.bfloat16)
    norm2_bias = gaussian(splits[13], (D,), 0.2, 1.25, ((0, 8),))
    feature_map = gaussian(splits[14], (D, 2 * HD), HD ** -0.5, 0.75, ((0, 8),))
    cotangent = gaussian(splits[15], (TOKENS, D), 1.0, 6.0, ((0, 32),))
    return dict(tokens=tokens, lengths=lengths, qkv_weight=qkv_weight, qkv_bias=qkv_bias, out_weight=out_weight, out_bias=out_bias, fc_weight=fc_weight, fc_bias=fc_bias, proj_weight=proj_weight, proj_bias=proj_bias, norm1_gain=norm1_gain, norm1_bias=norm1_bias, norm2_gain=norm2_gain, norm2_bias=norm2_bias, feature_map=feature_map, cotangent=cotangent)


@jax.custom_vjp
def low(v):
    return lax.optimization_barrier(v.astype(jnp.bfloat16)).astype(jnp.float32)

@jax.custom_vjp
def low_back(v):
    return v

def low_keep(v):
    return (low(v), None)

def low_pass(kept, grad):
    return (grad,)

def back_keep(v):
    return (v, None)

def back_low(kept, grad):
    return (low(grad),)
low.defvjp(low_keep, low_pass)
low_back.defvjp(back_keep, back_low)
EPSILON = 1e-05
PRECISE = lax.Precision.HIGHEST

def norm_rows(values, scale_row, shift_row):
    middle = lax.optimization_barrier(jnp.mean(values, -1, keepdims=True))
    centred = values - middle
    spread = lax.optimization_barrier(jnp.mean(centred * centred, -1, keepdims=True))
    return centred * lax.rsqrt(spread + EPSILON) * scale_row + shift_row

def feature_pair(logits):
    return jnp.concatenate([jax.nn.softmax(logits, -1), jax.nn.softmax(-logits, -1)], -1)

def earlier_sum(blocks):
    running = jnp.cumsum(blocks, 0)
    return jnp.concatenate([jnp.zeros_like(blocks[:1]), running[:-1]], 0)

def attend(query_feat, key_feat, value_rows, live_rows):
    block_count = TOK_DEV // SPAN
    query_blocks = query_feat.reshape(block_count, SPAN, HEADS, 2 * HD)
    key_blocks = key_feat.reshape(block_count, SPAN, HEADS, 2 * HD)
    value_blocks = value_rows.reshape(block_count, SPAN, HEADS, HD)
    lower_mask = (jnp.arange(SPAN)[:, None] >= jnp.arange(SPAN)[None, :]).astype(jnp.float32)
    scores = low_back(jnp.einsum('nchf,ndhf->nhcd', query_blocks, key_blocks, precision=PRECISE) * lower_mask)
    scores_low = low(scores)
    block_states = low_back(jnp.einsum('ndhf,ndhe->nhfe', key_blocks, value_blocks, precision=PRECISE))
    prior_states = low(earlier_sum(block_states))
    prior_totals = earlier_sum(lax.optimization_barrier(jnp.sum(key_blocks, 1)))
    numerator = low_back(jnp.einsum('nhcd,ndhe->nche', scores_low, value_blocks, precision=PRECISE) + jnp.einsum('nchf,nhfe->nche', query_blocks, prior_states, precision=PRECISE))
    denominator = jnp.swapaxes(lax.optimization_barrier(jnp.sum(scores, -1)), 1, 2) + jnp.einsum('nchf,nhf->nch', query_blocks, prior_totals, precision=PRECISE)
    live_blocks = live_rows.reshape(block_count, SPAN, 1, 1)
    return (numerator / denominator[..., None] * live_blocks).reshape(TOK_DEV, D)

def forward(params, inputs, live_rows):
    wide_qkv, bias_qkv, wide_out, bias_out, wide_fc, bias_fc, wide_proj, bias_proj, gain_one, shift_one, gain_two, shift_two, wide_map = params
    row_count = inputs.shape[0]
    seq_count = row_count // TOK_DEV
    hidden_one = low(norm_rows(inputs, gain_one, shift_one))
    projected = low_back(jnp.dot(hidden_one, wide_qkv, precision=PRECISE) + bias_qkv)
    query_rows = low(projected[:, :D]).reshape(row_count, HEADS, HD)
    key_rows = low(projected[:, D:2 * D]).reshape(row_count, HEADS, HD)
    value_rows = low(projected[:, 2 * D:]).reshape(row_count, HEADS, HD)
    query_map = wide_map[:, :HD].reshape(HEADS, HD, HD)
    key_map = wide_map[:, HD:].reshape(HEADS, HD, HD)
    query_logits = low_back(jnp.einsum('thi,hij->thj', query_rows, query_map, precision=PRECISE))
    key_logits = low_back(jnp.einsum('thi,hij->thj', key_rows, key_map, precision=PRECISE))
    query_feat = low(feature_pair(query_logits))
    key_feat = low(feature_pair(key_logits) * live_rows[:, None, None])
    attended = jax.vmap(attend)(query_feat.reshape(seq_count, TOK_DEV, HEADS, 2 * HD), key_feat.reshape(seq_count, TOK_DEV, HEADS, 2 * HD), value_rows.reshape(seq_count, TOK_DEV, HEADS, HD), live_rows.reshape(seq_count, TOK_DEV))
    attended = low(low_back(attended.reshape(row_count, D)))
    middle_rows = inputs + low_back(jnp.dot(attended, wide_out, precision=PRECISE) + bias_out)
    hidden_two = low(norm_rows(middle_rows, gain_two, shift_two))
    pre_act = low_back(jnp.dot(hidden_two, wide_fc, precision=PRECISE) + bias_fc)
    activated = low(jax.nn.gelu(pre_act, approximate=True))
    return middle_rows + low_back(jnp.dot(activated, wide_proj, precision=PRECISE) + bias_proj)

def reference(tokens, lengths, qkv_weight, qkv_bias, out_weight, out_bias, fc_weight, fc_bias, proj_weight, proj_bias, norm1_gain, norm1_bias, norm2_gain, norm2_bias, feature_map, cotangent):
    params = tuple((weight.astype(jnp.float32) for weight in (qkv_weight, qkv_bias, out_weight, out_bias, fc_weight, fc_bias, proj_weight, proj_bias, norm1_gain, norm1_bias, norm2_gain, norm2_bias, feature_map)))
    positions = jnp.arange(TOK_DEV, dtype=jnp.int32)
    live_rows = (positions[None, :] < lengths[:, None]).astype(jnp.float32)
    group_size = min(N_FSDP, max(1, 4096 // TOK_DEV))
    group_count = SEQS // group_size
    inputs = tokens.astype(jnp.float32).reshape(group_count, group_size * TOK_DEV, D)
    upstream = cotangent.astype(jnp.float32).reshape(group_count, group_size * TOK_DEV, D)
    live_groups = live_rows.reshape(group_count, group_size * TOK_DEV)

    def one_group(running, pieces):
        inputs_part, upstream_part, live_part = pieces

        def tied_forward(weights, input_rows):
            return forward(weights, input_rows, live_part)
        outputs, pullback = jax.vjp(tied_forward, params, inputs_part)
        weight_grads, input_grads = pullback(upstream_part)
        running = jax.tree.map(jnp.add, running, weight_grads)
        return (running, (outputs.astype(jnp.bfloat16), input_grads.astype(jnp.bfloat16)))
    initial = tuple((jnp.zeros_like(weight) for weight in params))
    summed, (block_rows, grad_rows) = lax.scan(one_group, initial, (inputs, upstream, live_groups))
    qkvw_grad, qkvb_full, outw_grad, outb_grad, fcw_grad, fcb_grad, projw_grad, projb_grad, gain1_grad, bias1_grad, gain2_grad, bias2_grad, fmap_grad = summed
    qkb_grad = qkvb_full[:2 * D]
    vb_grad = qkvb_full[2 * D:]
    return (block_rows.reshape(TOKENS, D), grad_rows.reshape(TOKENS, D), qkvw_grad, qkb_grad, vb_grad, outw_grad, outb_grad, fcw_grad, fcb_grad, projw_grad, projb_grad, gain1_grad, bias1_grad, gain2_grad, bias2_grad, fmap_grad)
```

```python
import functools

import jax
import jax.numpy as jnp
from jax import lax
from jax.experimental import pallas as pl
from jax.experimental.pallas import tpu as pltpu
from jax.sharding import PartitionSpec as P

D = 768
HEADS = 12
HD = 64
PAIRS = HEADS // 2
FF = 3072
ROWS = 256
CHUNK = 128
EPSILON = 1e-05
SAFE = 60.0
VMEM = 56 * 1024 * 1024
F32 = jnp.float32
BF16 = jnp.bfloat16


def nn(left, right):
    return lax.dot_general(left, right, (((1,), (0,)), ((), ())), preferred_element_type=F32)


def nt(left, right):
    return lax.dot_general(left, right, (((1,), (1,)), ((), ())), preferred_element_type=F32)


def tn(left, right):
    return lax.dot_general(left, right, (((0,), (0,)), ((), ())), preferred_element_type=F32)


def params(*semantics):
    return pltpu.CompilerParams(vmem_limit_bytes=VMEM, dimension_semantics=semantics or None)


def lanes(shape):
    return lax.broadcasted_iota(jnp.int32, shape, 1)


def inverse(values):
    first = pl.reciprocal(values, approx=True)
    return first * (2.0 - values * first)


def normalized(values):
    middle = jnp.mean(values, -1, keepdims=True)
    centred = values - middle
    spread = jnp.mean(centred * centred, -1, keepdims=True)
    scale = lax.rsqrt(spread + EPSILON)
    return centred * scale, scale


def norm_back(grad, gain, unit, scale):
    scaled = grad * gain
    first = jnp.mean(scaled, -1, keepdims=True)
    second = jnp.mean(scaled * unit, -1, keepdims=True)
    return (scaled - first - unit * second) * scale


def swap_halves(values):
    return pltpu.roll(values, 64, 1)


def block_ones(size):
    row = lax.broadcasted_iota(jnp.int32, (size, size), 0) // HD
    col = lax.broadcasted_iota(jnp.int32, (size, size), 1) // HD
    return jnp.where(row == col, 1.0, 0.0).astype(BF16)


def build_maps(map_ref, fq, fk):
    fq[...] = jnp.zeros_like(fq)
    fk[...] = jnp.zeros_like(fk)
    low = lanes((HD, 2 * HD)) < HD
    for head in range(HEADS):
        block = map_ref[head * HD : (head + 1) * HD, :].astype(F32)
        turned = swap_halves(block)
        row, col = (head % 2) * HD, (head % 2) * 2 * HD
        fq[head // 2, row : row + HD, col : col + 2 * HD] = jnp.where(low, block, -turned).astype(BF16)
        fk[head // 2, row : row + HD, col : col + 2 * HD] = jnp.where(low, turned, -block).astype(BF16)


def qkv_kernel(
    len_ref, tok_ref, w_ref, bias_ref, gain_ref, shift_ref, map_ref,
    h_ref, q_ref, k_ref, v_ref, pq_ref, pk_ref, fq, fk, ones, u,
):
    step = pl.program_id(0)

    @pl.when(step == 0)
    def _():
        build_maps(map_ref, fq, fk)
        ones[...] = block_ones(4 * HD)

    unit, _ = normalized(tok_ref[...].astype(F32))
    h = (unit * gain_ref[...] + shift_ref[...]).astype(BF16)
    h_ref[...] = h
    for part, (out, maps) in enumerate(((q_ref, fq), (k_ref, fk), (v_ref, None))):
        cols = slice(part * D, (part + 1) * D)
        rows = (nn(h, w_ref[:, cols]) + bias_ref[:, cols]).astype(BF16)
        out[...] = rows
        if maps is None:
            continue
        for pair in range(PAIRS):
            u[:, part * 2 * D + pair * 256 : part * 2 * D + (pair + 1) * 256] = nn(
                rows[:, pair * 128 : (pair + 1) * 128], maps[pair]
            )

    @pl.when(jnp.max(u[...]) > SAFE)
    def _():
        for group in range(4 * HEADS):
            cols = slice(group * HD, (group + 1) * HD)
            piece = u[:, cols]
            u[:, cols] = piece - jnp.max(piece, -1, keepdims=True)

    rows = step * ROWS + lax.broadcasted_iota(jnp.int32, (ROWS, 1), 0)
    live = (rows < len_ref[0]).astype(F32)
    for part, out in enumerate((pq_ref, pk_ref)):
        for pair in range(PAIRS):
            cols = slice(pair * 256, (pair + 1) * 256)
            e = jnp.exp(u[:, part * 2 * D + pair * 256 : part * 2 * D + (pair + 1) * 256])
            total = nn(e.astype(BF16), ones[...])
            share = e * inverse(total)
            if part == 1:
                share = share * live
            out[:, cols] = share.astype(BF16)


def whole(shape, single=True):
    zeros = (0,) * len(shape)
    if single:
        return pl.BlockSpec(shape, lambda *_: zeros, pipeline_mode=pl.Buffered(1))
    return pl.BlockSpec(shape, lambda *_: zeros)


def rows_of(count, width):
    return pl.BlockSpec((count, width), lambda i, *_: (i, 0))


SMEM = pl.BlockSpec(memory_space=pltpu.SMEM)


def cost(flops, size, trans=0):
    return pl.CostEstimate(flops=int(flops), bytes_accessed=int(size), transcendentals=int(trans))


def project(lengths, tokens, w, bias, gain, shift, fmap):
    count = tokens.shape[0]
    shape = lambda width: jax.ShapeDtypeStruct((count, width), BF16)
    return pl.pallas_call(
        qkv_kernel,
        name="project",
        grid=(count // ROWS,),
        in_specs=[
            SMEM, rows_of(ROWS, D), whole((D, 3 * D)), whole((1, 3 * D)), whole((1, D)), whole((1, D)), whole((D, 2 * HD)),
        ],
        out_specs=[rows_of(ROWS, D)] * 4 + [rows_of(ROWS, 2 * D)] * 2,
        out_shape=[shape(D)] * 4 + [shape(2 * D)] * 2,
        scratch_shapes=[
            pltpu.VMEM((PAIRS, 128, 256), BF16), pltpu.VMEM((PAIRS, 128, 256), BF16),
            pltpu.VMEM((256, 256), BF16), pltpu.VMEM((ROWS, 4 * D), F32),
        ],
        compiler_params=params("arbitrary"),
        cost_estimate=cost(2 * count * D * 3 * D, 14 * count * D + 6 * D * D, 4 * count * D),
    )(lengths, tokens, w, bias, gain, shift, fmap)


def value_pair(v_pair):
    low = lanes(v_pair.shape) < HD
    wide = v_pair.astype(F32)
    return (
        jnp.where(low, wide, 1.0).astype(BF16),
        jnp.where(low, swap_halves(wide), 1.0).astype(BF16),
    )


def attend_kernel(len_ref, pq_ref, pk_ref, v_ref, o_ref, rd_ref, s_ref, state):
    step = pl.program_id(0)

    @pl.when(step == 0)
    def _():
        state[...] = jnp.zeros_like(state)

    row = lax.broadcasted_iota(jnp.int32, (CHUNK, CHUNK), 0)
    col = lax.broadcasted_iota(jnp.int32, (CHUNK, CHUNK), 1)
    causal = row >= col
    low = col < HD
    live = (step * CHUNK + row < len_ref[0]).astype(F32)
    for pair in range(PAIRS):
        values = value_pair(v_ref[:, pair * 128 : (pair + 1) * 128])
        sums = []
        for half in range(2):
            head = 2 * pair + half
            cols = slice(head * 128, (head + 1) * 128)
            pq, pk, vx = pq_ref[:, cols], pk_ref[:, cols], values[half]
            prior = state[head].astype(BF16)
            s_ref[0, head] = prior
            scores = jnp.where(causal, nt(pq, pk), 0.0).astype(BF16)
            sums.append(
                nn(jnp.concatenate([scores, pq], 1), jnp.concatenate([vx, prior], 0))
            )
            state[head] += tn(pk, vx)
        numer = jnp.where(low, sums[0], swap_halves(sums[1]))
        denom = jnp.where(low, swap_halves(sums[0]), sums[1])
        rd = live / denom
        rd_ref[:, pair * 128 : (pair + 1) * 128] = rd
        o_ref[:, pair * 128 : (pair + 1) * 128] = (numer * rd).astype(BF16)


def attend(lengths, pq, pk, v):
    count = v.shape[0]
    steps = count // CHUNK
    return pl.pallas_call(
        attend_kernel,
        name="attend",
        grid=(steps,),
        in_specs=[SMEM, rows_of(CHUNK, 2 * D), rows_of(CHUNK, 2 * D), rows_of(CHUNK, D)],
        out_specs=[
            rows_of(CHUNK, D), rows_of(CHUNK, D), pl.BlockSpec((1, HEADS, 128, 128), lambda i: (i, 0, 0, 0)),
        ],
        out_shape=[
            jax.ShapeDtypeStruct((count, D), BF16),
            jax.ShapeDtypeStruct((count, D), F32),
            jax.ShapeDtypeStruct((steps, HEADS, 128, 128), BF16),
        ],
        scratch_shapes=[pltpu.VMEM((HEADS, 128, 128), F32)],
        compiler_params=params("arbitrary"),
        cost_estimate=cost(2 * count * HEADS * 128 * 512, 20 * count * D),
    )(lengths, pq, pk, v)


CUBE = 0.044715
ROOT = 0.7978845608028654


def widen_kernel(
    o_ref, tok_ref, wo_ref, bo_ref, gain_ref, shift_ref, wf_ref, bf_ref, x1_ref, h2_ref, g_ref, slope_ref
):
    x1 = tok_ref[...].astype(F32) + (nn(o_ref[...], wo_ref[...]) + bo_ref[...])
    x1_ref[...] = x1
    unit, _ = normalized(x1)
    h2 = (unit * gain_ref[...] + shift_ref[...]).astype(BF16)
    h2_ref[...] = h2
    for part in range(4):
        cols = slice(part * D, (part + 1) * D)
        f = nn(h2, wf_ref[:, cols]) + bf_ref[:, cols]
        square = f * f
        bend = jnp.tanh(f * (ROOT + (ROOT * CUBE) * square))
        half = 0.5 * f
        g_ref[:, cols] = (half + half * bend).astype(BF16)
        slope = (0.5 + 0.5 * bend) + half * (1.0 - bend * bend) * (ROOT + (3.0 * ROOT * CUBE) * square)
        slope_ref[:, cols] = slope.astype(BF16)


def widen(o, tokens, wo, bo, gain, shift, wf, bf):
    count = tokens.shape[0]
    return pl.pallas_call(
        widen_kernel,
        name="widen",
        grid=(count // ROWS,),
        in_specs=[
            rows_of(ROWS, D), rows_of(ROWS, D), whole((D, D)), whole((1, D)), whole((1, D)), whole((1, D)),
            whole((D, FF)), whole((1, FF)),
        ],
        out_specs=[rows_of(ROWS, D), rows_of(ROWS, D), rows_of(ROWS, FF), rows_of(ROWS, FF)],
        out_shape=[
            jax.ShapeDtypeStruct((count, D), F32), jax.ShapeDtypeStruct((count, D), BF16),
            jax.ShapeDtypeStruct((count, FF), BF16), jax.ShapeDtypeStruct((count, FF), BF16),
        ],
        compiler_params=params("arbitrary"),
        cost_estimate=cost(2 * count * D * 5 * D, 26 * count * D + 10 * D * D, count * FF),
    )(o, tokens, wo, bo, gain, shift, wf, bf)


def add_columns(step, out, values):
    total = jnp.sum(values, 0, keepdims=True)

    @pl.when(step == 0)
    def _():
        out[...] = total

    @pl.when(step > 0)
    def _():
        out[...] += total


def ffn_back_kernel(
    cot_ref, slope_ref, x1_ref, wp_ref, wf_ref, wo_ref, gain_ref,
    df_ref, dx1_ref, da_ref, do_ref, projb_ref, fcb_ref, gain2_ref, bias2_ref, outb_ref,
):
    step = pl.program_id(0)
    cot = cot_ref[...]
    total = jnp.zeros((ROWS, D), F32)
    for part in range(4):
        cols = slice(part * D, (part + 1) * D)
        df = (nt(cot, wp_ref[cols, :]) * slope_ref[:, cols].astype(F32)).astype(BF16)
        df_ref[:, cols] = df
        add_columns(step, fcb_ref.at[:, cols], df.astype(F32))
        total = total + nt(df, wf_ref[:, cols])
    unit, scale = normalized(x1_ref[...])
    wide = cot.astype(F32)
    dx1 = wide + norm_back(total, gain_ref[...], unit, scale)
    dx1_ref[...] = dx1
    da = dx1.astype(BF16)
    da_ref[...] = da
    do_ref[...] = nt(da, wo_ref[...]).astype(BF16)
    add_columns(step, projb_ref, wide)
    add_columns(step, gain2_ref, total * unit)
    add_columns(step, bias2_ref, total)
    add_columns(step, outb_ref, da.astype(F32))


def ffn_back(cot, slope, x1, wp, wf, wo, gain):
    count = cot.shape[0]
    rows = lambda width, kind=BF16: jax.ShapeDtypeStruct((count, width), kind)
    column = lambda width: jax.ShapeDtypeStruct((1, width), F32)
    return pl.pallas_call(
        ffn_back_kernel,
        name="ffn_back",
        grid=(count // ROWS,),
        in_specs=[
            rows_of(ROWS, D), rows_of(ROWS, FF), rows_of(ROWS, D), whole((FF, D)), whole((D, FF)), whole((D, D)), whole((1, D)),
        ],
        out_specs=[rows_of(ROWS, FF), rows_of(ROWS, D), rows_of(ROWS, D), rows_of(ROWS, D)]
        + [whole((1, D), False), whole((1, FF), False)]
        + [whole((1, D), False)] * 3,
        out_shape=[rows(FF), rows(D, F32), rows(D), rows(D), column(D), column(FF), column(D), column(D), column(D)],
        compiler_params=params("arbitrary"),
        cost_estimate=cost(2 * count * D * 9 * D, 30 * count * D + 18 * D * D),
    )(cot, slope, x1, wp, wf, wo, gain)


def attend_back_kernel(
    do_ref, rd_ref, o_ref, pq_ref, pk_ref, v_ref, s_ref, q_ref, k_ref, map_ref,
    dproj_ref, sums_ref, fmap_ref, fq, fk, ones, state, gq, gk,
):
    step = pl.program_id(0)

    @pl.when(step == 0)
    def _():
        build_maps(map_ref, fq, fk)
        ones[...] = block_ones(4 * HD)
        state[...] = jnp.zeros_like(state)
        gq[...] = jnp.zeros_like(gq)
        gk[...] = jnp.zeros_like(gk)

    row = lax.broadcasted_iota(jnp.int32, (CHUNK, CHUNK), 0)
    col = lax.broadcasted_iota(jnp.int32, (CHUNK, CHUNK), 1)
    causal = row >= col
    below = row <= col
    low = col < HD
    for pair in range(PAIRS):
        cols = slice(pair * 128, (pair + 1) * 128)
        numer_grad = (do_ref[:, cols].astype(F32) * rd_ref[:, cols]).astype(BF16).astype(F32)
        product = numer_grad * o_ref[:, cols].astype(F32)
        coarse = product.astype(BF16)
        fine = (product - coarse.astype(F32)).astype(BF16)
        dot_ones = ones[0:128, 0:128]
        denom_grad = -nn(jnp.concatenate([coarse, fine], 1), jnp.concatenate([dot_ones, dot_ones], 0))
        turned_grad = swap_halves(numer_grad)
        values = value_pair(v_ref[:, cols])
        grads = []
        for numer, denom in ((numer_grad, swap_halves(denom_grad)), (turned_grad, denom_grad)):
            rounded = denom.astype(BF16).astype(F32)
            tail = jnp.where(col == HD, rounded, jnp.where(col == HD + 1, denom - rounded, 0.0))
            grads.append(jnp.where(low, numer, tail).astype(BF16))
        query_grads, key_grads, value_grads = [], [], []
        for half in range(2):
            head = 2 * pair + half
            wide = slice(head * 128, (head + 1) * 128)
            pq, pk, vx, dn = pq_ref[:, wide], pk_ref[:, wide], values[half], grads[half]
            later = state[head].astype(BF16)
            scores_t = jnp.where(below, nt(pk, pq), 0.0).astype(BF16)
            dscores = jnp.where(causal, nt(dn, vx), 0.0).astype(BF16)
            dscores_t = jnp.where(below, nt(vx, dn), 0.0).astype(BF16)
            query_grads.append(nn(dscores, pk) + nt(dn, s_ref[0, head]))
            key_grads.append(nn(dscores_t, pq) + nt(vx, later))
            value_grads.append(nn(jnp.concatenate([scores_t, pk], 1), jnp.concatenate([dn, later], 0)))
            state[head] += tn(pq, dn)
        dv = jnp.where(low, value_grads[0], swap_halves(value_grads[1])).astype(BF16)
        dproj_ref[:, 2 * D + pair * 128 : 2 * D + (pair + 1) * 128] = dv
        both = slice(pair * 256, (pair + 1) * 256)
        for part, (grad, feat_ref, rows_ref, maps, total) in enumerate(
            ((query_grads, pq_ref, q_ref, fq, gq), (key_grads, pk_ref, k_ref, fk, gk))
        ):
            grad = jnp.concatenate(grad, 1)
            feat = feat_ref[:, both].astype(F32)
            inner = nn((grad * feat).astype(BF16), ones[...])
            logit = (feat * (grad - inner)).astype(BF16)
            dproj_ref[:, part * D + pair * 128 : part * D + (pair + 1) * 128] = nt(logit, maps[pair]).astype(BF16)
            total[pair] += tn(rows_ref[:, cols], logit)
    add_columns(step, sums_ref, dproj_ref[...].astype(F32))

    @pl.when(step == pl.num_programs(0) - 1)
    def _():
        first = lanes((HD, 2 * HD)) < HD
        for head in range(HEADS):
            r, c = (head % 2) * HD, (head % 2) * 2 * HD
            bq = gq[head // 2, r : r + HD, c : c + 2 * HD]
            bk = gk[head // 2, r : r + HD, c : c + 2 * HD]
            fmap_ref[head * HD : (head + 1) * HD, :] = jnp.where(first, bq - swap_halves(bq), swap_halves(bk) - bk)


def attend_back(do, rd, o, pq, pk, v, s, q, k, fmap):
    count = v.shape[0]
    steps = count // CHUNK
    back = lambda width: pl.BlockSpec((CHUNK, width), lambda i: (steps - 1 - i, 0))
    return pl.pallas_call(
        attend_back_kernel,
        name="attend_back",
        grid=(steps,),
        in_specs=[
            back(D), back(D), back(D), back(2 * D), back(2 * D), back(D),
            pl.BlockSpec((1, HEADS, 128, 128), lambda i: (steps - 1 - i, 0, 0, 0)),
            back(D), back(D), whole((D, 2 * HD)),
        ],
        out_specs=[back(3 * D), whole((1, 3 * D), False), whole((D, 2 * HD), False)],
        out_shape=[
            jax.ShapeDtypeStruct((count, 3 * D), BF16), jax.ShapeDtypeStruct((1, 3 * D), F32),
            jax.ShapeDtypeStruct((D, 2 * HD), F32),
        ],
        scratch_shapes=[
            pltpu.VMEM((PAIRS, 128, 256), BF16), pltpu.VMEM((PAIRS, 128, 256), BF16), pltpu.VMEM((256, 256), BF16),
            pltpu.VMEM((HEADS, 128, 128), F32), pltpu.VMEM((PAIRS, 128, 256), F32), pltpu.VMEM((PAIRS, 128, 256), F32),
        ],
        compiler_params=params("arbitrary"),
        cost_estimate=cost(2 * count * HEADS * 128 * 128 * 14, 40 * count * D),
    )(do, rd, o, pq, pk, v, s, q, k, fmap)


def outer_kernel(left_ref, right_ref, out_ref):
    out_ref[...] = tn(left_ref[...], right_ref[...]).astype(BF16)


def outer(left, right, tile=256):
    count, wide = left.shape
    across = right.shape[1]
    return pl.pallas_call(
        outer_kernel,
        name="outer",
        grid=(wide // tile,),
        in_specs=[pl.BlockSpec((count, tile), lambda i: (0, i)), whole((count, across))],
        out_specs=pl.BlockSpec((tile, across), lambda i: (i, 0)),
        out_shape=jax.ShapeDtypeStruct((wide, across), BF16),
        compiler_params=params("arbitrary"),
        cost_estimate=cost(2 * count * wide * across, 2 * (count * (wide + across) + wide * across)),
    )(left, right)


def input_back_kernel(dproj_ref, w_ref, tok_ref, dx1_ref, gain_ref, out_ref, gain1_ref, bias1_ref):
    step = pl.program_id(0)
    grad = nt(dproj_ref[...], w_ref[...])
    unit, scale = normalized(tok_ref[...].astype(F32))
    out_ref[...] = (dx1_ref[...] + norm_back(grad, gain_ref[...], unit, scale)).astype(BF16)
    add_columns(step, gain1_ref, grad * unit)
    add_columns(step, bias1_ref, grad)


def input_back(dproj, w, tokens, dx1, gain):
    count = tokens.shape[0]
    column = jax.ShapeDtypeStruct((1, D), F32)
    return pl.pallas_call(
        input_back_kernel,
        name="input_back",
        grid=(count // ROWS,),
        in_specs=[rows_of(ROWS, 3 * D), whole((D, 3 * D)), rows_of(ROWS, D), rows_of(ROWS, D), whole((1, D))],
        out_specs=[rows_of(ROWS, D), whole((1, D), False), whole((1, D), False)],
        out_shape=[jax.ShapeDtypeStruct((count, D), BF16), column, column],
        compiler_params=params("arbitrary"),
        cost_estimate=cost(2 * count * D * 3 * D, 14 * count * D + 6 * D * D),
    )(dproj, w, tokens, dx1, gain)


def narrow_kernel(g_ref, w_ref, bias_ref, x1_ref, out_ref):
    out_ref[...] = (x1_ref[...] + (nn(g_ref[...], w_ref[...]) + bias_ref[...])).astype(BF16)


def narrow(g, w, bias, x1):
    count = g.shape[0]
    return pl.pallas_call(
        narrow_kernel,
        name="narrow",
        grid=(count // ROWS,),
        in_specs=[rows_of(ROWS, FF), whole((FF, D)), whole((1, D)), rows_of(ROWS, D)],
        out_specs=rows_of(ROWS, D),
        out_shape=jax.ShapeDtypeStruct((count, D), BF16),
        compiler_params=params("arbitrary"),
        cost_estimate=cost(2 * count * D * FF, 14 * count * D + 8 * D * D),
    )(g, w, bias, x1)


def on_device(
    tokens, lengths, qkv_weight, qkv_bias, out_weight, out_bias, fc_weight, fc_bias, proj_weight, proj_bias,
    norm1_gain, norm1_bias, norm2_gain, norm2_bias, feature_map, cotangent,
):
    gather = lambda value: lax.all_gather(value, "fsdp", axis=0, tiled=True)
    w_qkv, w_out, w_fc, w_proj, fmap = map(gather, (qkv_weight, out_weight, fc_weight, proj_weight, feature_map))
    small = [qkv_bias, out_bias, fc_bias, proj_bias, norm1_gain, norm1_bias, norm2_gain, norm2_bias]
    packed = gather(jnp.concatenate(small)[None])
    bounds = [0]
    for value in small:
        bounds.append(bounds[-1] + value.shape[0])
    b_qkv, b_out, b_fc, b_proj, g1, s1, g2, s2 = (
        packed[:, a:b].reshape(1, -1).astype(F32) for a, b in zip(bounds[:-1], bounds[1:])
    )
    h1, q, k, v, pq, pk = project(lengths, tokens, w_qkv, b_qkv, g1, s1, fmap)
    o, rd, s = attend(lengths, pq, pk, v)
    x1, h2, g, slope = widen(o, tokens, w_out, b_out, g2, s2, w_fc, b_fc)
    projw_grad = outer(g, cotangent)
    df, dx1, da, do, projb, fcb, gain2, bias2, outb = ffn_back(cotangent, slope, x1, w_proj, w_fc, w_out, g2)
    fcw_grad = outer(h2, df)
    outw_grad = outer(o, da)
    dproj, sums, fmap_grad = attend_back(do, rd, o, pq, pk, v, s, q, k, fmap)
    qkvw_grad = outer(h1, dproj)
    input_grad, gain1, bias1 = input_back(dproj, w_qkv, tokens, dx1, g1)
    block_out = narrow(g, w_proj, b_proj, x1)

    def owned(value):
        share = lax.psum_scatter(value.astype(BF16), "fsdp", scatter_dimension=0, tiled=True)
        return lax.psum(share, "dp").astype(F32)

    shards = lax.axis_size("fsdp")
    vectors = [sums[0, : 2 * D], sums[0, 2 * D :], outb[0], fcb[0], projb[0], gain1[0], bias1[0], gain2[0], bias2[0]]
    packed = jnp.concatenate([vector.reshape(shards, -1) for vector in vectors], 1)
    mine = owned(packed)[0]
    bounds = [0]
    for vector in vectors:
        bounds.append(bounds[-1] + vector.shape[0] // shards)
    qkb, vb, outb, fcb, projb, gain1, bias1, gain2, bias2 = (mine[a:b] for a, b in zip(bounds[:-1], bounds[1:]))
    return (
        block_out, input_grad, owned(qkvw_grad), qkb, vb, owned(outw_grad), outb, owned(fcw_grad), fcb,
        owned(projw_grad), projb, gain1, bias1, gain2, bias2, owned(fmap_grad),
    )


def solution(mesh):
    rows = P(("dp", "fsdp"), None)
    wide = P("fsdp", None)
    flat = P("fsdp")
    in_specs = (
        rows, P(("dp", "fsdp")), wide, flat, wide, flat, wide, flat, wide, flat, flat, flat, flat, flat, wide, rows,
    )
    out_specs = (rows, rows, wide, flat, flat, wide, flat, wide, flat, wide, flat, flat, flat, flat, flat, wide)
    return jax.shard_map(on_device, mesh=mesh, in_specs=in_specs, out_specs=out_specs, check_vma=False)
```

```python
import functools

import jax
import jax.numpy as jnp
from jax import lax
from jax.experimental import pallas as pl
from jax.experimental.pallas import tpu as pltpu
from jax.sharding import PartitionSpec as P

D = 768
HEADS = 12
HD = 64
PAIRS = HEADS // 2
FF = 3072
ROWS = 256
CHUNK = 256
TILE = 256
EPSILON = 1e-05
SAFE = 60.0
SCALE = 5
F32 = jnp.float32
BF16 = jnp.bfloat16
ROOT = 0.7978845608028654
CUBE = 0.044715
VMEM = pl.BlockSpec(memory_space=pltpu.VMEM)
SMEM = pl.BlockSpec(memory_space=pltpu.SMEM)
ANY = pl.BlockSpec(memory_space=pl.ANY)
VECTORS = (8, FF)
MAPS = (PAIRS, 128, 256)


def nn(left, right):
    return lax.dot_general(left, right, (((1,), (0,)), ((), ())), preferred_element_type=F32)


def nt(left, right):
    return lax.dot_general(left, right, (((1,), (1,)), ((), ())), preferred_element_type=F32)


def tn(left, right):
    return lax.dot_general(left, right, (((0,), (0,)), ((), ())), preferred_element_type=F32)


def limit(mib):
    return pltpu.CompilerParams(vmem_limit_bytes=mib * 1024 * 1024)


def cost(flops, size, trans=0):
    return pl.CostEstimate(flops=int(SCALE * flops), bytes_accessed=int(size), transcendentals=int(trans))


def array(shape, kind=BF16):
    return jax.ShapeDtypeStruct(shape, kind)


def near(value):
    return pltpu.with_memory_space_constraint(value, pltpu.VMEM)


def far(value):
    return pltpu.with_memory_space_constraint(value, pltpu.HBM)


def lanes(shape):
    return lax.broadcasted_iota(jnp.int32, shape, 1)


def block_rows(index, count):
    return pl.ds(pl.multiple_of(index * count, count), count)


def normalized(values):
    middle = jnp.mean(values, -1, keepdims=True)
    centred = values - middle
    spread = jnp.mean(centred * centred, -1, keepdims=True)
    scale = lax.rsqrt(spread + EPSILON)
    return centred * scale, scale


def norm_back(grad, gain, unit, scale):
    scaled = grad * gain
    first = jnp.mean(scaled, -1, keepdims=True)
    second = jnp.mean(scaled * unit, -1, keepdims=True)
    return (scaled - first - unit * second) * scale


def swap_halves(values):
    return pltpu.roll(values, 64, 1)


def block_ones(size):
    row = lax.broadcasted_iota(jnp.int32, (size, size), 0) // HD
    col = lax.broadcasted_iota(jnp.int32, (size, size), 1) // HD
    return jnp.where(row == col, 1.0, 0.0).astype(BF16)


def build_maps(map_ref, fq, fk):
    fq[...] = jnp.zeros_like(fq)
    fk[...] = jnp.zeros_like(fk)
    low = lanes((HD, 2 * HD)) < HD
    for head in range(HEADS):
        block = map_ref[head * HD : (head + 1) * HD, :].astype(F32)
        turned = swap_halves(block)
        row, col = (head % 2) * HD, (head % 2) * 2 * HD
        fq[head // 2, row : row + HD, col : col + 2 * HD] = jnp.where(low, block, -turned).astype(BF16)
        fk[head // 2, row : row + HD, col : col + 2 * HD] = jnp.where(low, turned, -block).astype(BF16)


class Source:
    def __init__(self, places, arrays, rows, total):
        self.places, self.arrays, self.rows = places, [far(value) for value in arrays], rows
        self.shape = (total, arrays[0].shape[1])

    def specs(self):
        return [ANY] * len(self.arrays)

    def semaphores(self):
        return pltpu.SemaphoreType.DMA((len(self.arrays),))

    def copies(self, me, refs, held, sems):
        made = []
        for at, ((slot, offset), ref) in enumerate(zip(self.places, refs)):
            start = 0 if len(self.places) == 1 else pl.multiple_of((me ^ slot) * self.rows + offset, 16)
            made.append(pltpu.make_async_copy(ref, held.at[pl.ds(start, ref.shape[0]), :], sems.at[at]))
        return made


class Rows:
    def __init__(self, pairs, sems):
        self.pairs, self.sems = pairs, sems

    def copies(self, step):
        rows = block_rows(step, ROWS)
        return [
            pltpu.make_async_copy(source.at[rows, :], target.at[rows, :], self.sems.at[at, step])
            for at, (source, target) in enumerate(self.pairs)
        ]

    def start(self, step):
        for copy in self.copies(step):
            copy.start()

    def wait(self, step):
        for copy in self.copies(step):
            copy.wait()


def row_semaphores(pairs, count):
    return pltpu.SemaphoreType.DMA((pairs, count // ROWS))


def read_vectors(table, rows, sizes, out):
    for shard in range(table.shape[0] // rows):
        line = shard * rows
        for row, size in enumerate(sizes):
            for at in range(0, size, 128):
                count = min(128, size - at)
                out[row : row + 1, shard * size + at : shard * size + at + count] = table[line : line + 1, :count].astype(F32)
                line += 1


def project_kernel(source, sizes, me_ref, len_ref, tok_ref, *refs):
    count = len(source.arrays)
    v_ref, pq_ref, pk_ref, vec_ref, fq, fk, *far_refs, w_out, w_ref, h_ref, q_ref, k_ref, sems, out_sem, row_sems = refs[count:]
    leave = Rows(list(zip((h_ref, q_ref, k_ref, v_ref, pq_ref, pk_ref), far_refs)), row_sems)
    steps = tok_ref.shape[0] // ROWS
    copies = source.copies(me_ref[0], refs[:count], w_ref, sems)
    for copy in copies:
        copy.start()
    vec_ref[...] = jnp.zeros_like(vec_ref)
    ones = block_ones(4 * HD)
    for copy in copies:
        copy.wait()
    keep = pltpu.make_async_copy(w_ref, w_out, out_sem)
    keep.start()
    read_vectors(w_ref.at[:, 3 * D + 128 :], source.rows, sizes, vec_ref)
    build_maps(w_ref.at[:, 3 * D : 3 * D + 128], fq, fk)

    def body(step, carry):
        rows = block_rows(step, ROWS)
        unit, _ = normalized(tok_ref[rows, :].astype(F32))
        h = (unit * vec_ref[4:5, :D] + vec_ref[5:6, :D]).astype(BF16)
        h_ref[rows, :] = h
        wide = [(nn(h, w_ref[:, p * D : (p + 1) * D]) + vec_ref[0:1, p * D : (p + 1) * D]).astype(BF16) for p in range(3)]
        for out, value in zip((q_ref, k_ref, v_ref), wide):
            out[rows, :] = value
        place = step * ROWS + lax.broadcasted_iota(jnp.int32, (ROWS, 1), 0)
        live = (place < len_ref[0]).astype(F32)
        largest = jnp.zeros((ROWS, 256), F32)
        for part, (maps, out) in enumerate(((fq, pq_ref), (fk, pk_ref))):
            u = [nn(wide[part][:, p * 128 : (p + 1) * 128], maps[p]) for p in range(PAIRS)]
            e = [jnp.exp(value) for value in u]
            total = [nn(value.astype(BF16), ones) for value in e]
            for p in range(PAIRS):
                largest = jnp.maximum(largest, u[p])
                share = e[p] * pl.reciprocal(total[p], approx=True)
                if part == 1:
                    share = share * live
                out[rows, p * 256 : (p + 1) * 256] = share.astype(BF16)

        @pl.when(jnp.logical_not(jnp.max(largest) <= SAFE))
        def _():
            for part, (maps, rows_ref, out) in enumerate(((fq, q_ref, pq_ref), (fk, k_ref, pk_ref))):
                for p in range(PAIRS):
                    u = nn(rows_ref[rows, p * 128 : (p + 1) * 128], maps[p])
                    for group in range(4):
                        piece = u[:, group * HD : (group + 1) * HD]
                        e = jnp.exp(piece - jnp.max(piece, -1, keepdims=True))
                        share = e / jnp.sum(e, -1, keepdims=True)
                        if part == 1:
                            share = share * live
                        out[rows, p * 256 + group * HD : p * 256 + (group + 1) * HD] = share.astype(BF16)

        leave.start(step)
        return carry

    lax.fori_loop(0, steps, body, 0)
    keep.wait()
    for step in range(steps):
        leave.wait(step)


def project(me, lengths, tokens, source, sizes):
    count = tokens.shape[0]
    return pl.pallas_call(
        functools.partial(project_kernel, source, sizes),
        name="project",
        in_specs=[SMEM, SMEM, VMEM] + source.specs(),
        out_specs=[VMEM] * 6 + [ANY] * 7,
        out_shape=[array((count, D)), array((count, 2 * D)), array((count, 2 * D)), array(VECTORS, F32), array(MAPS), array(MAPS)]
        + [pltpu.HBM((count, D), BF16)] * 4 + [pltpu.HBM((count, 2 * D), BF16)] * 2 + [pltpu.HBM(source.shape, BF16)],
        scratch_shapes=[pltpu.VMEM(source.shape, BF16)] + [pltpu.VMEM((count, D), BF16)] * 3
        + [source.semaphores(), pltpu.SemaphoreType.DMA, row_semaphores(6, count)],
        compiler_params=limit(22),
        cost_estimate=cost(2 * count * D * 3 * D, 14 * count * D + 6 * D * D, 4 * count * D),
    )(me, lengths, tokens, *source.arrays)


def value_pair(v_pair):
    low = lanes(v_pair.shape) < HD
    wide = v_pair.astype(F32)
    return (
        jnp.where(low, wide, 1.0).astype(BF16),
        jnp.where(low, swap_halves(wide), 1.0).astype(BF16),
    )


def attend_kernel(group, len_ref, pq_ref, pk_ref, v_ref, o_ref, o_far, rd_far, s_far, rd_ref, s_ref, state, row_sems, s_sems):
    leave = Rows([(o_ref, o_far), (rd_ref, rd_far)], row_sems)
    leave_state = lambda step: pltpu.make_async_copy(s_ref.at[step], s_far.at[step], s_sems.at[step])
    steps = v_ref.shape[0] // CHUNK
    state[...] = jnp.zeros_like(state)
    row = lax.broadcasted_iota(jnp.int32, (CHUNK, CHUNK), 0)
    col = lax.broadcasted_iota(jnp.int32, (CHUNK, CHUNK), 1)
    causal = row >= col
    low = lanes((CHUNK, 128)) < HD
    place = lax.broadcasted_iota(jnp.int32, (CHUNK, 128), 0)

    def body(step, carry):
        rows = block_rows(step, CHUNK)
        live = (step * CHUNK + place < len_ref[0]).astype(F32)
        for first in range(0, PAIRS, group):
            pairs = range(first, first + group)
            heads = range(2 * first, 2 * (first + group))
            cols = [slice(head * 128, (head + 1) * 128) for head in range(HEADS)]
            pq = {head: pq_ref[rows, cols[head]] for head in heads}
            pk = {head: pk_ref[rows, cols[head]] for head in heads}
            vx = {}
            for pair in pairs:
                vx[2 * pair], vx[2 * pair + 1] = value_pair(v_ref[rows, cols[pair]])
            scores = {head: nt(pq[head], pk[head]) for head in heads}
            prior = {head: state[head].astype(BF16) for head in heads}
            more = {head: tn(pk[head], vx[head]) for head in heads}
            far = {head: nn(pq[head], prior[head]) for head in heads}
            scores = {head: jnp.where(causal, scores[head], 0.0).astype(BF16) for head in heads}
            sums = {head: nn(scores[head], vx[head]) + far[head] for head in heads}
            for head in heads:
                s_ref[step, head] = prior[head]
                state[head] += more[head]
            for pair in pairs:
                one, two = sums[2 * pair], sums[2 * pair + 1]
                numer = jnp.where(low, one, swap_halves(two))
                denom = jnp.where(low, swap_halves(one), two)
                rd = live / denom
                rd_ref[rows, cols[pair]] = rd.astype(BF16)
                o_ref[rows, cols[pair]] = (numer * rd).astype(BF16)
        leave.start(step)
        leave_state(step).start()
        return carry

    lax.fori_loop(0, steps, body, 0)
    for step in range(steps):
        leave.wait(step)
        leave_state(step).wait()


def attend(lengths, pq, pk, v, group=3):
    count = v.shape[0]
    steps = count // CHUNK
    return pl.pallas_call(
        functools.partial(attend_kernel, group),
        name="attend",
        in_specs=[SMEM, VMEM, VMEM, VMEM],
        out_specs=[VMEM] + [ANY] * 3,
        out_shape=[array((count, D))] + [pltpu.HBM((count, D), BF16)] * 2 + [pltpu.HBM((steps, HEADS, 128, 128), BF16)],
        scratch_shapes=[
            pltpu.VMEM((count, D), BF16), pltpu.VMEM((steps, HEADS, 128, 128), BF16), pltpu.VMEM((HEADS, 128, 128), F32),
            row_semaphores(2, count), pltpu.SemaphoreType.DMA((steps,)),
        ],
        compiler_params=limit(15),
        cost_estimate=cost(2 * count * HEADS * 128 * 512, 20 * count * D),
    )(lengths, pq, pk, v)


def gelu_pair(f):
    low = f.astype(BF16)
    square = low * low
    bend = jnp.tanh(low * (BF16(ROOT) + BF16(ROOT * CUBE) * square))
    share = BF16(0.5) + BF16(0.5) * bend
    value = low * share
    slope = share + value * (BF16(1.0) - share) * (BF16(2 * ROOT) + BF16(6 * ROOT * CUBE) * square)
    return value, slope


def widen_kernel(source, me_ref, o_ref, tok_ref, vec_ref, *refs):
    count = len(source.arrays)
    h2_ref, g_ref, slope_ref, w_ref, g_far, x1_far, x1_ref, sems, row_sems = refs[count:]
    leave = Rows([(g_ref, g_far), (x1_ref, x1_far)], row_sems)
    steps = tok_ref.shape[0] // ROWS
    copies = source.copies(me_ref[0], refs[:count], w_ref, sems)
    for copy in copies:
        copy.start()
    for copy in copies:
        copy.wait()

    def body(step, carry):
        rows = block_rows(step, ROWS)
        x1 = tok_ref[rows, :].astype(F32) + (nn(o_ref[rows, :], w_ref[:, FF:]) + vec_ref[1:2, :D])
        x1_ref[rows, :] = x1.astype(BF16)
        unit, _ = normalized(x1)
        h2 = (unit * vec_ref[6:7, :D] + vec_ref[7:8, :D]).astype(BF16)
        h2_ref[rows, :] = h2
        for part in range(4):
            cols = slice(part * D, (part + 1) * D)
            g_ref[rows, cols], slope_ref[rows, cols] = gelu_pair(nn(h2, w_ref[:, cols]) + vec_ref[2:3, cols])
        leave.start(step)
        return carry

    lax.fori_loop(0, steps, body, 0)
    for step in range(steps):
        leave.wait(step)


def widen(me, o, tokens, vectors, source):
    count = tokens.shape[0]
    return pl.pallas_call(
        functools.partial(widen_kernel, source),
        name="widen",
        in_specs=[SMEM, VMEM, VMEM, VMEM] + source.specs(),
        out_specs=[VMEM] * 4 + [ANY] * 2,
        out_shape=[
            array((count, D)), array((count, FF)), array((count, FF)), array(source.shape),
            pltpu.HBM((count, FF), BF16), pltpu.HBM((count, D), BF16),
        ],
        scratch_shapes=[pltpu.VMEM((count, D), BF16), source.semaphores(), row_semaphores(2, count)],
        compiler_params=limit(13),
        cost_estimate=cost(2 * count * D * 5 * D, 26 * count * D + 10 * D * D, count * FF),
    )(me, o, tokens, vectors, *source.arrays)


def column_sums(values):
    return jnp.sum(values, 0, keepdims=True)


def slope_back_kernel(source, me_ref, cot_ref, slope_ref, *refs):
    count = len(source.arrays)
    df_ref, projb_ref, fcb_ref, w_out, wp_ref, sems, out_sem = refs[count:]
    copies = source.copies(me_ref[0], refs[:count], wp_ref, sems)
    for copy in copies:
        copy.start()
    projb_ref[...] = column_sums(cot_ref[...].astype(F32))
    fcb_ref[...] = jnp.zeros_like(fcb_ref)
    for copy in copies:
        copy.wait()
    keep = pltpu.make_async_copy(wp_ref, w_out, out_sem)
    keep.start()

    def body(step, carry):
        rows = block_rows(step, ROWS)
        cot = cot_ref[rows, :]
        for part in range(4):
            cols = slice(part * D, (part + 1) * D)
            df = nt(cot, wp_ref[cols, :]).astype(BF16) * slope_ref[rows, cols]
            df_ref[rows, cols] = df
            fcb_ref[:, cols] += column_sums(df.astype(F32))
        return carry

    lax.fori_loop(0, cot_ref.shape[0] // ROWS, body, 0)
    keep.wait()


def slope_back(me, cot, slope, source):
    count = cot.shape[0]
    return pl.pallas_call(
        functools.partial(slope_back_kernel, source),
        name="slope_back",
        in_specs=[SMEM, VMEM, VMEM] + source.specs(),
        out_specs=[VMEM] * 3 + [ANY],
        out_shape=[array((count, FF)), array((1, D), F32), array((1, FF), F32), pltpu.HBM(source.shape, BF16)],
        scratch_shapes=[pltpu.VMEM(source.shape, BF16), source.semaphores(), pltpu.SemaphoreType.DMA],
        compiler_params=limit(16),
        cost_estimate=cost(2 * count * D * 4 * D, 30 * count * D + 18 * D * D),
    )(me, cot, slope, *source.arrays)


def middle_back_kernel(
    cot_ref, df_ref, x1_far, vec_ref, w_ref, da_ref, do_ref, gain2_ref, bias2_ref, outb_ref, x1_ref, row_sems
):
    enter = Rows([(x1_far, x1_ref)], row_sems)
    steps = cot_ref.shape[0] // ROWS
    for step in range(steps):
        enter.start(step)
    for ref in (gain2_ref, bias2_ref, outb_ref):
        ref[...] = jnp.zeros_like(ref)

    def body(step, carry):
        rows = block_rows(step, ROWS)
        total = nt(df_ref[rows, :], w_ref[:, :FF])
        enter.wait(step)
        unit, scale = normalized(x1_ref[rows, :].astype(F32))
        dx1 = cot_ref[rows, :].astype(F32) + norm_back(total, vec_ref[6:7, :D], unit, scale)
        da = dx1.astype(BF16)
        da_ref[rows, :] = da
        do_ref[rows, :] = nt(da, w_ref[:, FF:]).astype(BF16)
        gain2_ref[...] += column_sums(total * unit)
        bias2_ref[...] += column_sums(total)
        outb_ref[...] += column_sums(da.astype(F32))
        return carry

    lax.fori_loop(0, steps, body, 0)


def middle_back(cot, df, x1, vectors, w):
    count = cot.shape[0]
    return pl.pallas_call(
        middle_back_kernel,
        name="middle_back",
        in_specs=[VMEM] * 2 + [ANY] + [VMEM] * 2,
        out_specs=[VMEM] * 5,
        out_shape=[array((count, D)), array((count, D))] + [array((1, D), F32)] * 3,
        scratch_shapes=[pltpu.VMEM((count, D), BF16), row_semaphores(1, count)],
        compiler_params=limit(13),
        cost_estimate=cost(2 * count * D * 5 * D, 30 * count * D + 18 * D * D),
    )(cot, df, far(x1), vectors, w)


def attend_back_kernel(
    first_head, group, do_ref, rd_far, o_far, pq_far, pk_far, v_far, s_far, q_far, k_far, fq, fk,
    dproj_ref, sums_ref, fmap_ref, state, gq, gk, rd_ref, o_ref, pq_ref, pk_ref, v_ref, q_ref, k_ref, s_ref, row_sems, s_sems,
):
    heads_here = state.shape[0]
    width = heads_here * HD
    base = first_head // 2
    steps = do_ref.shape[0] // CHUNK
    enter = Rows(
        [(source.at[:, pl.ds(first_head * HD, width)], target) for source, target in ((rd_far, rd_ref), (o_far, o_ref), (v_far, v_ref))]
        + [(source.at[:, pl.ds(2 * first_head * HD, 2 * width)], target) for source, target in ((pq_far, pq_ref), (pk_far, pk_ref))]
        + [(source.at[:, pl.ds(first_head * HD, width)], target) for source, target in ((q_far, q_ref), (k_far, k_ref))],
        row_sems,
    )
    enter_state = lambda step: pltpu.make_async_copy(
        s_far.at[step, pl.ds(first_head, heads_here)], s_ref.at[step], s_sems.at[step]
    )
    for step in reversed(range(steps)):
        enter.start(step)
        enter_state(step).start()
    for ref in (state, gq, gk, sums_ref):
        ref[...] = jnp.zeros_like(ref)
    ones = block_ones(4 * HD)
    halves = jnp.concatenate([ones[0:128, 0:128], ones[0:128, 0:128]], 0)
    row = lax.broadcasted_iota(jnp.int32, (CHUNK, CHUNK), 0)
    col = lax.broadcasted_iota(jnp.int32, (CHUNK, CHUNK), 1)
    causal = row >= col
    below = row <= col
    lane = lanes((CHUNK, 128))
    low = lane < HD

    def body(index, carry):
        step = steps - 1 - index
        rows = block_rows(step, CHUNK)
        enter.wait(step)
        enter_state(step).wait()
        for start in range(0, heads_here // 2, group):
            pairs = range(start, start + group)
            heads = range(2 * start, 2 * (start + group))
            pair_cols = {pair: slice(pair * 128, (pair + 1) * 128) for pair in pairs}
            head_cols = {head: slice(head * 128, (head + 1) * 128) for head in heads}
            do_cols = {pair: slice((base + pair) * 128, (base + pair + 1) * 128) for pair in pairs}
            pq = {head: pq_ref[rows, head_cols[head]] for head in heads}
            pk = {head: pk_ref[rows, head_cols[head]] for head in heads}
            scores = {head: nt(pk[head], pq[head]) for head in heads}
            numer = {p: (do_ref[rows, do_cols[p]].astype(F32) * rd_ref[rows, pair_cols[p]].astype(F32)).astype(BF16).astype(F32) for p in pairs}
            denom = {}
            for p in pairs:
                product = numer[p] * o_ref[rows, pair_cols[p]].astype(F32)
                coarse = product.astype(BF16)
                fine = (product - coarse.astype(F32)).astype(BF16)
                denom[p] = -nn(jnp.concatenate([coarse, fine], 1), halves)
            vx = {}
            for p in pairs:
                vx[2 * p], vx[2 * p + 1] = value_pair(v_ref[rows, pair_cols[p]])
            scores = {head: jnp.where(below, scores[head], 0.0).astype(BF16) for head in heads}
            dn = {}
            for p in pairs:
                for head, top, rest in ((2 * p, numer[p], swap_halves(denom[p])), (2 * p + 1, swap_halves(numer[p]), denom[p])):
                    rounded = rest.astype(BF16).astype(F32)
                    tail = jnp.where(lane == HD, rounded, jnp.where(lane == HD + 1, rest - rounded, 0.0))
                    dn[head] = jnp.where(low, top, tail).astype(BF16)
            later = {head: state[head].astype(BF16) for head in heads}
            ds = {head: nt(dn[head], vx[head]) for head in heads}
            dst = {head: nt(vx[head], dn[head]) for head in heads}
            far_q = {head: nt(dn[head], s_ref[step, head]) for head in heads}
            far_k = {head: nt(vx[head], later[head]) for head in heads}
            far_v = {head: nn(pk[head], later[head]) for head in heads}
            dv = {head: nn(scores[head], dn[head]) + far_v[head] for head in heads}
            more = {head: tn(pq[head], dn[head]) for head in heads}
            ds = {head: jnp.where(causal, ds[head], 0.0).astype(BF16) for head in heads}
            dst = {head: jnp.where(below, dst[head], 0.0).astype(BF16) for head in heads}
            dq = {head: nn(ds[head], pk[head]) + far_q[head] for head in heads}
            dk = {head: nn(dst[head], pq[head]) + far_k[head] for head in heads}
            for head in heads:
                state[head] += more[head]
            out = {}
            for p in pairs:
                out[2, p] = jnp.where(low, dv[2 * p], swap_halves(dv[2 * p + 1])).astype(BF16)
            grads, feats, inner = {}, {}, {}
            for p in pairs:
                both = slice(p * 256, (p + 1) * 256)
                for part, (grad, feat_ref) in enumerate(((dq, pq_ref), (dk, pk_ref))):
                    grads[part, p] = jnp.concatenate([grad[2 * p], grad[2 * p + 1]], 1)
                    feats[part, p] = feat_ref[rows, both].astype(F32)
                    inner[part, p] = nn((grads[part, p] * feats[part, p]).astype(BF16), ones)
            logits = {key: (feats[key] * (grads[key] - inner[key])).astype(BF16) for key in inner}
            for p in pairs:
                for part, (rows_ref, maps, total) in enumerate(((q_ref, fq, gq), (k_ref, fk, gk))):
                    out[part, p] = nt(logits[part, p], maps[base + p]).astype(BF16)
                    total[p] += tn(rows_ref[rows, pair_cols[p]], logits[part, p])
            for (part, p), value in out.items():
                cols = slice(part * width + p * 128, part * width + (p + 1) * 128)
                dproj_ref[rows, cols] = value
                sums_ref[:, cols] += column_sums(value.astype(F32))
        return carry

    lax.fori_loop(0, steps, body, 0)
    first = lanes((HD, 2 * HD)) < HD
    for head in range(heads_here):
        r, c = (head % 2) * HD, (head % 2) * 2 * HD
        bq = gq[head // 2, r : r + HD, c : c + 2 * HD]
        bk = gk[head // 2, r : r + HD, c : c + 2 * HD]
        fmap_ref[head * HD : (head + 1) * HD, :] = jnp.where(first, bq - swap_halves(bq), swap_halves(bk) - bk)


def attend_back(first, heads, do, rd, o, pq, pk, v, s, q, k, fq, fk, group=2):
    count = v.shape[0]
    width = heads * HD
    return pl.pallas_call(
        functools.partial(attend_back_kernel, first, group),
        name="attend_back",
        in_specs=[VMEM] + [ANY] * 8 + [VMEM] * 2,
        out_specs=[VMEM] * 3,
        out_shape=[array((count, 3 * width)), array((1, 3 * width), F32), array((width, 2 * HD), F32)],
        scratch_shapes=[
            pltpu.VMEM((heads, 128, 128), F32), pltpu.VMEM((heads // 2, 128, 256), F32), pltpu.VMEM((heads // 2, 128, 256), F32),
        ]
        + [pltpu.VMEM((count, size), BF16) for size in (width, width, 2 * width, 2 * width, width, width, width)]
        + [pltpu.VMEM((count // CHUNK, heads, 128, 128), BF16), row_semaphores(7, count), pltpu.SemaphoreType.DMA((count // CHUNK,))],
        compiler_params=limit(28),
        cost_estimate=cost(2 * count * heads * 128 * 128 * 14, 40 * count * width),
    )(do, *map(far, (rd, o, pq, pk, v, s, q, k)), fq, fk)


def slot_of(index):
    return 2 * index if index < 4 else 2 * index - 7


def outer_rows_kernel(me_ref, left_ref, right_ref, send_ref, keep_ref):
    rows = send_ref.shape[1]
    right = right_ref[...]
    for index in range(8):
        start = pl.multiple_of((me_ref[0] ^ slot_of(index)) * rows, 128)
        ref = keep_ref if index < 4 else send_ref
        ref[index % 4] = tn(left_ref[:, pl.ds(start, rows)], right).astype(BF16)


def outer_rows(me, left, right):
    count, wide = left.shape
    across = right.shape[1]
    out = array((4, wide // 8, across))
    return pl.pallas_call(
        outer_rows_kernel,
        name="outer_rows",
        in_specs=[SMEM, VMEM, VMEM],
        out_specs=[VMEM, VMEM],
        out_shape=[out, out],
        compiler_params=limit(12),
        cost_estimate=cost(2 * count * wide * across, 2 * (count * (wide + across) + wide * across)),
    )(me, left, right)


def outer_cols_kernel(plan, away, me_ref, *refs):
    *ins, send_ref, keep_ref, turned = refs[: len(refs) - len(away) - 1]
    copies = {}
    for at, index in enumerate(away):
        held = refs[len(refs) - len(away) - 1 + at]
        copies[index] = pltpu.make_async_copy(ins[index], held, refs[-1].at[at])
        copies[index].start()
        ins[index] = held
    rows = send_ref.shape[1]
    at = 0

    def by_slot(value):
        for shard in range(8):
            slot = me_ref[0] ^ shard
            turned[(slot >> 1) + 4 * (slot & 1), :, : value.shape[1]] = value[shard * rows : (shard + 1) * rows]

    for left, right in plan:
        across = ins[right].shape[1]
        if left is None:
            by_slot(ins[right][...].astype(BF16))
            keep_ref[:, :, at : at + across] = turned[0:4, :, :across]
            send_ref[:, :, at : at + across] = turned[4:8, :, :across]
            at += across
            continue
        if left in copies:
            copies[left].wait()
        by_slot(ins[left][...].T)
        whole = turned[...].reshape(8 * rows, turned.shape[2])
        for start in range(0, across, TILE):
            value = nn(whole, ins[right][:, start : start + TILE]).astype(BF16)
            keep_ref[:, :, at : at + TILE] = value[: 4 * rows].reshape(4, rows, TILE)
            send_ref[:, :, at : at + TILE] = value[4 * rows :].reshape(4, rows, TILE)
            at += TILE


def outer_cols(me, arrays, plan, away=()):
    across = sum(arrays[right].shape[1] for _, right in plan)
    out = array((4, D // 8, across))
    size = sum(value.size for value in arrays) + D * across
    return pl.pallas_call(
        functools.partial(outer_cols_kernel, plan, away),
        name="outer_cols",
        in_specs=[SMEM] + [ANY if index in away else VMEM for index in range(len(arrays))],
        out_specs=[VMEM, VMEM],
        out_shape=[out, out],
        scratch_shapes=[pltpu.VMEM((8, D // 8, arrays[0].shape[0]), BF16)]
        + [pltpu.VMEM(arrays[index].shape, BF16) for index in away] + [pltpu.SemaphoreType.DMA((max(1, len(away)),))],
        compiler_params=limit(12),
        cost_estimate=cost(2 * 1024 * D * across, 2 * size),
    )(me, *[far(value) if index in away else value for index, value in enumerate(arrays)])


def input_back_kernel(groups, tok_ref, da_ref, vec_ref, w_in, *refs):
    *parts, out_ref, gain1_ref, bias1_ref, w_ref, sem = refs
    copy = pltpu.make_async_copy(w_in, w_ref, sem)
    copy.start()
    for ref in (gain1_ref, bias1_ref):
        ref[...] = jnp.zeros_like(ref)
    copy.wait()

    def body(step, carry):
        rows = block_rows(step, ROWS)
        grad = jnp.zeros((ROWS, D), F32)
        for (first, heads), part_ref in zip(groups, parts):
            width = heads * HD
            for part in range(3):
                cols = slice(part * D + first * HD, part * D + (first + heads) * HD)
                grad = grad + nt(part_ref[rows, part * width : (part + 1) * width], w_ref[:, cols])
        unit, scale = normalized(tok_ref[rows, :].astype(F32))
        out_ref[rows, :] = (da_ref[rows, :].astype(F32) + norm_back(grad, vec_ref[4:5, :D], unit, scale)).astype(BF16)
        gain1_ref[...] += column_sums(grad * unit)
        bias1_ref[...] += column_sums(grad)
        return carry

    lax.fori_loop(0, tok_ref.shape[0] // ROWS, body, 0)


def input_back(groups, parts, tokens, da, vectors, w):
    count = tokens.shape[0]
    return pl.pallas_call(
        functools.partial(input_back_kernel, groups),
        name="input_back",
        in_specs=[VMEM] * 3 + [ANY] + [VMEM] * len(parts),
        out_specs=[VMEM] * 3,
        out_shape=[array((count, D)), array((1, D), F32), array((1, D), F32)],
        scratch_shapes=[pltpu.VMEM(w.shape, BF16), pltpu.SemaphoreType.DMA],
        compiler_params=limit(16),
        cost_estimate=cost(2 * count * D * 3 * D, 14 * count * D + 6 * D * D),
    )(tokens, da, vectors, far(w), *parts)


def narrow_kernel(g_far, x1_far, vec_ref, w_in, out_ref, g_ref, x1_ref, w_ref, row_sems, w_sem):
    steps = g_ref.shape[0] // ROWS
    arrive = pltpu.make_async_copy(w_in, w_ref, w_sem)
    arrive.start()

    enter = Rows([(g_far, g_ref), (x1_far, x1_ref)], row_sems)
    for step in range(steps):
        enter.start(step)
    arrive.wait()

    def body(step, carry):
        enter.wait(step)
        rows = block_rows(step, ROWS)
        out_ref[rows, :] = (x1_ref[rows, :].astype(F32) + (nn(g_ref[rows, :], w_ref[...]) + vec_ref[3:4, :D])).astype(BF16)
        return carry

    lax.fori_loop(0, steps, body, 0)


def narrow(g, x1, vectors, w):
    count = g.shape[0]
    return pl.pallas_call(
        narrow_kernel,
        name="narrow",
        in_specs=[ANY, ANY, VMEM, ANY],
        out_specs=VMEM,
        out_shape=array((count, D)),
        scratch_shapes=[
            pltpu.VMEM(g.shape, BF16), pltpu.VMEM(x1.shape, BF16), pltpu.VMEM(w.shape, BF16),
            row_semaphores(2, count), pltpu.SemaphoreType.DMA,
        ],
        compiler_params=limit(20),
        cost_estimate=cost(2 * count * D * FF, 14 * count * D + 8 * D * D),
    )(far(g), far(x1), vectors, far(w))


def fold_kernel(keep_ref, arrived_ref, *outs):
    for index, out in enumerate(outs):
        out[...] = keep_ref[index] + arrived_ref[index]


def fold(keep, arrived):
    slots, rows, across = keep.shape
    return pl.pallas_call(
        fold_kernel,
        name="fold",
        in_specs=[VMEM] * 2,
        out_specs=[VMEM] * slots,
        out_shape=[array((rows, across))] * slots,
        compiler_params=limit(8),
        cost_estimate=cost(keep.size, 6 * keep.size),
    )(keep, arrived)


def total_kernel(*refs):
    *values, out = refs
    result = values[0][...].astype(F32)
    for value in values[1:]:
        result = result + value[...].astype(F32)
    out[...] = result.astype(out.dtype)


def total(*values):
    return pl.pallas_call(
        total_kernel,
        name="total",
        in_specs=[VMEM] * len(values),
        out_specs=VMEM,
        out_shape=array(values[0].shape),
        compiler_params=limit(8),
        cost_estimate=cost(4 * values[0].size, 10 * values[0].size),
    )(*values)


def halve_kernel(side_ref, *refs):
    *values, own_ref, other_ref = refs
    half = own_ref.shape[0]
    for side, out in ((side_ref[0], own_ref), (1 - side_ref[0], other_ref)):
        rows = block_rows(side, half)
        result = values[0][rows, :].astype(F32)
        for value in values[1:]:
            result = result + value[rows, :].astype(F32)
        out[...] = result.astype(BF16)


def halve(side, *values):
    rows, across = values[0].shape
    return pl.pallas_call(
        halve_kernel,
        name="halve",
        in_specs=[SMEM] + [VMEM] * len(values),
        out_specs=[VMEM] * 2,
        out_shape=[array((rows // 2, across))] * 2,
        compiler_params=limit(8),
        cost_estimate=cost(4 * rows * across, 10 * rows * across),
    )(side, *values)


def join_kernel(side_ref, own_ref, other_ref, out_ref):
    half = own_ref.shape[0]
    out_ref[block_rows(side_ref[0], half), :] = own_ref[...].astype(F32)
    out_ref[block_rows(1 - side_ref[0], half), :] = other_ref[...].astype(F32)


def join(side, own, other):
    half, across = own.shape
    return pl.pallas_call(
        join_kernel,
        name="join",
        in_specs=[SMEM] + [VMEM] * 2,
        out_specs=VMEM,
        out_shape=array((2 * half, across), F32),
        compiler_params=limit(8),
        cost_estimate=cost(half * across, 12 * half * across),
    )(side, own, other)


def publish_kernel(groups, side_ref, own_ref, other_ref, one_ref, two_ref, qkvw_ref, outw_ref, fmap_ref):
    half = own_ref.shape[0]
    for side, ref in ((side_ref[0], own_ref), (1 - side_ref[0], other_ref)):
        rows = block_rows(side, half)
        outw_ref[rows, :] = ref[:, :D].astype(F32)
        first, heads = groups[0]
        width = heads * HD
        for part in range(3):
            value = ref[:, D + part * width : D + (part + 1) * width]
            qkvw_ref[rows, part * D + first * HD : part * D + first * HD + width] = value.astype(F32)
    last = one_ref[...].astype(F32) + two_ref[...].astype(F32)
    first, heads = groups[1]
    width = heads * HD
    for part in range(3):
        qkvw_ref[:, part * D + first * HD : part * D + first * HD + width] = last[:, part * width : (part + 1) * width]
    fmap_ref[...] = last[:, 3 * width :]


def publish(groups, side, own, other, one, two):
    rows = one.shape[0]
    return pl.pallas_call(
        functools.partial(publish_kernel, groups),
        name="publish",
        in_specs=[SMEM] + [VMEM] * 4,
        out_specs=[VMEM] * 3,
        out_shape=[array((rows, 3 * D), F32), array((rows, D), F32), array((rows, 2 * HD), F32)],
        compiler_params=limit(12),
        cost_estimate=cost(rows * 3 * D * 4, rows * 3 * D * 12),
    )(side, own, other, one, two)


def line_count(sizes):
    return sum(-(-size // 128) for size in sizes)


def to_lines(vector, start, size):
    lines = []
    for at in range(0, size, 128):
        count = min(128, size - at)
        line = vector[:, start + at : start + at + count]
        if count < 128:
            line = jnp.concatenate([line, jnp.zeros((1, 128 - count), F32)], 1)
        lines.append(line)
    return lines


def pack_kernel(*refs):
    *vectors, fm_ref, w_ref, out_ref = refs
    width = w_ref.shape[1]
    out_ref[:, :width] = w_ref[...]
    out_ref[:, width : width + 128] = fm_ref[...]
    lines = []
    for vector in vectors:
        size = vector.shape[0]
        lines += to_lines(vector[...].astype(F32).reshape(1, size), 0, size)
    lines += [jnp.zeros((1, 128), F32)] * (w_ref.shape[0] - len(lines))
    out_ref[:, width + 128 :] = jnp.concatenate(lines, 0).astype(BF16)


def pack(w, fm, vectors):
    rows, width = w.shape
    return pl.pallas_call(
        pack_kernel,
        name="pack",
        in_specs=[VMEM] * (len(vectors) + 2),
        out_specs=VMEM,
        out_shape=array((rows, width + 256)),
        compiler_params=limit(56),
    )(*vectors, fm, w)


def small_grads_kernel(shards, *refs):
    *vectors, out_ref = refs
    for shard in range(shards):
        lines = []
        for vector in vectors:
            size = vector.shape[1] // shards
            lines += to_lines(vector[...], shard * size, size)
        lines += [jnp.zeros((1, 128), F32)] * (out_ref.shape[1] - len(lines))
        out_ref[shard] = jnp.concatenate(lines, 0).astype(BF16)


def small_grads(shards, vectors):
    lines = line_count([vector.shape[1] // shards for vector in vectors])
    return pl.pallas_call(
        functools.partial(small_grads_kernel, shards),
        name="small_grads",
        in_specs=[VMEM] * len(vectors),
        out_specs=VMEM,
        out_shape=jax.ShapeDtypeStruct((shards, -(-lines // 16) * 16, 128), BF16),
        compiler_params=limit(12),
    )(*vectors)


def small_owned_kernel(me_ref, table_ref, *outs):
    mine = table_ref[me_ref[0]].astype(F32)
    at = 0
    for out in outs:
        size = out.shape[0]
        for start in range(0, size, 128):
            count = min(128, size - start)
            out[pl.ds(start, count)] = mine[at : at + 1, :count].reshape(count)
            at += 1


def small_owned(me, table, sizes):
    return pl.pallas_call(
        small_owned_kernel,
        name="small_owned",
        in_specs=[SMEM, VMEM],
        out_specs=[VMEM] * len(sizes),
        out_shape=[jax.ShapeDtypeStruct((size,), F32) for size in sizes],
        compiler_params=limit(12),
    )(me, table)


GROUPS = ((0, 8), (8, 4))


def after(value, *others):
    return lax.optimization_barrier((value, *others))[0]


def exchange(value, axis, mask):
    return lax.ppermute(value, axis, [(i, i ^ mask) for i in range(lax.axis_size(axis))])


class Gather:
    def __init__(self, shard):
        self.shard, self.rows = shard, shard.shape[0]
        self.hand = by_hand(self.rows)

    def start(self, *others):
        if not self.hand:
            self.full = lax.all_gather(self.shard, "fsdp", axis=0, tiled=True)
            return ()
        shard = after(self.shard, *others) if others else self.shard
        self.over_x, self.over_y = exchange(shard, "fsdp", 2), exchange(shard, "fsdp", 4)
        self.sibling = exchange(shard, "fsdp", 1)
        return self.over_x, self.over_y

    def relay(self, *others):
        if not self.hand:
            return ()
        half = self.rows // 2
        over_x, over_y = self.over_x, self.over_y
        if others:
            over_x, over_y = lax.optimization_barrier((over_x, over_y, *others))[:2]
        self.pieces = over_y[:half], over_x[half:]
        self.upper, self.lower = exchange(self.pieces[0], "fsdp", 2), exchange(self.pieces[1], "fsdp", 4)
        self.shared = [((3, 0), exchange(over_x, "fsdp", 1)), ((5, 0), exchange(over_y, "fsdp", 1))]
        return self.pieces

    def finish(self, *others):
        if not self.hand:
            return Source([(0, 0)], [self.full], self.rows, self.full.shape[0])
        half = self.rows // 2
        upper, lower = self.upper, self.lower
        if others:
            upper, lower = lax.optimization_barrier((upper, lower, *others))[:2]
        held = [((0, 0), self.shard), ((2, 0), self.over_x), ((4, 0), self.over_y), ((1, 0), self.sibling)] + self.shared
        held += [((6, 0), upper), ((6, half), lower)]
        held += [((7, 0), exchange(upper, "fsdp", 1)), ((7, half), exchange(lower, "fsdp", 1))]
        return Source([place for place, _ in held], [part for _, part in held], self.rows, 8 * self.rows)


def by_hand(rows):
    return lax.axis_size("fsdp") == 8 and lax.axis_size("dp") == 4 and rows % 32 == 0


class Scatter:
    def __init__(self, pair):
        send, self.keep = pair
        self.arrived = exchange(send, "fsdp", 1)

    def cross(self, *others):
        self.mine, *away = fold(self.keep, after(self.arrived, *others))
        self.moved = [exchange(value, "fsdp", mask) for value, mask in zip(away, (2, 4, 6))]
        return away

    def finish(self, *others):
        return [self.mine, *lax.optimization_barrier((*self.moved, *others))[:3]]


class Planes:
    def __init__(self, side, values):
        self.own, self.other = halve(side, *values)
        self.moved = exchange(self.other, "dp", 1)

    def mirror(self, *others):
        self.own = self.own + after(self.moved, *others)
        self.moved = exchange(self.own, "dp", 3)
        return self.own

    def back(self, *others):
        self.own = self.own + after(self.moved, *others)
        self.moved = exchange(self.own, "dp", 1)
        return self.own

    def finish(self, *others):
        return self.own, after(self.moved, *others)


def outer(left, right):
    return tn(left, right).astype(BF16)


def on_device(
    tokens, lengths, qkv_weight, qkv_bias, out_weight, out_bias, fc_weight, fc_bias, proj_weight, proj_bias,
    norm1_gain, norm1_bias, norm2_gain, norm2_bias, feature_map, cotangent,
):
    shards = lax.axis_size("fsdp")
    me = lax.axis_index("fsdp").astype(jnp.int32).reshape(1)
    small = [qkv_bias, out_bias, fc_bias, proj_bias, norm1_gain, norm1_bias, norm2_gain, norm2_bias]
    first = Gather(pack(qkv_weight, feature_map, small))
    second = Gather(jnp.concatenate([fc_weight, out_weight], 1))
    third = Gather(proj_weight)
    first.start()
    second.start(*first.relay())
    v, pq, pk, vectors, fq, fk, h1, q, k, v_far, pq_far, pk_far, w_qkv = project(
        me, lengths, tokens, first.finish(), [value.shape[0] for value in small]
    )
    second.relay(v)
    third.start(v)
    o, o_far, rd, s = attend(lengths, pq, pk, v)
    parts = second.finish(o)
    third.relay(o)
    h2, g, slope, w_fc, g_far, x1 = widen(me, o, tokens, vectors, parts)
    parts = third.finish(g)
    hand = by_hand(qkv_weight.shape[0])
    plane = lax.axis_index("dp").astype(jnp.int32).reshape(1)
    side = (plane ^ (plane >> 1)) & 1
    summed = lambda share: lax.psum(share.astype(BF16), "dp").astype(F32)
    over = lambda value: lax.psum_scatter(value, "fsdp", scatter_dimension=0, tiled=True)
    if hand:
        pair = outer_rows(me, g, cotangent)
        proj_scatter = Scatter(pair)
        slope = after(slope, pair[0])
    df, projb, fcb, w_proj = slope_back(me, cotangent, slope, parts)
    if hand:
        pair = outer_cols(me, [after(h2, *proj_scatter.cross(df)), df], [(0, 1)])
        fc_scatter = Scatter(pair)
        df = after(df, pair[0])
    da, do, gain2, bias2, outb = middle_back(cotangent, df, x1, vectors, w_fc)
    if hand:
        share = total(*proj_scatter.finish(do))
        projw_grad = summed(share)
        do = after(do, share, *fc_scatter.cross(do))
    parts, sums, maps = [], [], []
    for index, (start, heads) in enumerate(GROUPS):
        dproj, sum_grad, fmap_grad = attend_back(start, heads, do, rd, o_far, pq_far, pk_far, v_far, s, q, k, fq, fk)
        parts.append(dproj)
        sums.append(sum_grad)
        maps.append(fmap_grad)
        if hand and index == 0:
            pair = outer_cols(me, [o_far, da, h1, dproj], [(0, 1), (2, 3)], (0, 2))
            qkv_scatter = Scatter(pair)
            fc_planes = Planes(side, fc_scatter.finish(pair[0]))
            do = after(do, pair[0], fc_planes.other)
    if hand:
        left = after(h1, *qkv_scatter.cross(dproj), fc_planes.mirror(dproj))
        pair = outer_cols(me, [left, dproj, jnp.concatenate(maps, 0)], [(0, 1), (None, 2)], (0,))
        last_scatter = Scatter(pair)
        tokens = after(tokens, pair[0])
    input_grad, gain1, bias1 = input_back(GROUPS, parts, tokens, da, vectors, w_qkv)
    spread = lambda values: jnp.concatenate([
        value[:, part * heads * HD : (part + 1) * heads * HD] for part in range(3) for (_, heads), value in zip(GROUPS, values)
    ], 1)
    ordered = spread(sums)
    small = [ordered[:, : 2 * D], ordered[:, 2 * D :], outb, fcb, projb, gain1, bias1, gain2, bias2]
    table = small_grads(shards, small)
    if hand:
        qkv_planes = Planes(side, qkv_scatter.finish(table))
        x1 = after(x1, qkv_planes.other, fc_planes.back(table), *last_scatter.cross(table))
    block_out = narrow(g_far, x1, vectors, w_proj)
    if hand:
        table = table + exchange(table, "fsdp", 1)
        table = total(table, *[exchange(table, "fsdp", mask) for mask in (2, 4, 6)])
        qkv_planes.mirror(block_out)
        share = total(*last_scatter.finish(block_out))
        share = share + exchange(share, "dp", 1)
        table = total(table, *[exchange(table, "dp", mask) for mask in (1, 2, 3)])
        qkv_planes.back()
        fcw_grad = join(side, *fc_planes.finish())
        qkvw_grad, outw_grad, fmap_grad = publish(GROUPS, side, *qkv_planes.finish(), share, exchange(share, "dp", 3))
    else:
        table = lax.psum(table, ("dp", "fsdp"))
    qkb, vb, outb, fcb, projb, gain1, bias1, gain2, bias2 = small_owned(
        me, table, [value.shape[1] // shards for value in small]
    )
    if not hand:
        projw_grad = summed(over(outer(g_far, cotangent)))
        fcw_grad, outw_grad = summed(over(outer(h2, df))), summed(over(outer(o_far, da)))
        qkvw_grad, fmap_grad = summed(over(outer(h1, spread(parts)))), summed(over(jnp.concatenate(maps, 0)))
    return (
        block_out, input_grad, qkvw_grad, qkb, vb, outw_grad, outb, fcw_grad, fcb,
        projw_grad, projb, gain1, bias1, gain2, bias2, fmap_grad,
    )


def solution(mesh):
    rows = P(("dp", "fsdp"), None)
    wide = P("fsdp", None)
    flat = P("fsdp")
    in_specs = (
        rows, P(("dp", "fsdp")), wide, flat, wide, flat, wide, flat, wide, flat, flat, flat, flat, flat, wide, rows,
    )
    out_specs = (rows, rows, wide, flat, flat, wide, flat, wide, flat, wide, flat, flat, flat, flat, flat, wide)
    return jax.shard_map(on_device, mesh=mesh, in_specs=in_specs, out_specs=out_specs, check_vma=False)
```

```python
import functools

import jax
import jax.numpy as jnp
from jax import lax
from jax.experimental import pallas as pl
from jax.experimental.pallas import tpu as pltpu
from jax.sharding import PartitionSpec as P

D = 768
HEADS = 12
HD = 64
PAIRS = HEADS // 2
FF = 3072
ROWS = 256
CHUNK = 256
TILE = 256
EPSILON = 1e-05
SAFE = 60.0
SCALE = 20
F32 = jnp.float32
BF16 = jnp.bfloat16
ROOT = 0.7978845608028654
CUBE = 0.044715
VMEM = pl.BlockSpec(memory_space=pltpu.VMEM)
SMEM = pl.BlockSpec(memory_space=pltpu.SMEM)
ANY = pl.BlockSpec(memory_space=pl.ANY)
VECTORS = (8, FF)
MAPS = (PAIRS, 128, 256)


def nn(left, right):
    return lax.dot_general(left, right, (((1,), (0,)), ((), ())), preferred_element_type=F32)


def nt(left, right):
    return lax.dot_general(left, right, (((1,), (1,)), ((), ())), preferred_element_type=F32)


def tn(left, right):
    return lax.dot_general(left, right, (((0,), (0,)), ((), ())), preferred_element_type=F32)


def limit(mib):
    return pltpu.CompilerParams(vmem_limit_bytes=mib * 1024 * 1024)


def cost(flops, size, trans=0):
    return pl.CostEstimate(flops=int(SCALE * flops), bytes_accessed=int(size), transcendentals=int(trans))


def array(shape, kind=BF16):
    return jax.ShapeDtypeStruct(shape, kind)


def near(value):
    return pltpu.with_memory_space_constraint(value, pltpu.VMEM)


def far(value):
    return pltpu.with_memory_space_constraint(value, pltpu.HBM)


def lanes(shape):
    return lax.broadcasted_iota(jnp.int32, shape, 1)


def block_rows(index, count):
    return pl.ds(pl.multiple_of(index * count, count), count)


def normalized(values):
    middle = jnp.mean(values, -1, keepdims=True)
    centred = values - middle
    spread = jnp.mean(centred * centred, -1, keepdims=True)
    scale = lax.rsqrt(spread + EPSILON)
    return centred * scale, scale


def norm_back(grad, gain, unit, scale):
    scaled = grad * gain
    first = jnp.mean(scaled, -1, keepdims=True)
    second = jnp.mean(scaled * unit, -1, keepdims=True)
    return (scaled - first - unit * second) * scale


def swap_halves(values):
    return pltpu.roll(values, 64, 1)


def block_ones(size):
    row = lax.broadcasted_iota(jnp.int32, (size, size), 0) // HD
    col = lax.broadcasted_iota(jnp.int32, (size, size), 1) // HD
    return jnp.where(row == col, 1.0, 0.0).astype(BF16)


def build_maps(map_ref, fq, fk):
    fq[...] = jnp.zeros_like(fq)
    fk[...] = jnp.zeros_like(fk)
    low = lanes((HD, 2 * HD)) < HD
    for head in range(HEADS):
        block = map_ref[head * HD : (head + 1) * HD, :].astype(F32)
        turned = swap_halves(block)
        row, col = (head % 2) * HD, (head % 2) * 2 * HD
        fq[head // 2, row : row + HD, col : col + 2 * HD] = jnp.where(low, block, -turned).astype(BF16)
        fk[head // 2, row : row + HD, col : col + 2 * HD] = jnp.where(low, turned, -block).astype(BF16)


class Source:
    def __init__(self, places, arrays, rows, total):
        self.places, self.arrays, self.rows = places, [far(value) for value in arrays], rows
        self.shape = (total, arrays[0].shape[1])

    def specs(self):
        return [ANY] * len(self.arrays)

    def semaphores(self):
        return pltpu.SemaphoreType.DMA((len(self.arrays),))

    def copies(self, me, refs, held, sems, first=0, count=None):
        made = []
        count = self.shape[1] - first if count is None else count
        cols = pl.ds(first, count)
        for at, ((slot, offset), ref) in enumerate(zip(self.places, refs)):
            start = 0 if len(self.places) == 1 else pl.multiple_of((me ^ slot) * self.rows + offset, 16)
            made.append(pltpu.make_async_copy(ref.at[:, cols], held.at[pl.ds(start, ref.shape[0]), cols], sems.at[at]))
        return made


class Rows:
    def __init__(self, pairs, sems):
        self.pairs, self.sems = pairs, sems

    def copies(self, step):
        rows = block_rows(step, ROWS)
        return [
            pltpu.make_async_copy(source.at[rows, :], target.at[rows, :], self.sems.at[at, step])
            for at, (source, target) in enumerate(self.pairs)
        ]

    def start(self, step):
        for copy in self.copies(step):
            copy.start()

    def wait(self, step):
        for copy in self.copies(step):
            copy.wait()


def row_semaphores(pairs, count):
    return pltpu.SemaphoreType.DMA((pairs, count // ROWS))


def read_vectors(table, rows, sizes, out):
    for shard in range(table.shape[0] // rows):
        line = shard * rows
        for row, size in enumerate(sizes):
            for at in range(0, size, 128):
                count = min(128, size - at)
                out[row : row + 1, shard * size + at : shard * size + at + count] = table[line : line + 1, :count].astype(F32)
                line += 1


def project_kernel(source, sizes, me_ref, len_ref, tok_ref, *refs):
    count = len(source.arrays)
    v_ref, pq_ref, pk_ref, vec_ref, fq, fk, *far_refs, w_ref, h_ref, q_ref, k_ref, side_sems, sems, row_sems = refs[count:]
    leave = Rows(list(zip((h_ref, q_ref, k_ref, v_ref, pq_ref, pk_ref), far_refs)), row_sems)
    steps = tok_ref.shape[0] // ROWS
    side = source.copies(me_ref[0], refs[:count], w_ref, side_sems, 3 * D)
    main = source.copies(me_ref[0], refs[:count], w_ref, sems, 0, 3 * D)
    for copy in side + main:
        copy.start()
    vec_ref[...] = jnp.zeros_like(vec_ref)
    ones = block_ones(4 * HD)
    for copy in side:
        copy.wait()
    read_vectors(w_ref.at[:, 3 * D + 128 :], source.rows, sizes, vec_ref)
    build_maps(w_ref.at[:, 3 * D : 3 * D + 128], fq, fk)

    def norm(step, carry):
        rows = block_rows(step, ROWS)
        unit, _ = normalized(tok_ref[rows, :].astype(F32))
        h_ref[rows, :] = (unit * vec_ref[4:5, :D] + vec_ref[5:6, :D]).astype(BF16)
        return carry

    lax.fori_loop(0, steps, norm, 0)
    for copy in main:
        copy.wait()

    def body(step, carry):
        rows = block_rows(step, ROWS)
        h = h_ref[rows, :]
        wide = [(nn(h, w_ref[:, p * D : (p + 1) * D]) + vec_ref[0:1, p * D : (p + 1) * D]).astype(BF16) for p in range(3)]
        for out, value in zip((q_ref, k_ref, v_ref), wide):
            out[rows, :] = value
        place = step * ROWS + lax.broadcasted_iota(jnp.int32, (ROWS, 1), 0)
        live = (place < len_ref[0]).astype(F32)
        largest = jnp.zeros((ROWS, 256), F32)
        for part, (maps, out) in enumerate(((fq, pq_ref), (fk, pk_ref))):
            u = [nn(wide[part][:, p * 128 : (p + 1) * 128], maps[p]) for p in range(PAIRS)]
            e = [jnp.exp(value) for value in u]
            total = [nn(value.astype(BF16), ones) for value in e]
            for p in range(PAIRS):
                largest = jnp.maximum(largest, u[p])
                share = e[p] * pl.reciprocal(total[p], approx=True)
                if part == 1:
                    share = share * live
                out[rows, p * 256 : (p + 1) * 256] = share.astype(BF16)

        @pl.when(jnp.logical_not(jnp.max(largest) <= SAFE))
        def _():
            for part, (maps, rows_ref, out) in enumerate(((fq, q_ref, pq_ref), (fk, k_ref, pk_ref))):
                for p in range(PAIRS):
                    u = nn(rows_ref[rows, p * 128 : (p + 1) * 128], maps[p])
                    for group in range(4):
                        piece = u[:, group * HD : (group + 1) * HD]
                        e = jnp.exp(piece - jnp.max(piece, -1, keepdims=True))
                        share = e / jnp.sum(e, -1, keepdims=True)
                        if part == 1:
                            share = share * live
                        out[rows, p * 256 + group * HD : p * 256 + (group + 1) * HD] = share.astype(BF16)

        leave.start(step)
        return carry

    lax.fori_loop(0, steps, body, 0)
    for step in range(steps):
        leave.wait(step)


def project(me, lengths, tokens, source, sizes):
    count = tokens.shape[0]
    return pl.pallas_call(
        functools.partial(project_kernel, source, sizes),
        name="project",
        in_specs=[SMEM, SMEM, VMEM] + source.specs(),
        out_specs=[VMEM] * 6 + [ANY] * 6,
        out_shape=[array((count, D)), array((count, 2 * D)), array((count, 2 * D)), array(VECTORS, F32), array(MAPS), array(MAPS)]
        + [pltpu.HBM((count, D), BF16)] * 4 + [pltpu.HBM((count, 2 * D), BF16)] * 2,
        scratch_shapes=[pltpu.VMEM(source.shape, BF16)] + [pltpu.VMEM((count, D), BF16)] * 3
        + [source.semaphores(), source.semaphores(), row_semaphores(6, count)],
        compiler_params=limit(17),
        cost_estimate=cost(2 * count * D * 3 * D, 14 * count * D + 6 * D * D, 4 * count * D),
    )(me, lengths, tokens, *source.arrays)


def value_pair(v_pair):
    low = lanes(v_pair.shape) < HD
    wide = v_pair.astype(F32)
    return (
        jnp.where(low, wide, 1.0).astype(BF16),
        jnp.where(low, swap_halves(wide), 1.0).astype(BF16),
    )


def attend_kernel(group, len_ref, pq_ref, pk_ref, v_ref, o_ref, o_far, rd_far, s_far, rd_ref, s_ref, state, row_sems, s_sems):
    leave = Rows([(o_ref, o_far), (rd_ref, rd_far)], row_sems)
    leave_state = lambda step: pltpu.make_async_copy(s_ref.at[step], s_far.at[step], s_sems.at[step])
    steps = v_ref.shape[0] // CHUNK
    state[...] = jnp.zeros_like(state)
    row = lax.broadcasted_iota(jnp.int32, (CHUNK, CHUNK), 0)
    col = lax.broadcasted_iota(jnp.int32, (CHUNK, CHUNK), 1)
    causal = row >= col
    low = lanes((CHUNK, 128)) < HD
    place = lax.broadcasted_iota(jnp.int32, (CHUNK, 128), 0)

    def body(step, carry):
        rows = block_rows(step, CHUNK)
        live = (step * CHUNK + place < len_ref[0]).astype(F32)
        for first in range(0, PAIRS, group):
            pairs = range(first, first + group)
            heads = range(2 * first, 2 * (first + group))
            cols = [slice(head * 128, (head + 1) * 128) for head in range(HEADS)]
            pq = {head: pq_ref[rows, cols[head]] for head in heads}
            pk = {head: pk_ref[rows, cols[head]] for head in heads}
            vx = {}
            for pair in pairs:
                vx[2 * pair], vx[2 * pair + 1] = value_pair(v_ref[rows, cols[pair]])
            scores = {head: nt(pq[head], pk[head]) for head in heads}
            prior = {head: state[head].astype(BF16) for head in heads}
            more = {head: tn(pk[head], vx[head]) for head in heads}
            far = {head: nn(pq[head], prior[head]) for head in heads}
            scores = {head: jnp.where(causal, scores[head], 0.0).astype(BF16) for head in heads}
            sums = {head: nn(scores[head], vx[head]) + far[head] for head in heads}
            for head in heads:
                s_ref[step, head] = prior[head]
                state[head] += more[head]
            for pair in pairs:
                one, two = sums[2 * pair], sums[2 * pair + 1]
                numer = jnp.where(low, one, swap_halves(two))
                denom = jnp.where(low, swap_halves(one), two)
                rd = live / denom
                rd_ref[rows, cols[pair]] = rd.astype(BF16)
                o_ref[rows, cols[pair]] = (numer * rd).astype(BF16)
        leave.start(step)
        leave_state(step).start()
        return carry

    lax.fori_loop(0, steps, body, 0)
    for step in range(steps):
        leave.wait(step)
        leave_state(step).wait()


def attend(lengths, pq, pk, v, group=3):
    count = v.shape[0]
    steps = count // CHUNK
    return pl.pallas_call(
        functools.partial(attend_kernel, group),
        name="attend",
        in_specs=[SMEM, VMEM, VMEM, VMEM],
        out_specs=[VMEM] + [ANY] * 3,
        out_shape=[array((count, D))] + [pltpu.HBM((count, D), BF16)] * 2 + [pltpu.HBM((steps, HEADS, 128, 128), BF16)],
        scratch_shapes=[
            pltpu.VMEM((count, D), BF16), pltpu.VMEM((steps, HEADS, 128, 128), BF16), pltpu.VMEM((HEADS, 128, 128), F32),
            row_semaphores(2, count), pltpu.SemaphoreType.DMA((steps,)),
        ],
        compiler_params=limit(10),
        cost_estimate=cost(2 * count * HEADS * 128 * 512, 20 * count * D),
    )(lengths, pq, pk, v)


def gelu_pair(f):
    low = f.astype(BF16)
    square = low * low
    bend = jnp.tanh(low * (BF16(ROOT) + BF16(ROOT * CUBE) * square))
    share = BF16(0.5) + BF16(0.5) * bend
    value = low * share
    slope = share + value * (BF16(1.0) - share) * (BF16(2 * ROOT) + BF16(6 * ROOT * CUBE) * square)
    return value, slope


def widen_kernel(source, me_ref, o_ref, tok_ref, vec_ref, *refs):
    count = len(source.arrays)
    h2_ref, g_ref, slope_ref, w_ref, g_far, x1_far, x1_ref, side_sems, sems, g_sems, x1_sems = refs[count:]
    leave, leave_x1 = Rows([(g_ref, g_far)], g_sems), Rows([(x1_ref, x1_far)], x1_sems)
    steps = tok_ref.shape[0] // ROWS
    side = source.copies(me_ref[0], refs[:count], w_ref, side_sems, FF)
    main = source.copies(me_ref[0], refs[:count], w_ref, sems, 0, FF)
    for copy in side + main:
        copy.start()
    for copy in side:
        copy.wait()

    def middle(step, carry):
        rows = block_rows(step, ROWS)
        x1 = tok_ref[rows, :].astype(F32) + (nn(o_ref[rows, :], w_ref[:, FF:]) + vec_ref[1:2, :D])
        x1_ref[rows, :] = x1.astype(BF16)
        unit, _ = normalized(x1)
        h2_ref[rows, :] = (unit * vec_ref[6:7, :D] + vec_ref[7:8, :D]).astype(BF16)
        leave_x1.start(step)
        return carry

    lax.fori_loop(0, steps, middle, 0)
    for copy in main:
        copy.wait()

    def body(step, carry):
        rows = block_rows(step, ROWS)
        h2 = h2_ref[rows, :]
        for part in range(4):
            cols = slice(part * D, (part + 1) * D)
            g_ref[rows, cols], slope_ref[rows, cols] = gelu_pair(nn(h2, w_ref[:, cols]) + vec_ref[2:3, cols])
        leave.start(step)
        return carry

    lax.fori_loop(0, steps, body, 0)
    for step in range(steps):
        leave_x1.wait(step)
        leave.wait(step)


def widen(me, o, tokens, vectors, source):
    count = tokens.shape[0]
    return pl.pallas_call(
        functools.partial(widen_kernel, source),
        name="widen",
        in_specs=[SMEM, VMEM, VMEM, VMEM] + source.specs(),
        out_specs=[VMEM] * 4 + [ANY] * 2,
        out_shape=[
            array((count, D)), array((count, FF)), pltpu.VMEM((count, FF), BF16), pltpu.VMEM(source.shape, BF16),
            pltpu.HBM((count, FF), BF16), pltpu.HBM((count, D), BF16),
        ],
        scratch_shapes=[
            pltpu.VMEM((count, D), BF16), source.semaphores(), source.semaphores(), row_semaphores(1, count), row_semaphores(1, count),
        ],
        compiler_params=limit(10),
        cost_estimate=cost(2 * count * D * 5 * D, 26 * count * D + 10 * D * D, count * FF),
    )(me, o, tokens, vectors, *source.arrays)


def column_sums(values):
    return jnp.sum(values, 0, keepdims=True)


def slope_back_kernel(source, me_ref, cot_ref, slope_ref, *refs):
    count = len(source.arrays)
    df_ref, projb_ref, fcb_ref, wp_ref, sems = refs[count:]
    copies = source.copies(me_ref[0], refs[:count], wp_ref, sems)
    for copy in copies:
        copy.start()
    projb_ref[...] = column_sums(cot_ref[...].astype(F32))
    fcb_ref[...] = jnp.zeros_like(fcb_ref)
    for copy in copies:
        copy.wait()

    def body(step, carry):
        rows = block_rows(step, ROWS)
        cot = cot_ref[rows, :]
        for part in range(4):
            cols = slice(part * D, (part + 1) * D)
            df = nt(cot, wp_ref[cols, :]).astype(BF16) * slope_ref[rows, cols]
            df_ref[rows, cols] = df
            fcb_ref[:, cols] += column_sums(df.astype(F32))
        return carry

    lax.fori_loop(0, cot_ref.shape[0] // ROWS, body, 0)


def slope_back(me, cot, slope, source):
    count = cot.shape[0]
    return pl.pallas_call(
        functools.partial(slope_back_kernel, source),
        name="slope_back",
        in_specs=[SMEM, VMEM, VMEM] + source.specs(),
        out_specs=[VMEM] * 3,
        out_shape=[array((count, FF)), array((1, D), F32), array((1, FF), F32)],
        scratch_shapes=[pltpu.VMEM(source.shape, BF16), source.semaphores()],
        compiler_params=limit(14),
        cost_estimate=cost(2 * count * D * 4 * D, 30 * count * D + 18 * D * D),
    )(me, cot, near(slope), *source.arrays)


def middle_back_kernel(
    cot_ref, df_ref, x1_far, vec_ref, w_ref, da_ref, do_ref, gain2_ref, bias2_ref, outb_ref, x1_ref, row_sems
):
    enter = Rows([(x1_far, x1_ref)], row_sems)
    steps = cot_ref.shape[0] // ROWS
    for step in range(steps):
        enter.start(step)
    for ref in (gain2_ref, bias2_ref, outb_ref):
        ref[...] = jnp.zeros_like(ref)

    def body(index, carry):
        blocks = [2 * index, 2 * index + 1]
        rows = [block_rows(step, ROWS) for step in blocks]
        totals = [nt(df_ref[at, :], w_ref[:, :FF]) for at in rows]
        for step in blocks:
            enter.wait(step)
        das = []
        for at, total in zip(rows, totals):
            unit, scale = normalized(x1_ref[at, :].astype(F32))
            dx1 = cot_ref[at, :].astype(F32) + norm_back(total, vec_ref[6:7, :D], unit, scale)
            da = dx1.astype(BF16)
            das.append(da)
            da_ref[at, :] = da
            do_ref[at, :] = nt(da, w_ref[:, FF:]).astype(BF16)
            gain2_ref[...] += column_sums(total * unit)
        bias2_ref[...] += column_sums(totals[0]) + column_sums(totals[1])
        outb_ref[...] += column_sums(das[0].astype(F32)) + column_sums(das[1].astype(F32))
        return carry

    lax.fori_loop(0, steps // 2, body, 0)


def middle_back(cot, df, x1, vectors, w):
    count = cot.shape[0]
    return pl.pallas_call(
        middle_back_kernel,
        name="middle_back",
        in_specs=[VMEM] * 2 + [ANY] + [VMEM] * 2,
        out_specs=[VMEM] * 5,
        out_shape=[array((count, D)), array((count, D))] + [array((1, D), F32)] * 3,
        scratch_shapes=[pltpu.VMEM((count, D), BF16), row_semaphores(1, count)],
        compiler_params=limit(12),
        cost_estimate=cost(2 * count * D * 5 * D, 30 * count * D + 18 * D * D),
    )(cot, df, far(x1), vectors, near(w))


def attend_back_kernel(
    first_head, group, do_ref, rd_far, o_far, pq_far, pk_far, v_far, s_far, q_far, k_far, fq, fk,
    dproj_ref, sums_ref, fmap_ref, state, gq, gk, rd_ref, o_ref, pq_ref, pk_ref, v_ref, q_ref, k_ref, s_ref, row_sems, s_sems,
):
    heads_here = state.shape[0]
    width = heads_here * HD
    base = first_head // 2
    steps = do_ref.shape[0] // CHUNK
    enter = Rows(
        [(source.at[:, pl.ds(first_head * HD, width)], target) for source, target in ((rd_far, rd_ref), (o_far, o_ref), (v_far, v_ref))]
        + [(source.at[:, pl.ds(2 * first_head * HD, 2 * width)], target) for source, target in ((pq_far, pq_ref), (pk_far, pk_ref))]
        + [(source.at[:, pl.ds(first_head * HD, width)], target) for source, target in ((q_far, q_ref), (k_far, k_ref))],
        row_sems,
    )
    enter_state = lambda step: pltpu.make_async_copy(
        s_far.at[step, pl.ds(first_head, heads_here)], s_ref.at[step], s_sems.at[step]
    )
    for step in reversed(range(steps)):
        enter.start(step)
        enter_state(step).start()
    for ref in (state, gq, gk, sums_ref):
        ref[...] = jnp.zeros_like(ref)
    ones = block_ones(4 * HD)
    halves = jnp.concatenate([ones[0:128, 0:128], ones[0:128, 0:128]], 0)
    row = lax.broadcasted_iota(jnp.int32, (CHUNK, CHUNK), 0)
    col = lax.broadcasted_iota(jnp.int32, (CHUNK, CHUNK), 1)
    causal = row >= col
    below = row <= col
    lane = lanes((CHUNK, 128))
    low = lane < HD

    def body(index, carry):
        step = steps - 1 - index
        rows = block_rows(step, CHUNK)
        enter.wait(step)
        enter_state(step).wait()
        for start in range(0, heads_here // 2, group):
            pairs = range(start, start + group)
            heads = range(2 * start, 2 * (start + group))
            pair_cols = {pair: slice(pair * 128, (pair + 1) * 128) for pair in pairs}
            head_cols = {head: slice(head * 128, (head + 1) * 128) for head in heads}
            do_cols = {pair: slice((base + pair) * 128, (base + pair + 1) * 128) for pair in pairs}
            pq = {head: pq_ref[rows, head_cols[head]] for head in heads}
            pk = {head: pk_ref[rows, head_cols[head]] for head in heads}
            scores = {head: nt(pk[head], pq[head]) for head in heads}
            numer = {p: (do_ref[rows, do_cols[p]].astype(F32) * rd_ref[rows, pair_cols[p]].astype(F32)).astype(BF16).astype(F32) for p in pairs}
            denom = {}
            for p in pairs:
                product = numer[p] * o_ref[rows, pair_cols[p]].astype(F32)
                coarse = product.astype(BF16)
                fine = (product - coarse.astype(F32)).astype(BF16)
                denom[p] = -nn(jnp.concatenate([coarse, fine], 1), halves)
            vx = {}
            for p in pairs:
                vx[2 * p], vx[2 * p + 1] = value_pair(v_ref[rows, pair_cols[p]])
            scores = {head: jnp.where(below, scores[head], 0.0).astype(BF16) for head in heads}
            dn = {}
            for p in pairs:
                for head, top, rest in ((2 * p, numer[p], swap_halves(denom[p])), (2 * p + 1, swap_halves(numer[p]), denom[p])):
                    rounded = rest.astype(BF16).astype(F32)
                    tail = jnp.where(lane == HD, rounded, jnp.where(lane == HD + 1, rest - rounded, 0.0))
                    dn[head] = jnp.where(low, top, tail).astype(BF16)
            later = {head: state[head].astype(BF16) for head in heads}
            ds = {head: nt(dn[head], vx[head]) for head in heads}
            dst = {head: nt(vx[head], dn[head]) for head in heads}
            far_q = {head: nt(dn[head], s_ref[step, head]) for head in heads}
            far_k = {head: nt(vx[head], later[head]) for head in heads}
            far_v = {head: nn(pk[head], later[head]) for head in heads}
            dv = {head: nn(scores[head], dn[head]) + far_v[head] for head in heads}
            more = {head: tn(pq[head], dn[head]) for head in heads}
            ds = {head: jnp.where(causal, ds[head], 0.0).astype(BF16) for head in heads}
            dst = {head: jnp.where(below, dst[head], 0.0).astype(BF16) for head in heads}
            dq = {head: nn(ds[head], pk[head]) + far_q[head] for head in heads}
            dk = {head: nn(dst[head], pq[head]) + far_k[head] for head in heads}
            for head in heads:
                state[head] += more[head]
            out = {}
            for p in pairs:
                out[2, p] = jnp.where(low, dv[2 * p], swap_halves(dv[2 * p + 1])).astype(BF16)
            grads, feats, inner = {}, {}, {}
            for p in pairs:
                both = slice(p * 256, (p + 1) * 256)
                for part, (grad, feat_ref) in enumerate(((dq, pq_ref), (dk, pk_ref))):
                    grads[part, p] = jnp.concatenate([grad[2 * p], grad[2 * p + 1]], 1)
                    feats[part, p] = feat_ref[rows, both].astype(F32)
                    inner[part, p] = nn((grads[part, p] * feats[part, p]).astype(BF16), ones)
            logits = {key: (feats[key] * (grads[key] - inner[key])).astype(BF16) for key in inner}
            for p in pairs:
                for part, (rows_ref, maps, total) in enumerate(((q_ref, fq, gq), (k_ref, fk, gk))):
                    out[part, p] = nt(logits[part, p], maps[base + p]).astype(BF16)
                    total[p] += tn(rows_ref[rows, pair_cols[p]], logits[part, p])
            for (part, p), value in out.items():
                cols = slice(part * width + p * 128, part * width + (p + 1) * 128)
                dproj_ref[rows, cols] = value
                sums_ref[:, cols] += column_sums(value.astype(F32))
        return carry

    lax.fori_loop(0, steps, body, 0)
    first = lanes((HD, 2 * HD)) < HD
    for head in range(heads_here):
        r, c = (head % 2) * HD, (head % 2) * 2 * HD
        bq = gq[head // 2, r : r + HD, c : c + 2 * HD]
        bk = gk[head // 2, r : r + HD, c : c + 2 * HD]
        fmap_ref[head * HD : (head + 1) * HD, :] = jnp.where(first, bq - swap_halves(bq), swap_halves(bk) - bk)


def attend_back(first, heads, do, rd, o, pq, pk, v, s, q, k, fq, fk, group=2):
    count = v.shape[0]
    width = heads * HD
    return pl.pallas_call(
        functools.partial(attend_back_kernel, first, group),
        name="attend_back",
        in_specs=[VMEM] + [ANY] * 8 + [VMEM] * 2,
        out_specs=[VMEM] * 3,
        out_shape=[array((count, 3 * width)), array((1, 3 * width), F32), array((width, 2 * HD), F32)],
        scratch_shapes=[
            pltpu.VMEM((heads, 128, 128), F32), pltpu.VMEM((heads // 2, 128, 256), F32), pltpu.VMEM((heads // 2, 128, 256), F32),
        ]
        + [pltpu.VMEM((count, size), BF16) for size in (width, width, 2 * width, 2 * width, width, width, width)]
        + [pltpu.VMEM((count // CHUNK, heads, 128, 128), BF16), row_semaphores(7, count), pltpu.SemaphoreType.DMA((count // CHUNK,))],
        compiler_params=limit(22),
        cost_estimate=cost(2 * count * heads * 128 * 128 * 14, 40 * count * width),
    )(do, *map(far, (rd, o, pq, pk, v, s, q, k)), fq, fk)


def slot_of(index):
    return 2 * index if index < 4 else 2 * index - 7


def outer_rows_kernel(me_ref, left_ref, right_ref, send_ref, keep_ref):
    rows = send_ref.shape[1]
    right = right_ref[...]
    for index in range(8):
        start = pl.multiple_of((me_ref[0] ^ slot_of(index)) * rows, 128)
        ref = keep_ref if index < 4 else send_ref
        ref[index % 4] = tn(left_ref[:, pl.ds(start, rows)], right).astype(BF16)


def outer_rows(me, left, right):
    count, wide = left.shape
    across = right.shape[1]
    out = array((4, wide // 8, across))
    return pl.pallas_call(
        outer_rows_kernel,
        name="outer_rows",
        in_specs=[SMEM, VMEM, VMEM],
        out_specs=[VMEM, VMEM],
        out_shape=[out, out],
        compiler_params=limit(10),
        cost_estimate=cost(2 * count * wide * across, 2 * (count * (wide + across) + wide * across)),
    )(me, left, right)


def outer_cols_kernel(plan, away, me_ref, *refs):
    *ins, send_ref, keep_ref, turned = refs[: len(refs) - len(away) - 1]
    copies = {}
    for at, index in enumerate(away):
        held = refs[len(refs) - len(away) - 1 + at]
        copies[index] = pltpu.make_async_copy(ins[index], held, refs[-1].at[at])
        copies[index].start()
        ins[index] = held
    rows = send_ref.shape[1]
    at = 0

    def by_slot(value):
        for shard in range(8):
            slot = me_ref[0] ^ shard
            turned[(slot >> 1) + 4 * (slot & 1), :, : value.shape[1]] = value[shard * rows : (shard + 1) * rows]

    for left, right in plan:
        across = ins[right].shape[1]
        if left is None:
            by_slot(ins[right][...].astype(BF16))
            keep_ref[:, :, at : at + across] = turned[0:4, :, :across]
            send_ref[:, :, at : at + across] = turned[4:8, :, :across]
            at += across
            continue
        if left in copies:
            copies[left].wait()
        by_slot(ins[left][...].T)
        whole = turned[...].reshape(8 * rows, turned.shape[2])
        for start in range(0, across, TILE):
            value = nn(whole, ins[right][:, start : start + TILE]).astype(BF16)
            keep_ref[:, :, at : at + TILE] = value[: 4 * rows].reshape(4, rows, TILE)
            send_ref[:, :, at : at + TILE] = value[4 * rows :].reshape(4, rows, TILE)
            at += TILE


def outer_cols(me, arrays, plan, away=()):
    across = sum(arrays[right].shape[1] for _, right in plan)
    out = array((4, D // 8, across))
    size = sum(value.size for value in arrays) + D * across
    return pl.pallas_call(
        functools.partial(outer_cols_kernel, plan, away),
        name="outer_cols",
        in_specs=[SMEM] + [ANY if index in away else VMEM for index in range(len(arrays))],
        out_specs=[VMEM, VMEM],
        out_shape=[out, out],
        scratch_shapes=[pltpu.VMEM((8, D // 8, arrays[0].shape[0]), BF16)]
        + [pltpu.VMEM(arrays[index].shape, BF16) for index in away] + [pltpu.SemaphoreType.DMA((max(1, len(away)),))],
        compiler_params=limit(11),
        cost_estimate=cost(2 * 1024 * D * across, 2 * size),
    )(me, *[far(value) if index in away else value for index, value in enumerate(arrays)])


def input_back_kernel(source, groups, me_ref, tok_ref, da_ref, vec_ref, *refs):
    parts, refs = refs[: len(groups)], refs[len(groups) :]
    count = len(source.arrays)
    out_ref, gain1_ref, bias1_ref, w_ref, sems = refs[count:]
    copies = source.copies(me_ref[0], refs[:count], w_ref, sems)
    for copy in copies:
        copy.start()
    for ref in (gain1_ref, bias1_ref):
        ref[...] = jnp.zeros_like(ref)
    for copy in copies:
        copy.wait()

    def body(index, carry):
        rows = [block_rows(2 * index + half, ROWS) for half in range(2)]
        grads = []
        for at in rows:
            grad = None
            for (first, heads), part_ref in zip(groups, parts):
                width = heads * HD
                for part in range(3):
                    cols = slice(part * D + first * HD, part * D + (first + heads) * HD)
                    more = nt(part_ref[at, part * width : (part + 1) * width], w_ref[:, cols])
                    grad = more if grad is None else grad + more
            grads.append(grad)
        for at, grad in zip(rows, grads):
            unit, scale = normalized(tok_ref[at, :].astype(F32))
            value = da_ref[at, :].astype(F32) + norm_back(grad, vec_ref[4:5, :D], unit, scale)
            out_ref[at, :] = value.astype(BF16)
            gain1_ref[...] += column_sums(grad * unit)
        bias1_ref[...] += column_sums(grads[0]) + column_sums(grads[1])
        return carry

    lax.fori_loop(0, tok_ref.shape[0] // (2 * ROWS), body, 0)


def input_back(me, groups, parts, tokens, da, vectors, source):
    count = tokens.shape[0]
    return pl.pallas_call(
        functools.partial(input_back_kernel, source, groups),
        name="input_back",
        in_specs=[SMEM] + [VMEM] * (3 + len(parts)) + source.specs(),
        out_specs=[VMEM] * 3,
        out_shape=[array((count, D)), array((1, D), F32), array((1, D), F32)],
        scratch_shapes=[pltpu.VMEM(source.shape, BF16), source.semaphores()],
        compiler_params=limit(14),
        cost_estimate=cost(2 * count * D * 3 * D, 14 * count * D + 6 * D * D),
    )(me, tokens, da, vectors, *parts, *source.arrays)


def narrow_kernel(source, base, me_ref, g_far, x1_far, vec_ref, *refs):
    if source is None:
        w_ref, out_ref, g_ref, x1_ref, row_sems = refs
        copies = []
    else:
        count = len(source.arrays)
        out_ref, w_ref, g_ref, x1_ref, row_sems, sems = refs[count:]
        copies = source.copies(me_ref[0], refs[:count], w_ref, sems)
    steps = out_ref.shape[0] // ROWS
    rows_here = pl.ds(base, out_ref.shape[0])
    enter = Rows([(g_far.at[rows_here, :], g_ref), (x1_far.at[rows_here, :], x1_ref)], row_sems)
    for copy in copies:
        copy.start()
    for step in range(steps):
        enter.start(step)
    for copy in copies:
        copy.wait()

    def body(step, carry):
        enter.wait(step)
        rows = block_rows(step, ROWS)
        out_ref[rows, :] = (x1_ref[rows, :].astype(F32) + (nn(g_ref[rows, :], w_ref[...]) + vec_ref[3:4, :D])).astype(BF16)
        return carry

    lax.fori_loop(0, steps, body, 0)


def narrow(me, base, count, g, x1, vectors, source):
    first = isinstance(source, Source)
    return pl.pallas_call(
        functools.partial(narrow_kernel, source if first else None, base),
        name="narrow",
        in_specs=[SMEM, ANY, ANY, VMEM] + (source.specs() if first else [VMEM]),
        out_specs=[VMEM] * 2 if first else VMEM,
        out_shape=[array((count, D)), array(source.shape)] if first else array((count, D)),
        scratch_shapes=[pltpu.VMEM((count, FF), BF16), pltpu.VMEM((count, D), BF16), row_semaphores(2, count)]
        + ([source.semaphores()] if first else []),
        compiler_params=limit(10),
        cost_estimate=cost(2 * count * D * FF, 14 * count * D + 8 * D * D),
    )(me, far(g), far(x1), vectors, *(source.arrays if first else [source]))


def fold_kernel(keep_ref, arrived_ref, *outs):
    for index, out in enumerate(outs):
        out[...] = keep_ref[index] + arrived_ref[index]


def fold(keep, arrived):
    slots, rows, across = keep.shape
    return pl.pallas_call(
        fold_kernel,
        name="fold",
        in_specs=[VMEM] * 2,
        out_specs=[VMEM] * slots,
        out_shape=[array((rows, across))] * slots,
        compiler_params=limit(8),
        cost_estimate=cost(keep.size, 6 * keep.size),
    )(keep, arrived)


def total_kernel(*refs):
    *values, out = refs
    result = values[0][...].astype(F32)
    for value in values[1:]:
        result = result + value[...].astype(F32)
    out[...] = result.astype(out.dtype)


def total(*values):
    return pl.pallas_call(
        total_kernel,
        name="total",
        in_specs=[VMEM] * len(values),
        out_specs=VMEM,
        out_shape=array(values[0].shape),
        compiler_params=limit(8),
        cost_estimate=cost(4 * values[0].size, 10 * values[0].size),
    )(*values)


def cross_kernel(keep_ref, arrived_ref, send_x, send_y, top, bottom):
    half = top.shape[1]
    for outs, rows in (((top, send_x, top, send_x), slice(0, half)), ((bottom, bottom, send_y, send_y), slice(half, 2 * half))):
        for slot, out in enumerate(outs):
            out[slot // 2 if outs[0] is outs[2] else slot % 2] = keep_ref[slot, rows, :] + arrived_ref[slot, rows, :]


def cross_over(keep, arrived):
    _, rows, across = keep.shape
    return pl.pallas_call(
        cross_kernel,
        name="cross_over",
        in_specs=[VMEM] * 2,
        out_specs=[VMEM] * 4,
        out_shape=[array((2, rows // 2, across))] * 4,
        compiler_params=limit(8),
        cost_estimate=cost(keep.size, 6 * keep.size),
    )(keep, arrived)


def turn_kernel(top, bottom, over_x, over_y, send_y, send_x, mine_top, mine_bottom):
    mine_top[...] = top[0] + over_x[0]
    send_y[...] = top[1] + over_x[1]
    mine_bottom[...] = bottom[0] + over_y[0]
    send_x[...] = bottom[1] + over_y[1]


def turn_over(top, bottom, over_x, over_y):
    _, half, across = top.shape
    return pl.pallas_call(
        turn_kernel,
        name="turn_over",
        in_specs=[VMEM] * 4,
        out_specs=[VMEM] * 4,
        out_shape=[array((half, across))] * 4,
        compiler_params=limit(8),
        cost_estimate=cost(4 * half * across, 24 * half * across),
    )(top, bottom, over_x, over_y)


def halve_kernel(side_ref, top, last_y, bottom, last_x, own_ref, other_ref):
    for side, one, two in ((0, top, last_y), (1, bottom, last_x)):
        value = one[...] + two[...]

        @pl.when(side_ref[0] == side)
        def _():
            own_ref[...] = value

        @pl.when(side_ref[0] != side)
        def _():
            other_ref[...] = value


def halve(side, top, last_y, bottom, last_x):
    return pl.pallas_call(
        halve_kernel,
        name="halve",
        in_specs=[SMEM] + [VMEM] * 4,
        out_specs=[VMEM] * 2,
        out_shape=[array(top.shape)] * 2,
        compiler_params=limit(8),
        cost_estimate=cost(2 * top.size, 12 * top.size),
    )(side, top, last_y, bottom, last_x)


def stack_kernel(top, last_y, bottom, last_x, out_ref):
    half = top.shape[0]
    out_ref[:half, :] = top[...] + last_y[...]
    out_ref[half:, :] = bottom[...] + last_x[...]


def stack(top, last_y, bottom, last_x):
    half, across = top.shape
    return pl.pallas_call(
        stack_kernel,
        name="stack",
        in_specs=[VMEM] * 4,
        out_specs=VMEM,
        out_shape=array((2 * half, across)),
        compiler_params=limit(8),
        cost_estimate=cost(2 * top.size, 12 * top.size),
    )(top, last_y, bottom, last_x)


def join_kernel(side_ref, own_ref, other_ref, out_ref):
    half = own_ref.shape[0]
    out_ref[block_rows(side_ref[0], half), :] = own_ref[...].astype(F32)
    out_ref[block_rows(1 - side_ref[0], half), :] = other_ref[...].astype(F32)


def join(side, own, other):
    half, across = own.shape
    return pl.pallas_call(
        join_kernel,
        name="join",
        in_specs=[SMEM] + [VMEM] * 2,
        out_specs=VMEM,
        out_shape=array((2 * half, across), F32),
        compiler_params=limit(8),
        cost_estimate=cost(half * across, 12 * half * across),
    )(side, own, other)


def write_lines(lines, outs):
    at = 0
    for out in outs:
        size = out.shape[0]
        for start in range(0, size, 128):
            count = min(128, size - start)
            out[pl.ds(start, count)] = lines[at : at + 1, :count].reshape(count)
            at += 1


def publish_kernel(groups, side_ref, own_ref, other_ref, one_ref, two_ref, qkvw_ref, outw_ref, fmap_ref, *outs):
    half = own_ref.shape[0]
    for side, ref in ((side_ref[0], own_ref), (1 - side_ref[0], other_ref)):
        rows = block_rows(side, half)
        outw_ref[rows, :] = ref[:, :D].astype(F32)
        first, heads = groups[0]
        width = heads * HD
        for part in range(3):
            value = ref[:, D + part * width : D + (part + 1) * width]
            qkvw_ref[rows, part * D + first * HD : part * D + first * HD + width] = value.astype(F32)
    last = one_ref[...].astype(F32) + two_ref[...].astype(F32)
    first, heads = groups[1]
    width = heads * HD
    for part in range(3):
        qkvw_ref[:, part * D + first * HD : part * D + first * HD + width] = last[:, part * width : (part + 1) * width]
    fmap_ref[...] = last[:, 3 * width : 3 * width + 2 * HD]
    write_lines(last[:, 3 * width + 2 * HD :], outs)


def publish(groups, side, own, other, one, two, sizes):
    rows = one.shape[0]
    return pl.pallas_call(
        functools.partial(publish_kernel, groups),
        name="publish",
        in_specs=[SMEM] + [VMEM] * 4,
        out_specs=[VMEM] * (3 + len(sizes)),
        out_shape=[array((rows, 3 * D), F32), array((rows, D), F32), array((rows, 2 * HD), F32)] + [array((size,), F32) for size in sizes],
        compiler_params=limit(8),
        cost_estimate=cost(rows * 3 * D * 4, rows * 3 * D * 12),
    )(side, own, other, one, two)


def line_count(sizes):
    return sum(-(-size // 128) for size in sizes)


def to_lines(vector, start, size):
    lines = []
    for at in range(0, size, 128):
        count = min(128, size - at)
        line = vector[:, start + at : start + at + count]
        if count < 128:
            line = jnp.concatenate([line, jnp.zeros((1, 128 - count), F32)], 1)
        lines.append(line)
    return lines


def pack_kernel(*refs):
    *vectors, fm_ref, w_ref, out_ref = refs
    width = w_ref.shape[1]
    out_ref[:, :width] = w_ref[...]
    out_ref[:, width : width + 128] = fm_ref[...]
    lines = []
    for vector in vectors:
        size = vector.shape[0]
        lines += to_lines(vector[...].astype(F32).reshape(1, size), 0, size)
    lines += [jnp.zeros((1, 128), F32)] * (w_ref.shape[0] - len(lines))
    out_ref[:, width + 128 :] = jnp.concatenate(lines, 0).astype(BF16)


def pack(w, fm, vectors):
    rows, width = w.shape
    return pl.pallas_call(
        pack_kernel,
        name="pack",
        in_specs=[VMEM] * (len(vectors) + 2),
        out_specs=VMEM,
        out_shape=array((rows, width + 256)),
        compiler_params=limit(56),
    )(*vectors, fm, w)


def small_grads_kernel(shards, *refs):
    *vectors, out_ref = refs
    rows = out_ref.shape[0] // shards
    for shard in range(shards):
        lines = []
        for vector in vectors:
            size = vector.shape[1] // shards
            lines += to_lines(vector[...], shard * size, size)
        lines += [jnp.zeros((1, 128), F32)] * (rows - len(lines))
        out_ref[shard * rows : (shard + 1) * rows, :] = jnp.concatenate(lines, 0)


def small_grads(shards, vectors):
    return pl.pallas_call(
        functools.partial(small_grads_kernel, shards),
        name="small_grads",
        in_specs=[VMEM] * len(vectors),
        out_specs=VMEM,
        out_shape=array((D, 128), F32),
        compiler_params=limit(8),
    )(*vectors)


def small_owned_kernel(lines_ref, *outs):
    write_lines(lines_ref[...], outs)


def small_owned(lines, sizes):
    return pl.pallas_call(
        small_owned_kernel,
        name="small_owned",
        in_specs=[VMEM],
        out_specs=[VMEM] * len(sizes),
        out_shape=[array((size,), F32) for size in sizes],
        compiler_params=limit(8),
    )(lines)


GROUPS = ((0, 8), (8, 4))


def after(value, *others):
    return lax.optimization_barrier((value, *others))[0]


def exchange(value, axis, mask):
    return lax.ppermute(value, axis, [(i, i ^ mask) for i in range(lax.axis_size(axis))])


class Gather:
    def __init__(self, shard):
        self.shard, self.rows = shard, shard.shape[0]
        self.hand = by_hand(self.rows)

    def start(self, *others):
        if not self.hand:
            self.full = lax.all_gather(self.shard, "fsdp", axis=0, tiled=True)
            return ()
        shard = after(self.shard, *others) if others else self.shard
        self.over_x, self.over_y = exchange(shard, "fsdp", 2), exchange(shard, "fsdp", 4)
        self.sibling = exchange(shard, "fsdp", 1)
        return self.over_x, self.over_y

    def relay(self, *others):
        if not self.hand:
            return ()
        half = self.rows // 2
        over_x, over_y = self.over_x, self.over_y
        if others:
            over_x, over_y = lax.optimization_barrier((over_x, over_y, *others))[:2]
        self.pieces = over_y[:half], over_x[half:]
        self.upper, self.lower = exchange(self.pieces[0], "fsdp", 2), exchange(self.pieces[1], "fsdp", 4)
        self.shared = [((3, 0), exchange(over_x, "fsdp", 1)), ((5, 0), exchange(over_y, "fsdp", 1))]
        return self.pieces

    def finish(self, *others):
        if not self.hand:
            return Source([(0, 0)], [self.full], self.rows, self.full.shape[0])
        half = self.rows // 2
        upper, lower = self.upper, self.lower
        if others:
            upper, lower = lax.optimization_barrier((upper, lower, *others))[:2]
        held = [((0, 0), self.shard), ((2, 0), self.over_x), ((4, 0), self.over_y), ((1, 0), self.sibling)] + self.shared
        held += [((6, 0), upper), ((6, half), lower)]
        held += [((7, 0), exchange(upper, "fsdp", 1)), ((7, half), exchange(lower, "fsdp", 1))]
        return Source([place for place, _ in held], [part for _, part in held], self.rows, 8 * self.rows)


def by_hand(rows):
    return lax.axis_size("fsdp") == 8 and lax.axis_size("dp") == 4 and rows % 32 == 0


class Scatter:
    def __init__(self, pair):
        send, self.keep = pair
        self.arrived = exchange(send, "fsdp", 1)

    def cross(self, *others):
        send_x, send_y, self.top, self.bottom = cross_over(self.keep, after(self.arrived, *others))
        self.over_x, self.over_y = exchange(send_x, "fsdp", 2), exchange(send_y, "fsdp", 4)
        return send_x, send_y

    def turn(self, *others):
        over_x, over_y = lax.optimization_barrier((self.over_x, self.over_y, *others))[:2]
        send_y, send_x, self.top, self.bottom = turn_over(self.top, self.bottom, over_x, over_y)
        self.last_y, self.last_x = exchange(send_y, "fsdp", 4), exchange(send_x, "fsdp", 2)
        return send_y, send_x

    def finish(self, *others):
        last_y, last_x = lax.optimization_barrier((self.last_y, self.last_x, *others))[:2]
        return self.top, last_y, self.bottom, last_x

    def straight(self, *others):
        self.mine, *away = fold(self.keep, after(self.arrived, *others))
        self.moved = [exchange(value, "fsdp", mask) for value, mask in zip(away, (2, 4, 6))]
        return away

    def arrive(self, *others):
        return total(self.mine, *lax.optimization_barrier((*self.moved, *others))[:3])


class Planes:
    def __init__(self, side, values):
        self.own, self.other = halve(side, *values)
        self.moved = exchange(self.other, "dp", 1)

    def mirror(self, *others):
        self.own = self.own + after(self.moved, *others)
        self.moved = exchange(self.own, "dp", 3)
        return self.own

    def back(self, *others):
        self.own = self.own + after(self.moved, *others)
        self.moved = exchange(self.own, "dp", 1)
        return self.own

    def finish(self, *others):
        return self.own, after(self.moved, *others)


def outer(left, right):
    return tn(left, right).astype(BF16)


def on_device(
    tokens, lengths, qkv_weight, qkv_bias, out_weight, out_bias, fc_weight, fc_bias, proj_weight, proj_bias,
    norm1_gain, norm1_bias, norm2_gain, norm2_bias, feature_map, cotangent,
):
    shards = lax.axis_size("fsdp")
    me = lax.axis_index("fsdp").astype(jnp.int32).reshape(1)
    plane = lax.axis_index("dp").astype(jnp.int32).reshape(1)
    side = (plane ^ (plane >> 1)) & 1
    qkv_weight, me, side = lax.optimization_barrier((qkv_weight, me, side))
    small = [qkv_bias, out_bias, fc_bias, proj_bias, norm1_gain, norm1_bias, norm2_gain, norm2_bias]
    first = Gather(pack(qkv_weight, feature_map, small))
    second = Gather(jnp.concatenate([fc_weight, out_weight], 1))
    third = Gather(proj_weight)
    first.start()
    second.start(*first.relay())
    first_source = first.finish()
    v, pq, pk, vectors, fq, fk, h1, q, k, v_far, pq_far, pk_far = project(
        me, lengths, tokens, first_source, [value.shape[0] for value in small]
    )
    second.relay(v)
    o, o_far, rd, s = attend(lengths, pq, pk, v)
    parts = second.finish(o)
    third.start(o)
    h2, g, slope, w_fc, g_far, x1 = widen(me, o, tokens, vectors, parts)
    g = after(g, *third.relay(g))
    hand = by_hand(qkv_weight.shape[0])
    summed = lambda share: lax.psum(share.astype(BF16), "dp").astype(F32)
    over = lambda value: lax.psum_scatter(value, "fsdp", scatter_dimension=0, tiled=True)
    if hand:
        pair = outer_rows(me, g, cotangent)
        proj_scatter = Scatter(pair)
        slope = after(slope, pair[0])
        third_source = third.finish(pair[0])
    else:
        third_source = third.finish()
    df, projb, fcb = slope_back(me, cotangent, slope, third_source)
    if hand:
        pair = outer_cols(me, [h2, df], [(0, 1)])
        fc_scatter = Scatter(pair)
        df = after(df, *proj_scatter.cross(pair[0]))
    da, do, gain2, bias2, outb = middle_back(cotangent, df, x1, vectors, w_fc)
    if hand:
        do = after(do, *proj_scatter.turn(do), *fc_scatter.cross(do))
    parts, sums, maps = [], [], []
    for index, (start, heads) in enumerate(GROUPS):
        dproj, sum_grad, fmap_grad = attend_back(start, heads, do, rd, o_far, pq_far, pk_far, v_far, s, q, k, fq, fk)
        parts.append(dproj)
        sums.append(sum_grad)
        maps.append(fmap_grad)
        if hand and index == 0:
            proj_planes = Planes(side, proj_scatter.finish(dproj))
            left = after(h1, proj_planes.other, *fc_scatter.turn(dproj))
            pair = outer_cols(me, [o_far, da, left, dproj], [(0, 1), (2, 3)], (0, 2))
            qkv_scatter = Scatter(pair)
            fc_planes = Planes(side, fc_scatter.finish(pair[0]))
            do = after(do, fc_planes.other, proj_planes.mirror(pair[0]))
    if hand:
        tokens = after(tokens, proj_planes.back(dproj), *qkv_scatter.cross(dproj), fc_planes.mirror(dproj))
    input_grad, gain1, bias1 = input_back(me, GROUPS, parts, tokens, da, vectors, first_source)
    spread = lambda values: jnp.concatenate([
        value[:, part * heads * HD : (part + 1) * heads * HD] for part in range(3) for (_, heads), value in zip(GROUPS, values)
    ], 1)
    ordered = spread(sums)
    small = [ordered[:, : 2 * D], ordered[:, 2 * D :], outb, fcb, projb, gain1, bias1, gain2, bias2]
    table = small_grads(shards, small)
    sizes = [value.shape[1] // shards for value in small]
    if hand:
        left = after(h1, *qkv_scatter.turn(table))
        pair = outer_cols(me, [left, dproj, jnp.concatenate(maps, 0), table], [(0, 1), (None, 2), (None, 3)], (0,))
        last_scatter = Scatter(pair)
        projw_grad = join(side, *proj_planes.finish(pair[0]))
        x1 = after(x1, pair[0], projw_grad, fc_planes.back(pair[0]))
    if hand:
        qkv_planes = Planes(side, qkv_scatter.finish(pair[0]))
        x1 = after(x1, qkv_planes.other)
    piece, w_proj = narrow(me, 0, ROWS, g_far, x1, vectors, third_source)
    pieces = [piece]
    for base in range(ROWS, tokens.shape[0], ROWS):
        if hand and base == ROWS:
            x1 = after(x1, *last_scatter.straight(piece))
        if hand and base == 2 * ROWS:
            fcw_grad = join(side, *fc_planes.finish(pieces[-1]))
            x1 = after(x1, fcw_grad, qkv_planes.mirror(pieces[-1]))
        if hand and base == 3 * ROWS:
            share = last_scatter.arrive(pieces[-1])
            x1 = after(x1, share)
        pieces.append(narrow(me, base, ROWS, g_far, x1, vectors, w_proj))
    block_out = jnp.concatenate(pieces, 0)
    if hand:
        qkv_planes.back(pieces[-1])
        share = share + after(exchange(share, "dp", 1), pieces[-1])
        qkvw_grad, outw_grad, fmap_grad, *vectors = publish(
            GROUPS, side, *qkv_planes.finish(), share, exchange(share, "dp", 3), sizes
        )
    else:
        vectors = small_owned(lax.psum(over(table), "dp"), sizes)
    qkb, vb, outb, fcb, projb, gain1, bias1, gain2, bias2 = vectors
    if not hand:
        projw_grad = summed(over(outer(g_far, cotangent)))
        fcw_grad, outw_grad = summed(over(outer(h2, df))), summed(over(outer(o_far, da)))
        qkvw_grad, fmap_grad = summed(over(outer(h1, spread(parts)))), summed(over(jnp.concatenate(maps, 0)))
    return (
        block_out, input_grad, qkvw_grad, qkb, vb, outw_grad, outb, fcw_grad, fcb,
        projw_grad, projb, gain1, bias1, gain2, bias2, fmap_grad,
    )


def solution(mesh):
    rows = P(("dp", "fsdp"), None)
    wide = P("fsdp", None)
    flat = P("fsdp")
    in_specs = (
        rows, P(("dp", "fsdp")), wide, flat, wide, flat, wide, flat, wide, flat, flat, flat, flat, flat, wide, rows,
    )
    out_specs = (rows, rows, wide, flat, flat, wide, flat, wide, flat, wide, flat, flat, flat, flat, flat, wide)
    return jax.shard_map(on_device, mesh=mesh, in_specs=in_specs, out_specs=out_specs, check_vma=False)
```

```python
import functools

import jax
import jax.numpy as jnp
from jax import lax
from jax.experimental import pallas as pl
from jax.experimental.pallas import tpu as pltpu
from jax.sharding import PartitionSpec as P

D = 768
HEADS = 12
HD = 64
PAIRS = HEADS // 2
FF = 3072
ROWS = 256
CHUNK = 256
TILE = 256
EPSILON = 1e-05
SAFE = 60.0
SCALE = 20
F32 = jnp.float32
BF16 = jnp.bfloat16
ROOT = 0.7978845608028654
CUBE = 0.044715
VMEM = pl.BlockSpec(memory_space=pltpu.VMEM)
SMEM = pl.BlockSpec(memory_space=pltpu.SMEM)
ANY = pl.BlockSpec(memory_space=pl.ANY)
VECTORS = (8, FF)
MAPS = (PAIRS, 128, 256)


def nn(left, right):
    return lax.dot_general(left, right, (((1,), (0,)), ((), ())), preferred_element_type=F32)


def nt(left, right):
    return lax.dot_general(left, right, (((1,), (1,)), ((), ())), preferred_element_type=F32)


def tn(left, right):
    return lax.dot_general(left, right, (((0,), (0,)), ((), ())), preferred_element_type=F32)


def limit(mib):
    return pltpu.CompilerParams(vmem_limit_bytes=mib * 1024 * 1024)


def cost(flops, size, trans=0):
    return pl.CostEstimate(flops=int(SCALE * flops), bytes_accessed=int(size), transcendentals=int(trans))


def array(shape, kind=BF16):
    return jax.ShapeDtypeStruct(shape, kind)


def near(value):
    return pltpu.with_memory_space_constraint(value, pltpu.VMEM)


def far(value):
    return pltpu.with_memory_space_constraint(value, pltpu.HBM)


def lanes(shape):
    return lax.broadcasted_iota(jnp.int32, shape, 1)


def block_rows(index, count):
    return pl.ds(pl.multiple_of(index * count, count), count)


def normalized(values):
    middle = jnp.mean(values, -1, keepdims=True)
    centred = values - middle
    spread = jnp.mean(centred * centred, -1, keepdims=True)
    scale = lax.rsqrt(spread + EPSILON)
    return centred * scale, scale


def norm_back(grad, gain, unit, scale):
    scaled = grad * gain
    first = jnp.mean(scaled, -1, keepdims=True)
    second = jnp.mean(scaled * unit, -1, keepdims=True)
    return (scaled - first - unit * second) * scale


def swap_halves(values):
    return pltpu.roll(values, 64, 1)


def block_ones(size):
    row = lax.broadcasted_iota(jnp.int32, (size, size), 0) // HD
    col = lax.broadcasted_iota(jnp.int32, (size, size), 1) // HD
    return jnp.where(row == col, 1.0, 0.0).astype(BF16)


def build_maps(map_ref, fq, fk):
    fq[...] = jnp.zeros_like(fq)
    fk[...] = jnp.zeros_like(fk)
    low = lanes((HD, 2 * HD)) < HD
    for head in range(HEADS):
        block = map_ref[head * HD : (head + 1) * HD, :].astype(F32)
        turned = swap_halves(block)
        row, col = (head % 2) * HD, (head % 2) * 2 * HD
        fq[head // 2, row : row + HD, col : col + 2 * HD] = jnp.where(low, block, -turned).astype(BF16)
        fk[head // 2, row : row + HD, col : col + 2 * HD] = jnp.where(low, turned, -block).astype(BF16)


class Source:
    def __init__(self, places, arrays, rows, total):
        self.places, self.arrays, self.rows = places, list(arrays), rows
        self.shape = (total, arrays[0].shape[1])

    def specs(self):
        return [ANY] * len(self.arrays)

    def semaphores(self):
        return pltpu.SemaphoreType.DMA((len(self.arrays),))

    def copies(self, me, refs, held, sems, first=0, count=None):
        made = []
        count = self.shape[1] - first if count is None else count
        cols = pl.ds(first, count)
        for at, ((slot, offset), ref) in enumerate(zip(self.places, refs)):
            start = 0 if len(self.places) == 1 else pl.multiple_of((me ^ slot) * self.rows + offset, 16)
            made.append(pltpu.make_async_copy(ref.at[:, cols], held.at[pl.ds(start, ref.shape[0]), cols], sems.at[at]))
        return made


class Rows:
    def __init__(self, pairs, sems):
        self.pairs, self.sems = pairs, sems

    def copies(self, step):
        rows = block_rows(step, ROWS)
        return [
            pltpu.make_async_copy(source.at[rows, :], target.at[rows, :], self.sems.at[at, step])
            for at, (source, target) in enumerate(self.pairs)
        ]

    def start(self, step):
        for copy in self.copies(step):
            copy.start()

    def wait(self, step):
        for copy in self.copies(step):
            copy.wait()


def row_semaphores(pairs, count):
    return pltpu.SemaphoreType.DMA((pairs, count // ROWS))


def read_vectors(table, rows, sizes, out):
    for shard in range(table.shape[0] // rows):
        line = shard * rows
        for row, size in enumerate(sizes):
            for at in range(0, size, 128):
                count = min(128, size - at)
                out[row : row + 1, shard * size + at : shard * size + at + count] = table[line : line + 1, :count].astype(F32)
                line += 1


def project_kernel(source, sizes, me_ref, len_ref, tok_ref, *refs):
    count = len(source.arrays)
    v_ref, pq_ref, pk_ref, vec_ref, fq, fk, *far_refs, w_ref, h_ref, q_ref, k_ref, side_sems, sems, row_sems = refs[count:]
    leave = Rows(list(zip((h_ref, q_ref, k_ref, v_ref, pq_ref, pk_ref), far_refs)), row_sems)
    steps = tok_ref.shape[0] // ROWS
    side = source.copies(me_ref[0], refs[:count], w_ref, side_sems, 3 * D)
    main = source.copies(me_ref[0], refs[:count], w_ref, sems, 0, 3 * D)
    for copy in side + main:
        copy.start()
    vec_ref[...] = jnp.zeros_like(vec_ref)
    ones = block_ones(4 * HD)
    for copy in side:
        copy.wait()
    read_vectors(w_ref.at[:, 3 * D + 128 :], source.rows, sizes, vec_ref)
    build_maps(w_ref.at[:, 3 * D : 3 * D + 128], fq, fk)

    def norm(step, carry):
        rows = block_rows(step, ROWS)
        unit, _ = normalized(tok_ref[rows, :].astype(F32))
        h_ref[rows, :] = (unit * vec_ref[4:5, :D] + vec_ref[5:6, :D]).astype(BF16)
        return carry

    lax.fori_loop(0, steps, norm, 0)
    for copy in main:
        copy.wait()

    def body(step, carry):
        rows = block_rows(step, ROWS)
        h = h_ref[rows, :]
        wide = [(nn(h, w_ref[:, p * D : (p + 1) * D]) + vec_ref[0:1, p * D : (p + 1) * D]).astype(BF16) for p in range(3)]
        for out, value in zip((q_ref, k_ref, v_ref), wide):
            out[rows, :] = value
        place = step * ROWS + lax.broadcasted_iota(jnp.int32, (ROWS, 1), 0)
        live = (place < len_ref[0]).astype(F32)
        largest = jnp.zeros((ROWS, 256), F32)
        for part, (maps, out) in enumerate(((fq, pq_ref), (fk, pk_ref))):
            u = [nn(wide[part][:, p * 128 : (p + 1) * 128], maps[p]) for p in range(PAIRS)]
            e = [jnp.exp(value) for value in u]
            total = [nn(value.astype(BF16), ones) for value in e]
            for p in range(PAIRS):
                largest = jnp.maximum(largest, u[p])
                share = e[p] * pl.reciprocal(total[p], approx=True)
                if part == 1:
                    share = share * live
                out[rows, p * 256 : (p + 1) * 256] = share.astype(BF16)

        @pl.when(jnp.logical_not(jnp.max(largest) <= SAFE))
        def _():
            for part, (maps, rows_ref, out) in enumerate(((fq, q_ref, pq_ref), (fk, k_ref, pk_ref))):
                for p in range(PAIRS):
                    u = nn(rows_ref[rows, p * 128 : (p + 1) * 128], maps[p])
                    for group in range(4):
                        piece = u[:, group * HD : (group + 1) * HD]
                        e = jnp.exp(piece - jnp.max(piece, -1, keepdims=True))
                        share = e / jnp.sum(e, -1, keepdims=True)
                        if part == 1:
                            share = share * live
                        out[rows, p * 256 + group * HD : p * 256 + (group + 1) * HD] = share.astype(BF16)

        leave.start(step)
        return carry

    lax.fori_loop(0, steps, body, 0)
    for step in range(steps):
        leave.wait(step)


def project(me, lengths, tokens, source, sizes):
    count = tokens.shape[0]
    return pl.pallas_call(
        functools.partial(project_kernel, source, sizes),
        name="project",
        in_specs=[SMEM, SMEM, VMEM] + source.specs(),
        out_specs=[VMEM] * 6 + [ANY] * 6,
        out_shape=[array((count, D)), array((count, 2 * D)), array((count, 2 * D)), array(VECTORS, F32), array(MAPS), array(MAPS)]
        + [pltpu.HBM((count, D), BF16)] * 4 + [pltpu.HBM((count, 2 * D), BF16)] * 2,
        scratch_shapes=[pltpu.VMEM(source.shape, BF16)] + [pltpu.VMEM((count, D), BF16)] * 3
        + [source.semaphores(), source.semaphores(), row_semaphores(6, count)],
        compiler_params=limit(17),
        cost_estimate=cost(0, 0),
    )(me, lengths, tokens, *source.arrays)


def value_pair(v_pair):
    low = lanes(v_pair.shape) < HD
    wide = v_pair.astype(F32)
    return (
        jnp.where(low, wide, 1.0).astype(BF16),
        jnp.where(low, swap_halves(wide), 1.0).astype(BF16),
    )


def attend_kernel(group, len_ref, pq_ref, pk_ref, v_ref, o_ref, o_far, rd_far, s_far, rd_ref, s_ref, state, row_sems, s_sems):
    leave = Rows([(o_ref, o_far), (rd_ref, rd_far)], row_sems)
    leave_state = lambda step: pltpu.make_async_copy(s_ref.at[step], s_far.at[step], s_sems.at[step])
    steps = v_ref.shape[0] // CHUNK
    state[...] = jnp.zeros_like(state)
    row = lax.broadcasted_iota(jnp.int32, (CHUNK, CHUNK), 0)
    col = lax.broadcasted_iota(jnp.int32, (CHUNK, CHUNK), 1)
    causal = row >= col
    low = lanes((CHUNK, 128)) < HD
    place = lax.broadcasted_iota(jnp.int32, (CHUNK, 128), 0)

    def body(step, carry):
        rows = block_rows(step, CHUNK)
        live = (step * CHUNK + place < len_ref[0]).astype(F32)
        for first in range(0, PAIRS, group):
            pairs = range(first, first + group)
            heads = range(2 * first, 2 * (first + group))
            cols = [slice(head * 128, (head + 1) * 128) for head in range(HEADS)]
            pq = {head: pq_ref[rows, cols[head]] for head in heads}
            pk = {head: pk_ref[rows, cols[head]] for head in heads}
            vx = {}
            for pair in pairs:
                vx[2 * pair], vx[2 * pair + 1] = value_pair(v_ref[rows, cols[pair]])
            scores = {head: nt(pq[head], pk[head]) for head in heads}
            prior = {head: state[head].astype(BF16) for head in heads}
            more = {head: tn(pk[head], vx[head]) for head in heads}
            far = {head: nn(pq[head], prior[head]) for head in heads}
            scores = {head: jnp.where(causal, scores[head], 0.0).astype(BF16) for head in heads}
            sums = {head: nn(scores[head], vx[head]) + far[head] for head in heads}
            for head in heads:
                s_ref[step, head] = prior[head]
                state[head] += more[head]
            for pair in pairs:
                one, two = sums[2 * pair], sums[2 * pair + 1]
                numer = jnp.where(low, one, swap_halves(two))
                denom = jnp.where(low, swap_halves(one), two)
                rd = live / denom
                rd_ref[rows, cols[pair]] = rd.astype(BF16)
                o_ref[rows, cols[pair]] = (numer * rd).astype(BF16)
        leave.start(step)
        leave_state(step).start()
        return carry

    lax.fori_loop(0, steps, body, 0)
    for step in range(steps):
        leave.wait(step)
        leave_state(step).wait()


def attend(lengths, pq, pk, v, group=3):
    count = v.shape[0]
    steps = count // CHUNK
    return pl.pallas_call(
        functools.partial(attend_kernel, group),
        name="attend",
        in_specs=[SMEM, VMEM, VMEM, VMEM],
        out_specs=[VMEM] + [ANY] * 3,
        out_shape=[array((count, D))] + [pltpu.HBM((count, D), BF16)] * 2 + [pltpu.HBM((steps, HEADS, 128, 128), BF16)],
        scratch_shapes=[
            pltpu.VMEM((count, D), BF16), pltpu.VMEM((steps, HEADS, 128, 128), BF16), pltpu.VMEM((HEADS, 128, 128), F32),
            row_semaphores(2, count), pltpu.SemaphoreType.DMA((steps,)),
        ],
        compiler_params=limit(10),
        cost_estimate=cost(2 * count * HEADS * 128 * 512, 20 * count * D),
    )(lengths, pq, pk, v)


def gelu_pair(f):
    low = f.astype(BF16)
    square = low * low
    bend = jnp.tanh(low * (BF16(ROOT) + BF16(ROOT * CUBE) * square))
    share = BF16(0.5) + BF16(0.5) * bend
    value = low * share
    slope = share + value * (BF16(1.0) - share) * (BF16(2 * ROOT) + BF16(6 * ROOT * CUBE) * square)
    return value, slope


def widen_kernel(source, me_ref, o_ref, tok_ref, vec_ref, *refs):
    count = len(source.arrays)
    h2_ref, g_ref, slope_ref, w_ref, g_far, x1_far, x1_ref, side_sems, sems, g_sems, x1_sems = refs[count:]
    leave, leave_x1 = Rows([(g_ref, g_far)], g_sems), Rows([(x1_ref, x1_far)], x1_sems)
    steps = tok_ref.shape[0] // ROWS
    side = source.copies(me_ref[0], refs[:count], w_ref, side_sems, FF)
    main = source.copies(me_ref[0], refs[:count], w_ref, sems, 0, FF)
    for copy in side + main:
        copy.start()
    for copy in side:
        copy.wait()

    def middle(index, carry):
        rows = block_rows(index, 2 * ROWS)
        x1 = tok_ref[rows, :].astype(F32) + (nn(o_ref[rows, :], w_ref[:, FF:]) + vec_ref[1:2, :D])
        x1_ref[rows, :] = x1.astype(BF16)
        unit, _ = normalized(x1)
        h2_ref[rows, :] = (unit * vec_ref[6:7, :D] + vec_ref[7:8, :D]).astype(BF16)
        leave_x1.start(2 * index)
        leave_x1.start(2 * index + 1)
        return carry

    lax.fori_loop(0, steps // 2, middle, 0)
    for copy in main:
        copy.wait()

    def body(index, carry):
        rows = block_rows(index, 2 * ROWS)
        h2 = h2_ref[rows, :]
        for part in range(4):
            cols = slice(part * D, (part + 1) * D)
            g_ref[rows, cols], slope_ref[rows, cols] = gelu_pair(nn(h2, w_ref[:, cols]) + vec_ref[2:3, cols])
        leave.start(2 * index)
        leave.start(2 * index + 1)
        return carry

    lax.fori_loop(0, steps // 2, body, 0)
    for step in range(steps):
        leave_x1.wait(step)
        leave.wait(step)


def widen(me, o, tokens, vectors, source):
    count = tokens.shape[0]
    return pl.pallas_call(
        functools.partial(widen_kernel, source),
        name="widen",
        in_specs=[SMEM, VMEM, VMEM, VMEM] + source.specs(),
        out_specs=[VMEM] * 4 + [ANY] * 2,
        out_shape=[
            array((count, D)), array((count, FF)), pltpu.VMEM((count, FF), BF16), pltpu.VMEM(source.shape, BF16),
            pltpu.HBM((count, FF), BF16), pltpu.HBM((count, D), BF16),
        ],
        scratch_shapes=[
            pltpu.VMEM((count, D), BF16), source.semaphores(), source.semaphores(), row_semaphores(1, count), row_semaphores(1, count),
        ],
        compiler_params=limit(10),
        cost_estimate=cost(2 * count * D * 5 * D, 26 * count * D + 10 * D * D, count * FF),
    )(me, o, tokens, vectors, *source.arrays)


def column_sums(values):
    return jnp.sum(values, 0, keepdims=True)


def slope_back_kernel(source, me_ref, cot_ref, slope_ref, *refs):
    count = len(source.arrays)
    df_ref, projb_ref, fcb_ref, wp_ref, sems = refs[count:]
    copies = source.copies(me_ref[0], refs[:count], wp_ref, sems)
    for copy in copies:
        copy.start()
    projb_ref[...] = column_sums(cot_ref[...].astype(F32))
    fcb_ref[...] = jnp.zeros_like(fcb_ref)
    for copy in copies:
        copy.wait()

    def body(step, carry):
        rows = block_rows(step, 2 * ROWS)
        cot = cot_ref[rows, :]
        for part in range(4):
            cols = slice(part * D, (part + 1) * D)
            df = nt(cot, wp_ref[cols, :]).astype(BF16) * slope_ref[rows, cols]
            df_ref[rows, cols] = df
            fcb_ref[:, cols] += column_sums(df.astype(F32))
        return carry

    lax.fori_loop(0, cot_ref.shape[0] // (2 * ROWS), body, 0)


def slope_back(me, cot, slope, source):
    count = cot.shape[0]
    return pl.pallas_call(
        functools.partial(slope_back_kernel, source),
        name="slope_back",
        in_specs=[SMEM, VMEM, VMEM] + source.specs(),
        out_specs=[VMEM] * 3,
        out_shape=[array((count, FF)), array((1, D), F32), array((1, FF), F32)],
        scratch_shapes=[pltpu.VMEM(source.shape, BF16), source.semaphores()],
        compiler_params=limit(14),
        cost_estimate=cost(2 * count * D * 4 * D, 30 * count * D + 18 * D * D),
    )(me, cot, near(slope), *source.arrays)


def middle_back_kernel(
    cot_ref, df_ref, x1_far, vec_ref, w_ref, da_ref, do_ref, gain2_ref, bias2_ref, outb_ref, x1_ref, row_sems
):
    enter = Rows([(x1_far, x1_ref)], row_sems)
    steps = cot_ref.shape[0] // ROWS
    for step in range(steps):
        enter.start(step)
    for ref in (gain2_ref, bias2_ref, outb_ref):
        ref[...] = jnp.zeros_like(ref)

    def body(index, carry):
        blocks = [2 * index, 2 * index + 1]
        rows = [block_rows(step, ROWS) for step in blocks]
        totals = [nt(df_ref[at, :], w_ref[:, :FF]) for at in rows]
        for step in blocks:
            enter.wait(step)
        das = []
        for at, total in zip(rows, totals):
            unit, scale = normalized(x1_ref[at, :].astype(F32))
            dx1 = cot_ref[at, :].astype(F32) + norm_back(total, vec_ref[6:7, :D], unit, scale)
            da = dx1.astype(BF16)
            das.append(da)
            da_ref[at, :] = da
            do_ref[at, :] = nt(da, w_ref[:, FF:]).astype(BF16)
            gain2_ref[...] += column_sums(total * unit)
        bias2_ref[...] += column_sums(totals[0]) + column_sums(totals[1])
        outb_ref[...] += column_sums(das[0].astype(F32)) + column_sums(das[1].astype(F32))
        return carry

    lax.fori_loop(0, steps // 2, body, 0)


def middle_back(cot, df, x1, vectors, w):
    count = cot.shape[0]
    return pl.pallas_call(
        middle_back_kernel,
        name="middle_back",
        in_specs=[VMEM] * 2 + [ANY] + [VMEM] * 2,
        out_specs=[VMEM] * 5,
        out_shape=[array((count, D)), array((count, D))] + [array((1, D), F32)] * 3,
        scratch_shapes=[pltpu.VMEM((count, D), BF16), row_semaphores(1, count)],
        compiler_params=limit(12),
        cost_estimate=cost(2 * count * D * 5 * D, 30 * count * D + 18 * D * D),
    )(cot, df, far(x1), vectors, near(w))


def attend_back_kernel(
    first_head, group, do_ref, rd_far, o_far, pq_far, pk_far, v_far, s_far, q_far, k_far, fq, fk,
    dproj_ref, sums_ref, fmap_ref, state, gq, gk, rd_ref, o_ref, pq_ref, pk_ref, v_ref, q_ref, k_ref, s_ref, row_sems, s_sems,
):
    heads_here = state.shape[0]
    width = heads_here * HD
    base = first_head // 2
    steps = do_ref.shape[0] // CHUNK
    enter = Rows(
        [(source.at[:, pl.ds(first_head * HD, width)], target) for source, target in ((rd_far, rd_ref), (o_far, o_ref), (v_far, v_ref))]
        + [(source.at[:, pl.ds(2 * first_head * HD, 2 * width)], target) for source, target in ((pq_far, pq_ref), (pk_far, pk_ref))]
        + [(source.at[:, pl.ds(first_head * HD, width)], target) for source, target in ((q_far, q_ref), (k_far, k_ref))],
        row_sems,
    )
    enter_state = lambda step: pltpu.make_async_copy(
        s_far.at[step, pl.ds(first_head, heads_here)], s_ref.at[step], s_sems.at[step]
    )
    for step in reversed(range(steps)):
        enter.start(step)
        enter_state(step).start()
    for ref in (state, gq, gk, sums_ref):
        ref[...] = jnp.zeros_like(ref)
    ones = block_ones(4 * HD)
    halves = jnp.concatenate([ones[0:128, 0:128], ones[0:128, 0:128]], 0)
    row = lax.broadcasted_iota(jnp.int32, (CHUNK, CHUNK), 0)
    col = lax.broadcasted_iota(jnp.int32, (CHUNK, CHUNK), 1)
    causal = row >= col
    below = row <= col
    lane = lanes((CHUNK, 128))
    low = lane < HD

    def body(index, carry):
        step = steps - 1 - index
        rows = block_rows(step, CHUNK)
        enter.wait(step)
        enter_state(step).wait()
        for start in range(0, heads_here // 2, group):
            pairs = range(start, start + group)
            heads = range(2 * start, 2 * (start + group))
            pair_cols = {pair: slice(pair * 128, (pair + 1) * 128) for pair in pairs}
            head_cols = {head: slice(head * 128, (head + 1) * 128) for head in heads}
            do_cols = {pair: slice((base + pair) * 128, (base + pair + 1) * 128) for pair in pairs}
            pq = {head: pq_ref[rows, head_cols[head]] for head in heads}
            pk = {head: pk_ref[rows, head_cols[head]] for head in heads}
            scores = {head: nt(pk[head], pq[head]) for head in heads}
            numer = {p: (do_ref[rows, do_cols[p]].astype(F32) * rd_ref[rows, pair_cols[p]].astype(F32)).astype(BF16).astype(F32) for p in pairs}
            denom = {}
            for p in pairs:
                product = numer[p] * o_ref[rows, pair_cols[p]].astype(F32)
                coarse = product.astype(BF16)
                fine = (product - coarse.astype(F32)).astype(BF16)
                denom[p] = -nn(jnp.concatenate([coarse, fine], 1), halves)
            vx = {}
            for p in pairs:
                vx[2 * p], vx[2 * p + 1] = value_pair(v_ref[rows, pair_cols[p]])
            scores = {head: jnp.where(below, scores[head], 0.0).astype(BF16) for head in heads}
            dn = {}
            for p in pairs:
                for head, top, rest in ((2 * p, numer[p], swap_halves(denom[p])), (2 * p + 1, swap_halves(numer[p]), denom[p])):
                    rounded = rest.astype(BF16).astype(F32)
                    tail = jnp.where(lane == HD, rounded, jnp.where(lane == HD + 1, rest - rounded, 0.0))
                    dn[head] = jnp.where(low, top, tail).astype(BF16)
            later = {head: state[head].astype(BF16) for head in heads}
            ds = {head: nt(dn[head], vx[head]) for head in heads}
            dst = {head: nt(vx[head], dn[head]) for head in heads}
            far_q = {head: nt(dn[head], s_ref[step, head]) for head in heads}
            far_k = {head: nt(vx[head], later[head]) for head in heads}
            far_v = {head: nn(pk[head], later[head]) for head in heads}
            dv = {head: nn(scores[head], dn[head]) + far_v[head] for head in heads}
            more = {head: tn(pq[head], dn[head]) for head in heads}
            ds = {head: jnp.where(causal, ds[head], 0.0).astype(BF16) for head in heads}
            dst = {head: jnp.where(below, dst[head], 0.0).astype(BF16) for head in heads}
            dq = {head: nn(ds[head], pk[head]) + far_q[head] for head in heads}
            dk = {head: nn(dst[head], pq[head]) + far_k[head] for head in heads}
            for head in heads:
                state[head] += more[head]
            out = {}
            for p in pairs:
                out[2, p] = jnp.where(low, dv[2 * p], swap_halves(dv[2 * p + 1])).astype(BF16)
            grads, feats, inner = {}, {}, {}
            for p in pairs:
                both = slice(p * 256, (p + 1) * 256)
                for part, (grad, feat_ref) in enumerate(((dq, pq_ref), (dk, pk_ref))):
                    grads[part, p] = jnp.concatenate([grad[2 * p], grad[2 * p + 1]], 1)
                    feats[part, p] = feat_ref[rows, both].astype(F32)
                    inner[part, p] = nn((grads[part, p] * feats[part, p]).astype(BF16), ones)
            logits = {key: (feats[key] * (grads[key] - inner[key])).astype(BF16) for key in inner}
            for p in pairs:
                for part, (rows_ref, maps, total) in enumerate(((q_ref, fq, gq), (k_ref, fk, gk))):
                    out[part, p] = nt(logits[part, p], maps[base + p]).astype(BF16)
                    total[p] += tn(rows_ref[rows, pair_cols[p]], logits[part, p])
            for (part, p), value in out.items():
                cols = slice(part * width + p * 128, part * width + (p + 1) * 128)
                dproj_ref[rows, cols] = value
                sums_ref[:, cols] += column_sums(value.astype(F32))
        return carry

    lax.fori_loop(0, steps, body, 0)
    first = lanes((HD, 2 * HD)) < HD
    for head in range(heads_here):
        r, c = (head % 2) * HD, (head % 2) * 2 * HD
        bq = gq[head // 2, r : r + HD, c : c + 2 * HD]
        bk = gk[head // 2, r : r + HD, c : c + 2 * HD]
        fmap_ref[head * HD : (head + 1) * HD, :] = jnp.where(first, bq - swap_halves(bq), swap_halves(bk) - bk)


def attend_back(first, heads, do, rd, o, pq, pk, v, s, q, k, fq, fk, group=2):
    count = v.shape[0]
    width = heads * HD
    return pl.pallas_call(
        functools.partial(attend_back_kernel, first, group),
        name="attend_back",
        in_specs=[VMEM] + [ANY] * 8 + [VMEM] * 2,
        out_specs=[VMEM] * 3,
        out_shape=[array((count, 3 * width)), array((1, 3 * width), F32), array((width, 2 * HD), F32)],
        scratch_shapes=[
            pltpu.VMEM((heads, 128, 128), F32), pltpu.VMEM((heads // 2, 128, 256), F32), pltpu.VMEM((heads // 2, 128, 256), F32),
        ]
        + [pltpu.VMEM((count, size), BF16) for size in (width, width, 2 * width, 2 * width, width, width, width)]
        + [pltpu.VMEM((count // CHUNK, heads, 128, 128), BF16), row_semaphores(7, count), pltpu.SemaphoreType.DMA((count // CHUNK,))],
        compiler_params=limit(22),
        cost_estimate=cost(2 * count * heads * 128 * 128 * 14, 40 * count * width),
    )(do, *map(far, (rd, o, pq, pk, v, s, q, k)), fq, fk)


def slot_of(index):
    return 2 * index if index < 4 else 2 * index - 7


def outer_rows_kernel(first, me_ref, left_ref, right_ref, out_ref):
    rows = out_ref.shape[1]
    right = right_ref[...]
    for index in range(4):
        start = pl.multiple_of((me_ref[0] ^ slot_of(first + index)) * rows, 128)
        out_ref[index] = tn(left_ref[:, pl.ds(start, rows)], right).astype(BF16)


def outer_rows(me, first, left, right):
    count, wide = left.shape
    across = right.shape[1]
    return pl.pallas_call(
        functools.partial(outer_rows_kernel, first),
        name="outer_rows",
        in_specs=[SMEM, VMEM, VMEM],
        out_specs=VMEM,
        out_shape=array((4, wide // 8, across)),
        compiler_params=limit(10),
        cost_estimate=cost(0 if first else count * wide * across, 0),
    )(me, left, right)


def outer_cols_kernel(plan, away, me_ref, *refs):
    *ins, send_ref, keep_ref, turned = refs[: len(refs) - len(away) - 1]
    copies = {}
    for at, index in enumerate(away):
        held = refs[len(refs) - len(away) - 1 + at]
        copies[index] = pltpu.make_async_copy(ins[index], held, refs[-1].at[at])
        copies[index].start()
        ins[index] = held
    rows = send_ref.shape[1]
    at = 0

    def by_slot(value):
        for shard in range(8):
            slot = me_ref[0] ^ shard
            turned[(slot >> 1) + 4 * (slot & 1), :, : value.shape[1]] = value[shard * rows : (shard + 1) * rows]

    for left, right in plan:
        across = ins[right].shape[1]
        if left is None:
            by_slot(ins[right][...].astype(BF16))
            keep_ref[:, :, at : at + across] = turned[0:4, :, :across]
            send_ref[:, :, at : at + across] = turned[4:8, :, :across]
            at += across
            continue
        if left in copies:
            copies[left].wait()
        by_slot(ins[left][...].T)
        whole = turned[...].reshape(8 * rows, turned.shape[2])
        for start in range(0, across, TILE):
            value = nn(whole, ins[right][:, start : start + TILE]).astype(BF16)
            keep_ref[:, :, at : at + TILE] = value[: 4 * rows].reshape(4, rows, TILE)
            send_ref[:, :, at : at + TILE] = value[4 * rows :].reshape(4, rows, TILE)
            at += TILE


def outer_cols(me, arrays, plan, away=()):
    across = sum(arrays[right].shape[1] for _, right in plan)
    out = array((4, D // 8, across))
    return pl.pallas_call(
        functools.partial(outer_cols_kernel, plan, away),
        name="outer_cols",
        in_specs=[SMEM] + [ANY if index in away else VMEM for index in range(len(arrays))],
        out_specs=[VMEM, VMEM],
        out_shape=[out, out],
        scratch_shapes=[pltpu.VMEM((8, D // 8, arrays[0].shape[0]), BF16)]
        + [pltpu.VMEM(arrays[index].shape, BF16) for index in away] + [pltpu.SemaphoreType.DMA((max(1, len(away)),))],
        compiler_params=limit(11),
        cost_estimate=cost(0, 0),
    )(me, *[far(value) if index in away else value for index, value in enumerate(arrays)])


def input_back_kernel(source, groups, me_ref, tok_ref, da_ref, vec_ref, *refs):
    parts, refs = refs[: len(groups)], refs[len(groups) :]
    count = len(source.arrays)
    out_ref, gain1_ref, bias1_ref, w_ref, sems = refs[count:]
    copies = source.copies(me_ref[0], refs[:count], w_ref, sems)
    for copy in copies:
        copy.start()
    for ref in (gain1_ref, bias1_ref):
        ref[...] = jnp.zeros_like(ref)
    for copy in copies:
        copy.wait()

    def body(index, carry):
        rows = [block_rows(2 * index + half, ROWS) for half in range(2)]
        grads = []
        for at in rows:
            grad = None
            for (first, heads), part_ref in zip(groups, parts):
                width = heads * HD
                for part in range(3):
                    cols = slice(part * D + first * HD, part * D + (first + heads) * HD)
                    more = nt(part_ref[at, part * width : (part + 1) * width], w_ref[:, cols])
                    grad = more if grad is None else grad + more
            grads.append(grad)
        for at, grad in zip(rows, grads):
            unit, scale = normalized(tok_ref[at, :].astype(F32))
            value = da_ref[at, :].astype(F32) + norm_back(grad, vec_ref[4:5, :D], unit, scale)
            out_ref[at, :] = value.astype(BF16)
            gain1_ref[...] += column_sums(grad * unit)
        bias1_ref[...] += column_sums(grads[0]) + column_sums(grads[1])
        return carry

    lax.fori_loop(0, tok_ref.shape[0] // (2 * ROWS), body, 0)


def input_back(me, groups, parts, tokens, da, vectors, source):
    count = tokens.shape[0]
    return pl.pallas_call(
        functools.partial(input_back_kernel, source, groups),
        name="input_back",
        in_specs=[SMEM] + [VMEM] * (3 + len(parts)) + source.specs(),
        out_specs=[VMEM] * 3,
        out_shape=[array((count, D)), array((1, D), F32), array((1, D), F32)],
        scratch_shapes=[pltpu.VMEM(source.shape, BF16), source.semaphores()],
        compiler_params=limit(14),
        cost_estimate=cost(2 * count * D * 3 * D, 14 * count * D + 6 * D * D),
    )(me, tokens, da, vectors, *parts, *source.arrays)


def narrow_kernel(source, base, me_ref, g_far, x1_far, vec_ref, *refs):
    if source is None:
        w_ref, out_ref, g_ref, x1_ref, row_sems = refs
        copies = []
    else:
        count = len(source.arrays)
        out_ref, w_ref, g_ref, x1_ref, row_sems, sems = refs[count:]
        copies = source.copies(me_ref[0], refs[:count], w_ref, sems)
    steps = out_ref.shape[0] // ROWS
    rows_here = pl.ds(base, out_ref.shape[0])
    enter = Rows([(g_far.at[rows_here, :], g_ref), (x1_far.at[rows_here, :], x1_ref)], row_sems)
    for copy in copies:
        copy.start()
    for step in range(steps):
        enter.start(step)
    for copy in copies:
        copy.wait()

    def body(step, carry):
        enter.wait(step)
        rows = block_rows(step, ROWS)
        out_ref[rows, :] = (x1_ref[rows, :].astype(F32) + (nn(g_ref[rows, :], w_ref[...]) + vec_ref[3:4, :D])).astype(BF16)
        return carry

    lax.fori_loop(0, steps, body, 0)


def narrow(me, base, count, g, x1, vectors, source):
    first = isinstance(source, Source)
    return pl.pallas_call(
        functools.partial(narrow_kernel, source if first else None, base),
        name="narrow",
        in_specs=[SMEM, ANY, ANY, VMEM] + (source.specs() if first else [VMEM]),
        out_specs=[VMEM] * 2 if first else VMEM,
        out_shape=[array((count, D)), array(source.shape)] if first else array((count, D)),
        scratch_shapes=[pltpu.VMEM((count, FF), BF16), pltpu.VMEM((count, D), BF16), row_semaphores(2, count)]
        + ([source.semaphores()] if first else []),
        compiler_params=limit(10),
        cost_estimate=cost(2 * count * D * FF, 14 * count * D + 8 * D * D),
    )(me, far(g), far(x1), vectors, *(source.arrays if first else [source]))


def fold_kernel(keep_ref, arrived_ref, *outs):
    for index, out in enumerate(outs):
        out[...] = keep_ref[index] + arrived_ref[index]


def fold(keep, arrived):
    slots, rows, across = keep.shape
    return pl.pallas_call(
        fold_kernel,
        name="fold",
        in_specs=[VMEM] * 2,
        out_specs=[VMEM] * slots,
        out_shape=[array((rows, across))] * slots,
        compiler_params=limit(8),
        cost_estimate=cost(keep.size, 6 * keep.size),
    )(keep, arrived)


def total_kernel(*refs):
    *values, out = refs
    result = values[0][...].astype(F32)
    for value in values[1:]:
        result = result + value[...].astype(F32)
    out[...] = result.astype(out.dtype)


def total(*values):
    return pl.pallas_call(
        total_kernel,
        name="total",
        in_specs=[VMEM] * len(values),
        out_specs=VMEM,
        out_shape=array(values[0].shape),
        compiler_params=limit(8),
        cost_estimate=cost(4 * values[0].size, 10 * values[0].size),
    )(*values)


def cross_kernel(keep_ref, arrived_ref, send_x, send_y, top, bottom):
    half = top.shape[1]
    for outs, rows in (((top, send_x, top, send_x), slice(0, half)), ((bottom, bottom, send_y, send_y), slice(half, 2 * half))):
        for slot, out in enumerate(outs):
            out[slot // 2 if outs[0] is outs[2] else slot % 2] = keep_ref[slot, rows, :] + arrived_ref[slot, rows, :]


def cross_over(keep, arrived):
    _, rows, across = keep.shape
    return pl.pallas_call(
        cross_kernel,
        name="cross_over",
        in_specs=[VMEM] * 2,
        out_specs=[VMEM] * 4,
        out_shape=[array((2, rows // 2, across))] * 4,
        compiler_params=limit(8),
        cost_estimate=cost(keep.size, 6 * keep.size),
    )(keep, arrived)


def turn_kernel(top, bottom, over_x, over_y, send_y, send_x, mine_top, mine_bottom):
    mine_top[...] = top[0] + over_x[0]
    send_y[...] = top[1] + over_x[1]
    mine_bottom[...] = bottom[0] + over_y[0]
    send_x[...] = bottom[1] + over_y[1]


def turn_over(top, bottom, over_x, over_y):
    _, half, across = top.shape
    return pl.pallas_call(
        turn_kernel,
        name="turn_over",
        in_specs=[VMEM] * 4,
        out_specs=[VMEM] * 4,
        out_shape=[array((half, across))] * 4,
        compiler_params=limit(8),
        cost_estimate=cost(4 * half * across, 24 * half * across),
    )(top, bottom, over_x, over_y)


def halve_kernel(side_ref, top, last_y, bottom, last_x, own_ref, other_ref):
    for side, one, two in ((0, top, last_y), (1, bottom, last_x)):
        value = one[...] + two[...]

        @pl.when(side_ref[0] == side)
        def _():
            own_ref[...] = value

        @pl.when(side_ref[0] != side)
        def _():
            other_ref[...] = value


def halve(side, top, last_y, bottom, last_x):
    return pl.pallas_call(
        halve_kernel,
        name="halve",
        in_specs=[SMEM] + [VMEM] * 4,
        out_specs=[VMEM] * 2,
        out_shape=[array(top.shape)] * 2,
        compiler_params=limit(8),
        cost_estimate=cost(2 * top.size, 12 * top.size),
    )(side, top, last_y, bottom, last_x)


def stack_kernel(top, last_y, bottom, last_x, out_ref):
    half = top.shape[0]
    out_ref[:half, :] = top[...] + last_y[...]
    out_ref[half:, :] = bottom[...] + last_x[...]


def stack(top, last_y, bottom, last_x):
    half, across = top.shape
    return pl.pallas_call(
        stack_kernel,
        name="stack",
        in_specs=[VMEM] * 4,
        out_specs=VMEM,
        out_shape=array((2 * half, across)),
        compiler_params=limit(8),
        cost_estimate=cost(2 * top.size, 12 * top.size),
    )(top, last_y, bottom, last_x)


def join_kernel(side_ref, own_ref, other_ref, out_ref):
    half = own_ref.shape[0]
    out_ref[block_rows(side_ref[0], half), :] = own_ref[...].astype(F32)
    out_ref[block_rows(1 - side_ref[0], half), :] = other_ref[...].astype(F32)


def join(side, own, other):
    half, across = own.shape
    return pl.pallas_call(
        join_kernel,
        name="join",
        in_specs=[SMEM] + [VMEM] * 2,
        out_specs=VMEM,
        out_shape=array((2 * half, across), F32),
        compiler_params=limit(8),
        cost_estimate=cost(half * across, 12 * half * across),
    )(side, own, other)


def write_lines(lines, outs):
    at = 0
    for out in outs:
        size = out.shape[0]
        for start in range(0, size, 128):
            count = min(128, size - start)
            out[pl.ds(start, count)] = lines[at : at + 1, :count].reshape(count)
            at += 1


def publish_kernel(groups, side_ref, own_ref, other_ref, one_ref, two_ref, qkvw_ref, outw_ref, fmap_ref, *outs):
    half = own_ref.shape[0]
    for side, ref in ((side_ref[0], own_ref), (1 - side_ref[0], other_ref)):
        rows = block_rows(side, half)
        outw_ref[rows, :] = ref[:, :D].astype(F32)
        first, heads = groups[0]
        width = heads * HD
        for part in range(3):
            value = ref[:, D + part * width : D + (part + 1) * width]
            qkvw_ref[rows, part * D + first * HD : part * D + first * HD + width] = value.astype(F32)
    last = one_ref[...].astype(F32) + two_ref[...].astype(F32)
    first, heads = groups[1]
    width = heads * HD
    for part in range(3):
        qkvw_ref[:, part * D + first * HD : part * D + first * HD + width] = last[:, part * width : (part + 1) * width]
    fmap_ref[...] = last[:, 3 * width : 3 * width + 2 * HD]
    write_lines(last[:, 3 * width + 2 * HD :], outs)


def publish(groups, side, own, other, one, two, sizes):
    rows = one.shape[0]
    return pl.pallas_call(
        functools.partial(publish_kernel, groups),
        name="publish",
        in_specs=[SMEM] + [VMEM] * 4,
        out_specs=[VMEM] * (3 + len(sizes)),
        out_shape=[array((rows, 3 * D), F32), array((rows, D), F32), array((rows, 2 * HD), F32)] + [array((size,), F32) for size in sizes],
        compiler_params=limit(8),
        cost_estimate=cost(rows * 3 * D * 4, rows * 3 * D * 12),
    )(side, own, other, one, two)


def line_count(sizes):
    return sum(-(-size // 128) for size in sizes)


def to_lines(vector, start, size):
    lines = []
    for at in range(0, size, 128):
        count = min(128, size - at)
        line = vector[:, start + at : start + at + count]
        if count < 128:
            line = jnp.concatenate([line, jnp.zeros((1, 128 - count), F32)], 1)
        lines.append(line)
    return lines


def pack_kernel(*refs):
    *vectors, fm_ref, w_ref, out_ref = refs
    width = w_ref.shape[1]
    out_ref[:, :width] = w_ref[...]
    out_ref[:, width : width + 128] = fm_ref[...]
    lines = []
    for vector in vectors:
        size = vector.shape[0]
        lines += to_lines(vector[...].astype(F32).reshape(1, size), 0, size)
    lines += [jnp.zeros((1, 128), F32)] * (w_ref.shape[0] - len(lines))
    out_ref[:, width + 128 :] = jnp.concatenate(lines, 0).astype(BF16)


def pack(w, fm, vectors):
    rows, width = w.shape
    return pl.pallas_call(
        pack_kernel,
        name="pack",
        in_specs=[VMEM] * (len(vectors) + 2),
        out_specs=VMEM,
        out_shape=array((rows, width + 256)),
        compiler_params=limit(56),
    )(*vectors, fm, w)


def small_grads_kernel(shards, *refs):
    *vectors, out_ref = refs
    rows = out_ref.shape[0] // shards
    for shard in range(shards):
        lines = []
        for vector in vectors:
            size = vector.shape[1] // shards
            lines += to_lines(vector[...], shard * size, size)
        lines += [jnp.zeros((1, 128), F32)] * (rows - len(lines))
        out_ref[shard * rows : (shard + 1) * rows, :] = jnp.concatenate(lines, 0)


def small_grads(shards, vectors):
    return pl.pallas_call(
        functools.partial(small_grads_kernel, shards),
        name="small_grads",
        in_specs=[VMEM] * len(vectors),
        out_specs=VMEM,
        out_shape=array((D, 128), F32),
        compiler_params=limit(8),
    )(*vectors)


def small_owned_kernel(lines_ref, *outs):
    write_lines(lines_ref[...], outs)


def small_owned(lines, sizes):
    return pl.pallas_call(
        small_owned_kernel,
        name="small_owned",
        in_specs=[VMEM],
        out_specs=[VMEM] * len(sizes),
        out_shape=[array((size,), F32) for size in sizes],
        compiler_params=limit(8),
    )(lines)


GROUPS = ((0, 8), (8, 4))


def after(value, *others):
    return lax.optimization_barrier((value, *others))[0]


def exchange(value, axis, mask):
    return lax.ppermute(value, axis, [(i, i ^ mask) for i in range(lax.axis_size(axis))])


class Gather:
    def __init__(self, shard):
        self.shard, self.rows = shard, shard.shape[0]
        self.hand = by_hand(self.rows)

    def start(self, *others):
        if not self.hand:
            self.full = lax.all_gather(self.shard, "fsdp", axis=0, tiled=True)
            return ()
        shard = after(self.shard, *others) if others else self.shard
        self.over_x, self.over_y = exchange(shard, "fsdp", 2), exchange(shard, "fsdp", 4)
        self.sibling = exchange(shard, "fsdp", 1)
        return self.over_x, self.over_y

    def relay(self, *others):
        if not self.hand:
            return ()
        half = self.rows // 2
        over_x, over_y, self.sibling = lax.optimization_barrier((self.over_x, self.over_y, self.sibling, *others))[:3]
        self.pieces = over_y[:half], over_x[half:]
        self.upper, self.lower = exchange(self.pieces[0], "fsdp", 2), exchange(self.pieces[1], "fsdp", 4)
        self.shared = [((3, 0), exchange(over_x, "fsdp", 1)), ((5, 0), exchange(over_y, "fsdp", 1))]
        return self.pieces

    def settled(self):
        return [value for _, value in self.shared] if self.hand else []

    def finish(self, *others):
        if not self.hand:
            return Source([(0, 0)], [self.full], self.rows, self.full.shape[0])
        half = self.rows // 2
        upper, lower = self.upper, self.lower
        if others:
            upper, lower = lax.optimization_barrier((upper, lower, *others))[:2]
        held = [((0, 0), self.shard), ((2, 0), self.over_x), ((4, 0), self.over_y), ((1, 0), self.sibling)] + self.shared
        held += [((6, 0), upper), ((6, half), lower)]
        held += [((7, 0), exchange(upper, "fsdp", 1)), ((7, half), exchange(lower, "fsdp", 1))]
        return Source([place for place, _ in held], [part for _, part in held], self.rows, 8 * self.rows)


def by_hand(rows):
    return lax.axis_size("fsdp") == 8 and lax.axis_size("dp") == 4 and rows % 32 == 0


class Scatter:
    def __init__(self, pair):
        send, self.keep = pair
        self.arrived = exchange(send, "fsdp", 1)

    def cross(self, *others):
        send_x, send_y, self.top, self.bottom = cross_over(self.keep, after(self.arrived, *others))
        self.over_x, self.over_y = exchange(send_x, "fsdp", 2), exchange(send_y, "fsdp", 4)
        return send_x, send_y

    def turn(self, *others):
        over_x, over_y = lax.optimization_barrier((self.over_x, self.over_y, *others))[:2]
        send_y, send_x, self.top, self.bottom = turn_over(self.top, self.bottom, over_x, over_y)
        self.last_y, self.last_x = exchange(send_y, "fsdp", 4), exchange(send_x, "fsdp", 2)
        return send_y, send_x

    def finish(self, *others):
        last_y, last_x = lax.optimization_barrier((self.last_y, self.last_x, *others))[:2]
        return self.top, last_y, self.bottom, last_x

    def straight(self, *others):
        self.mine, *away = fold(self.keep, after(self.arrived, *others))
        self.moved = [exchange(value, "fsdp", mask) for value, mask in zip(away, (2, 4, 6))]
        return away

    def arrive(self, *others):
        return total(self.mine, *lax.optimization_barrier((*self.moved, *others))[:3])


class Planes:
    def __init__(self, side, values):
        self.own, self.other = halve(side, *values)
        self.moved = exchange(self.other, "dp", 1)

    def mirror(self, *others):
        self.own = self.own + after(self.moved, *others)
        self.moved = exchange(self.own, "dp", 3)
        return self.own

    def back(self, *others):
        self.own = self.own + after(self.moved, *others)
        self.moved = exchange(self.own, "dp", 1)
        return self.own

    def finish(self, *others):
        return self.own, after(self.moved, *others)


def outer(left, right):
    return tn(left, right).astype(BF16)


def on_device(
    tokens, lengths, qkv_weight, qkv_bias, out_weight, out_bias, fc_weight, fc_bias, proj_weight, proj_bias,
    norm1_gain, norm1_bias, norm2_gain, norm2_bias, feature_map, cotangent,
):
    shards = lax.axis_size("fsdp")
    me = lax.axis_index("fsdp").astype(jnp.int32).reshape(1)
    plane = lax.axis_index("dp").astype(jnp.int32).reshape(1)
    side = (plane ^ (plane >> 1)) & 1
    qkv_weight, me, side = lax.optimization_barrier((qkv_weight, me, side))
    small = [qkv_bias, out_bias, fc_bias, proj_bias, norm1_gain, norm1_bias, norm2_gain, norm2_bias]
    first = Gather(pack(qkv_weight, feature_map, small))
    second = Gather(jnp.concatenate([fc_weight, out_weight], 1))
    third = Gather(proj_weight)
    first.start()
    second.start(*first.relay())
    first_source = first.finish()
    v, pq, pk, vectors, fq, fk, h1, q, k, v_far, pq_far, pk_far = project(
        me, lengths, tokens, first_source, [value.shape[0] for value in small]
    )
    second.relay(v)
    o, o_far, rd, s = attend(lengths, pq, pk, v)
    parts = second.finish(o)
    third.start(o)
    h2, g, slope, w_fc, g_far, x1 = widen(me, o, tokens, vectors, parts)
    g = after(g, *third.relay(g))
    hand = by_hand(qkv_weight.shape[0])
    summed = lambda share: lax.psum(share.astype(BF16), "dp").astype(F32)
    over = lambda value: lax.psum_scatter(value, "fsdp", scatter_dimension=0, tiled=True)
    if hand:
        send = after(outer_rows(me, 4, g, cotangent), *third.settled())
        keep = outer_rows(me, 0, after(g, send), cotangent)
        proj_scatter = Scatter((send, keep))
        third_source = third.finish(keep)
        slope = after(slope, *proj_scatter.cross(keep))
    else:
        third_source = third.finish()
    df, projb, fcb = slope_back(me, cotangent, slope, third_source)
    if hand:
        pair = outer_cols(me, [h2, df], [(0, 1)])
        fc_scatter = Scatter(pair)
        df = after(df, *proj_scatter.turn(pair[0]))
    da, do, gain2, bias2, outb = middle_back(cotangent, df, x1, vectors, w_fc)
    if hand:
        proj_planes = Planes(side, proj_scatter.finish(do))
        do = after(do, proj_planes.other, *fc_scatter.cross(do))
    parts, sums, maps = [], [], []
    for index, (start, heads) in enumerate(GROUPS):
        dproj, sum_grad, fmap_grad = attend_back(start, heads, do, rd, o_far, pq_far, pk_far, v_far, s, q, k, fq, fk)
        parts.append(dproj)
        sums.append(sum_grad)
        maps.append(fmap_grad)
        if hand and index == 0:
            left = after(h1, proj_planes.mirror(dproj), *fc_scatter.turn(dproj))
            pair = outer_cols(me, [o_far, da, left, dproj], [(0, 1), (2, 3)], (0, 2))
            qkv_scatter = Scatter(pair)
            fc_planes = Planes(side, fc_scatter.finish(pair[0]))
            do = after(do, fc_planes.other)
    if hand:
        tokens = after(tokens, proj_planes.back(dproj), *qkv_scatter.cross(dproj), fc_planes.mirror(dproj))
    input_grad, gain1, bias1 = input_back(me, GROUPS, parts, tokens, da, vectors, first_source)
    spread = lambda values: jnp.concatenate([
        value[:, part * heads * HD : (part + 1) * heads * HD] for part in range(3) for (_, heads), value in zip(GROUPS, values)
    ], 1)
    ordered = spread(sums)
    small = [ordered[:, : 2 * D], ordered[:, 2 * D :], outb, fcb, projb, gain1, bias1, gain2, bias2]
    table = small_grads(shards, small)
    sizes = [value.shape[1] // shards for value in small]
    if hand:
        left = after(h1, *qkv_scatter.turn(table), fc_planes.back(table))
        pair = outer_cols(me, [left, dproj, jnp.concatenate(maps, 0), table], [(0, 1), (None, 2), (None, 3)], (0,))
        last_scatter = Scatter(pair)
        projw_grad = join(side, *proj_planes.finish(pair[0]))
        x1 = after(x1, pair[0], projw_grad)
    if hand:
        qkv_planes = Planes(side, qkv_scatter.finish(pair[0]))
        x1 = after(x1, qkv_planes.other)
    piece, w_proj = narrow(me, 0, ROWS, g_far, x1, vectors, third_source)
    pieces = [piece]
    for base in range(ROWS, tokens.shape[0], ROWS):
        if hand and base == ROWS:
            x1 = after(x1, *last_scatter.straight(piece))
        if hand and base == 2 * ROWS:
            fcw_grad = join(side, *fc_planes.finish(pieces[-1]))
            x1 = after(x1, fcw_grad, qkv_planes.mirror(pieces[-1]))
        if hand and base == 3 * ROWS:
            share = last_scatter.arrive(pieces[-1])
            x1 = after(x1, share)
        pieces.append(narrow(me, base, ROWS, g_far, x1, vectors, w_proj))
    block_out = jnp.concatenate(pieces, 0)
    if hand:
        qkv_planes.back(pieces[-1])
        share = share + after(exchange(share, "dp", 1), pieces[-1])
        qkvw_grad, outw_grad, fmap_grad, *vectors = publish(
            GROUPS, side, *qkv_planes.finish(), share, exchange(share, "dp", 3), sizes
        )
    else:
        vectors = small_owned(lax.psum(over(table), "dp"), sizes)
    qkb, vb, outb, fcb, projb, gain1, bias1, gain2, bias2 = vectors
    if not hand:
        projw_grad = summed(over(outer(g_far, cotangent)))
        fcw_grad, outw_grad = summed(over(outer(h2, df))), summed(over(outer(o_far, da)))
        qkvw_grad, fmap_grad = summed(over(outer(h1, spread(parts)))), summed(over(jnp.concatenate(maps, 0)))
    return (
        block_out, input_grad, qkvw_grad, qkb, vb, outw_grad, outb, fcw_grad, fcb,
        projw_grad, projb, gain1, bias1, gain2, bias2, fmap_grad,
    )


def solution(mesh):
    rows = P(("dp", "fsdp"), None)
    wide = P("fsdp", None)
    flat = P("fsdp")
    in_specs = (
        rows, P(("dp", "fsdp")), wide, flat, wide, flat, wide, flat, wide, flat, flat, flat, flat, flat, wide, rows,
    )
    out_specs = (rows, rows, wide, flat, flat, wide, flat, wide, flat, wide, flat, flat, flat, flat, flat, wide)
    return jax.shard_map(on_device, mesh=mesh, in_specs=in_specs, out_specs=out_specs, check_vma=False)
```

```python
import functools

import jax
import jax.numpy as jnp
from jax import lax
from jax.experimental import pallas as pl
from jax.experimental.pallas import tpu as pltpu
from jax.sharding import PartitionSpec as P

D = 768
HEADS = 12
HD = 64
PAIRS = HEADS // 2
FF = 3072
ROWS = 256
CHUNK = 256
TILE = 256
EPSILON = 1e-05
SAFE = 60.0
SCALE = 20
F32 = jnp.float32
BF16 = jnp.bfloat16
ROOT = 0.7978845608028654
CUBE = 0.044715
VMEM = pl.BlockSpec(memory_space=pltpu.VMEM)
SMEM = pl.BlockSpec(memory_space=pltpu.SMEM)
ANY = pl.BlockSpec(memory_space=pl.ANY)
VECTORS = (8, FF)
MAPS = (PAIRS, 128, 256)


def nn(left, right):
    return lax.dot_general(left, right, (((1,), (0,)), ((), ())), preferred_element_type=F32)


def nt(left, right):
    return lax.dot_general(left, right, (((1,), (1,)), ((), ())), preferred_element_type=F32)


def tn(left, right):
    return lax.dot_general(left, right, (((0,), (0,)), ((), ())), preferred_element_type=F32)


def limit(mib):
    return pltpu.CompilerParams(vmem_limit_bytes=mib * 1024 * 1024)


def cost(flops, size, trans=0):
    return pl.CostEstimate(flops=int(SCALE * flops), bytes_accessed=int(size), transcendentals=int(trans))


def array(shape, kind=BF16):
    return jax.ShapeDtypeStruct(shape, kind)


def near(value):
    return pltpu.with_memory_space_constraint(value, pltpu.VMEM)


def far(value):
    return pltpu.with_memory_space_constraint(value, pltpu.HBM)


def lanes(shape):
    return lax.broadcasted_iota(jnp.int32, shape, 1)


def block_rows(index, count):
    return pl.ds(pl.multiple_of(index * count, count), count)


def normalized(values):
    middle = jnp.mean(values, -1, keepdims=True)
    centred = values - middle
    spread = jnp.mean(centred * centred, -1, keepdims=True)
    scale = lax.rsqrt(spread + EPSILON)
    return centred * scale, scale


def norm_back(grad, gain, unit, scale):
    scaled = grad * gain
    first = jnp.mean(scaled, -1, keepdims=True)
    second = jnp.mean(scaled * unit, -1, keepdims=True)
    return (scaled - first - unit * second) * scale


def swap_halves(values):
    return pltpu.roll(values, 64, 1)


def block_ones(size):
    row = lax.broadcasted_iota(jnp.int32, (size, size), 0) // HD
    col = lax.broadcasted_iota(jnp.int32, (size, size), 1) // HD
    return jnp.where(row == col, 1.0, 0.0).astype(BF16)


def build_maps(map_ref, fq, fk):
    fq[...] = jnp.zeros_like(fq)
    fk[...] = jnp.zeros_like(fk)
    low = lanes((HD, 2 * HD)) < HD
    for head in range(HEADS):
        block = map_ref[head * HD : (head + 1) * HD, :].astype(F32)
        turned = swap_halves(block)
        row, col = (head % 2) * HD, (head % 2) * 2 * HD
        fq[head // 2, row : row + HD, col : col + 2 * HD] = jnp.where(low, block, -turned).astype(BF16)
        fk[head // 2, row : row + HD, col : col + 2 * HD] = jnp.where(low, turned, -block).astype(BF16)


class Source:
    def __init__(self, places, arrays, rows, total):
        self.places, self.arrays, self.rows = places, list(arrays), rows
        self.shape = (total, arrays[0].shape[1])

    def specs(self):
        return [ANY] * len(self.arrays)

    def semaphores(self):
        return pltpu.SemaphoreType.DMA((len(self.arrays),))

    def copies(self, me, refs, held, sems, first=0, count=None):
        made = []
        count = self.shape[1] - first if count is None else count
        cols = pl.ds(first, count)
        for at, ((slot, offset), ref) in enumerate(zip(self.places, refs)):
            start = 0 if len(self.places) == 1 else pl.multiple_of((me ^ slot) * self.rows + offset, 16)
            made.append(pltpu.make_async_copy(ref.at[:, cols], held.at[pl.ds(start, ref.shape[0]), cols], sems.at[at]))
        return made


class Rows:
    def __init__(self, pairs, sems):
        self.pairs, self.sems = pairs, sems

    def copies(self, step):
        rows = block_rows(step, ROWS)
        return [
            pltpu.make_async_copy(source.at[rows, :], target.at[rows, :], self.sems.at[at, step])
            for at, (source, target) in enumerate(self.pairs)
        ]

    def start(self, step):
        for copy in self.copies(step):
            copy.start()

    def wait(self, step):
        for copy in self.copies(step):
            copy.wait()


def row_semaphores(pairs, count):
    return pltpu.SemaphoreType.DMA((pairs, count // ROWS))


def read_vectors(table, rows, sizes, out):
    for shard in range(table.shape[0] // rows):
        line = shard * rows
        for row, size in enumerate(sizes):
            for at in range(0, size, 128):
                count = min(128, size - at)
                out[row : row + 1, shard * size + at : shard * size + at + count] = table[line : line + 1, :count].astype(F32)
                line += 1


def project_kernel(source, sizes, me_ref, len_ref, tok_ref, *refs):
    count = len(source.arrays)
    v_ref, pq_ref, pk_ref, vec_ref, fq, fk, *far_refs, w_ref, h_ref, q_ref, k_ref, side_sems, sems, row_sems = refs[count:]
    leave = Rows(list(zip((h_ref, q_ref, k_ref, v_ref, pq_ref, pk_ref), far_refs)), row_sems)
    steps = tok_ref.shape[0] // ROWS
    side = source.copies(me_ref[0], refs[:count], w_ref, side_sems, 3 * D)
    main = source.copies(me_ref[0], refs[:count], w_ref, sems, 0, 3 * D)
    for copy in side + main:
        copy.start()
    vec_ref[...] = jnp.zeros_like(vec_ref)
    ones = block_ones(4 * HD)
    for copy in side:
        copy.wait()
    read_vectors(w_ref.at[:, 3 * D + 128 :], source.rows, sizes, vec_ref)
    build_maps(w_ref.at[:, 3 * D : 3 * D + 128], fq, fk)

    def norm(step, carry):
        rows = block_rows(step, ROWS)
        unit, _ = normalized(tok_ref[rows, :].astype(F32))
        h_ref[rows, :] = (unit * vec_ref[4:5, :D] + vec_ref[5:6, :D]).astype(BF16)
        return carry

    lax.fori_loop(0, steps, norm, 0)
    for copy in main:
        copy.wait()

    def body(step, carry):
        rows = block_rows(step, ROWS)
        h = h_ref[rows, :]
        wide = [(nn(h, w_ref[:, p * D : (p + 1) * D]) + vec_ref[0:1, p * D : (p + 1) * D]).astype(BF16) for p in range(3)]
        for out, value in zip((q_ref, k_ref, v_ref), wide):
            out[rows, :] = value
        place = step * ROWS + lax.broadcasted_iota(jnp.int32, (ROWS, 1), 0)
        live = (place < len_ref[0]).astype(F32)
        largest = jnp.zeros((ROWS, 256), F32)
        for part, (maps, out) in enumerate(((fq, pq_ref), (fk, pk_ref))):
            u = [nn(wide[part][:, p * 128 : (p + 1) * 128], maps[p]) for p in range(PAIRS)]
            e = [jnp.exp(value) for value in u]
            total = [nn(value.astype(BF16), ones) for value in e]
            for p in range(PAIRS):
                largest = jnp.maximum(largest, u[p])
                share = e[p] * pl.reciprocal(total[p], approx=True)
                if part == 1:
                    share = share * live
                out[rows, p * 256 : (p + 1) * 256] = share.astype(BF16)

        @pl.when(jnp.logical_not(jnp.max(largest) <= SAFE))
        def _():
            for part, (maps, rows_ref, out) in enumerate(((fq, q_ref, pq_ref), (fk, k_ref, pk_ref))):
                for p in range(PAIRS):
                    u = nn(rows_ref[rows, p * 128 : (p + 1) * 128], maps[p])
                    for group in range(4):
                        piece = u[:, group * HD : (group + 1) * HD]
                        e = jnp.exp(piece - jnp.max(piece, -1, keepdims=True))
                        share = e / jnp.sum(e, -1, keepdims=True)
                        if part == 1:
                            share = share * live
                        out[rows, p * 256 + group * HD : p * 256 + (group + 1) * HD] = share.astype(BF16)

        leave.start(step)
        return carry

    lax.fori_loop(0, steps, body, 0)
    for step in range(steps):
        leave.wait(step)


def project(me, lengths, tokens, source, sizes):
    count = tokens.shape[0]
    return pl.pallas_call(
        functools.partial(project_kernel, source, sizes),
        name="project",
        in_specs=[SMEM, SMEM, VMEM] + source.specs(),
        out_specs=[VMEM] * 6 + [ANY] * 6,
        out_shape=[array((count, D)), array((count, 2 * D)), array((count, 2 * D)), array(VECTORS, F32), array(MAPS), array(MAPS)]
        + [pltpu.HBM((count, D), BF16)] * 4 + [pltpu.HBM((count, 2 * D), BF16)] * 2,
        scratch_shapes=[pltpu.VMEM(source.shape, BF16)] + [pltpu.VMEM((count, D), BF16)] * 3
        + [source.semaphores(), source.semaphores(), row_semaphores(6, count)],
        compiler_params=limit(17),
        cost_estimate=cost(0, 0),
    )(me, lengths, tokens, *source.arrays)


def value_pair(v_pair):
    low = lanes(v_pair.shape) < HD
    wide = v_pair.astype(F32)
    return (
        jnp.where(low, wide, 1.0).astype(BF16),
        jnp.where(low, swap_halves(wide), 1.0).astype(BF16),
    )


def attend_kernel(group, len_ref, pq_ref, pk_ref, v_ref, o_ref, o_far, rd_far, s_far, rd_ref, s_ref, state, row_sems, s_sems):
    leave = Rows([(o_ref, o_far), (rd_ref, rd_far)], row_sems)
    leave_state = lambda step: pltpu.make_async_copy(s_ref.at[step], s_far.at[step], s_sems.at[step])
    steps = v_ref.shape[0] // CHUNK
    state[...] = jnp.zeros_like(state)
    row = lax.broadcasted_iota(jnp.int32, (CHUNK, CHUNK), 0)
    col = lax.broadcasted_iota(jnp.int32, (CHUNK, CHUNK), 1)
    causal = row >= col
    low = lanes((CHUNK, 128)) < HD
    place = lax.broadcasted_iota(jnp.int32, (CHUNK, 128), 0)

    def body(step, carry):
        rows = block_rows(step, CHUNK)
        live = (step * CHUNK + place < len_ref[0]).astype(F32)
        for first in range(0, PAIRS, group):
            pairs = range(first, first + group)
            heads = range(2 * first, 2 * (first + group))
            cols = [slice(head * 128, (head + 1) * 128) for head in range(HEADS)]
            pq = {head: pq_ref[rows, cols[head]] for head in heads}
            pk = {head: pk_ref[rows, cols[head]] for head in heads}
            vx = {}
            for pair in pairs:
                vx[2 * pair], vx[2 * pair + 1] = value_pair(v_ref[rows, cols[pair]])
            scores = {head: nt(pq[head], pk[head]) for head in heads}
            prior = {head: state[head].astype(BF16) for head in heads}
            more = {head: tn(pk[head], vx[head]) for head in heads}
            far = {head: nn(pq[head], prior[head]) for head in heads}
            scores = {head: jnp.where(causal, scores[head], 0.0).astype(BF16) for head in heads}
            sums = {head: nn(scores[head], vx[head]) + far[head] for head in heads}
            for head in heads:
                s_ref[step, head] = prior[head]
                state[head] += more[head]
            for pair in pairs:
                one, two = sums[2 * pair], sums[2 * pair + 1]
                numer = jnp.where(low, one, swap_halves(two))
                denom = jnp.where(low, swap_halves(one), two)
                rd = live / denom
                rd_ref[rows, cols[pair]] = rd.astype(BF16)
                o_ref[rows, cols[pair]] = (numer * rd).astype(BF16)
        leave.start(step)
        leave_state(step).start()
        return carry

    lax.fori_loop(0, steps, body, 0)
    for step in range(steps):
        leave.wait(step)
        leave_state(step).wait()


def attend(lengths, pq, pk, v, group=3):
    count = v.shape[0]
    steps = count // CHUNK
    return pl.pallas_call(
        functools.partial(attend_kernel, group),
        name="attend",
        in_specs=[SMEM, VMEM, VMEM, VMEM],
        out_specs=[VMEM] + [ANY] * 3,
        out_shape=[array((count, D))] + [pltpu.HBM((count, D), BF16)] * 2 + [pltpu.HBM((steps, HEADS, 128, 128), BF16)],
        scratch_shapes=[
            pltpu.VMEM((count, D), BF16), pltpu.VMEM((steps, HEADS, 128, 128), BF16), pltpu.VMEM((HEADS, 128, 128), F32),
            row_semaphores(2, count), pltpu.SemaphoreType.DMA((steps,)),
        ],
        compiler_params=limit(10),
        cost_estimate=cost(2 * count * HEADS * 128 * 512, 20 * count * D),
    )(lengths, pq, pk, v)


def gelu_pair(f):
    low = f.astype(BF16)
    square = low * low
    bend = jnp.tanh(low * (BF16(ROOT) + BF16(ROOT * CUBE) * square))
    share = BF16(0.5) + BF16(0.5) * bend
    value = low * share
    slope = share + value * (BF16(1.0) - share) * (BF16(2 * ROOT) + BF16(6 * ROOT * CUBE) * square)
    return value, slope


def widen_kernel(source, me_ref, o_ref, tok_ref, vec_ref, *refs):
    count = len(source.arrays)
    h2_ref, g_ref, slope_ref, w_far, g_far, x1_far, w_ref, x1_ref, side_sems, sems, g_sems, x1_sems, w_sem = refs[count:]
    leave, leave_x1 = Rows([(g_ref, g_far)], g_sems), Rows([(x1_ref, x1_far)], x1_sems)
    steps = tok_ref.shape[0] // ROWS
    side = source.copies(me_ref[0], refs[:count], w_ref, side_sems, FF)
    main = source.copies(me_ref[0], refs[:count], w_ref, sems, 0, FF)
    for copy in side + main:
        copy.start()
    for copy in side:
        copy.wait()

    def middle(index, carry):
        rows = block_rows(index, 2 * ROWS)
        x1 = tok_ref[rows, :].astype(F32) + (nn(o_ref[rows, :], w_ref[:, FF:]) + vec_ref[1:2, :D])
        x1_ref[rows, :] = x1.astype(BF16)
        unit, _ = normalized(x1)
        h2_ref[rows, :] = (unit * vec_ref[6:7, :D] + vec_ref[7:8, :D]).astype(BF16)
        leave_x1.start(2 * index)
        leave_x1.start(2 * index + 1)
        return carry

    lax.fori_loop(0, steps // 2, middle, 0)
    for copy in main:
        copy.wait()
    leave_w = pltpu.make_async_copy(w_ref, w_far, w_sem)
    leave_w.start()

    def body(index, carry):
        rows = block_rows(index, 2 * ROWS)
        h2 = h2_ref[rows, :]
        for part in range(4):
            cols = slice(part * D, (part + 1) * D)
            g_ref[rows, cols], slope_ref[rows, cols] = gelu_pair(nn(h2, w_ref[:, cols]) + vec_ref[2:3, cols])
        leave.start(2 * index)
        leave.start(2 * index + 1)
        return carry

    lax.fori_loop(0, steps // 2, body, 0)
    for step in range(steps):
        leave_x1.wait(step)
        leave.wait(step)
    leave_w.wait()


def widen(me, o, tokens, vectors, source):
    count = tokens.shape[0]
    return pl.pallas_call(
        functools.partial(widen_kernel, source),
        name="widen",
        in_specs=[SMEM, VMEM, VMEM, VMEM] + source.specs(),
        out_specs=[VMEM] * 3 + [ANY] * 3,
        out_shape=[
            array((count, D)), array((count, FF)), array((count, FF)), pltpu.HBM(source.shape, BF16),
            pltpu.HBM((count, FF), BF16), pltpu.HBM((count, D), BF16),
        ],
        scratch_shapes=[
            pltpu.VMEM(source.shape, BF16), pltpu.VMEM((count, D), BF16), source.semaphores(), source.semaphores(),
            row_semaphores(1, count), row_semaphores(1, count), pltpu.SemaphoreType.DMA,
        ],
        compiler_params=limit(16),
        cost_estimate=cost(2 * count * D * 5 * D, 26 * count * D + 10 * D * D, count * FF),
    )(me, o, tokens, vectors, *source.arrays)


def column_sums(values):
    return jnp.sum(values, 0, keepdims=True)


def slope_back_kernel(source, me_ref, cot_ref, slope_ref, *refs):
    count = len(source.arrays)
    df_ref, projb_ref, fcb_ref, wp_ref, sems = refs[count:]
    copies = source.copies(me_ref[0], refs[:count], wp_ref, sems)
    for copy in copies:
        copy.start()
    projb_ref[...] = column_sums(cot_ref[...].astype(F32))
    fcb_ref[...] = jnp.zeros_like(fcb_ref)
    for copy in copies:
        copy.wait()

    def body(step, carry):
        rows = block_rows(step, 2 * ROWS)
        cot = cot_ref[rows, :]
        for part in range(4):
            cols = slice(part * D, (part + 1) * D)
            df = nt(cot, wp_ref[cols, :]).astype(BF16) * slope_ref[rows, cols]
            df_ref[rows, cols] = df
            fcb_ref[:, cols] += column_sums(df.astype(F32))
        return carry

    lax.fori_loop(0, cot_ref.shape[0] // (2 * ROWS), body, 0)


def slope_back(me, cot, slope, source):
    count = cot.shape[0]
    return pl.pallas_call(
        functools.partial(slope_back_kernel, source),
        name="slope_back",
        in_specs=[SMEM, VMEM, VMEM] + source.specs(),
        out_specs=[VMEM] * 3,
        out_shape=[array((count, FF)), array((1, D), F32), array((1, FF), F32)],
        scratch_shapes=[pltpu.VMEM(source.shape, BF16), source.semaphores()],
        compiler_params=limit(14),
        cost_estimate=cost(2 * count * D * 4 * D, 30 * count * D + 18 * D * D),
    )(me, cot, near(slope), *source.arrays)


def middle_back_kernel(
    ahead, cot_ref, df_ref, x1_far, vec_ref, w_ref, *refs
):
    away, refs = refs[:ahead], refs[ahead:]
    da_ref, do_ref, gain2_ref, bias2_ref, outb_ref, *held, x1_ref, row_sems, sems = refs
    enter = Rows([(x1_far, x1_ref)], row_sems)
    steps = cot_ref.shape[0] // ROWS
    for step in range(steps):
        enter.start(step)
    copies = [pltpu.make_async_copy(source, target, sems.at[at]) for at, (source, target) in enumerate(zip(away, held))]
    for copy in copies:
        copy.start()
    for ref in (gain2_ref, bias2_ref, outb_ref):
        ref[...] = jnp.zeros_like(ref)

    def body(index, carry):
        blocks = [2 * index, 2 * index + 1]
        rows = [block_rows(step, ROWS) for step in blocks]
        totals = [nt(df_ref[at, :], w_ref[:, :FF]) for at in rows]
        for step in blocks:
            enter.wait(step)
        das = []
        for at, total in zip(rows, totals):
            unit, scale = normalized(x1_ref[at, :].astype(F32))
            dx1 = cot_ref[at, :].astype(F32) + norm_back(total, vec_ref[6:7, :D], unit, scale)
            da = dx1.astype(BF16)
            das.append(da)
            da_ref[at, :] = da
            do_ref[at, :] = nt(da, w_ref[:, FF:]).astype(BF16)
            gain2_ref[...] += column_sums(total * unit)
        bias2_ref[...] += column_sums(totals[0]) + column_sums(totals[1])
        outb_ref[...] += column_sums(das[0].astype(F32)) + column_sums(das[1].astype(F32))
        return carry

    lax.fori_loop(0, steps // 2, body, 0)
    for copy in copies:
        copy.wait()


def middle_back(cot, df, x1, vectors, w, away):
    count = cot.shape[0]
    return pl.pallas_call(
        functools.partial(middle_back_kernel, len(away)),
        name="middle_back",
        in_specs=[VMEM] * 2 + [ANY] + [VMEM] * 2 + [ANY] * len(away),
        out_specs=[VMEM] * (5 + len(away)),
        out_shape=[array((count, D)), array((count, D))] + [array((1, D), F32)] * 3
        + [pltpu.VMEM(value.shape, BF16) for value in away],
        scratch_shapes=[pltpu.VMEM((count, D), BF16), row_semaphores(1, count), pltpu.SemaphoreType.DMA((len(away),))],
        compiler_params=limit(10),
        cost_estimate=cost(2 * count * D * 5 * D, 30 * count * D + 18 * D * D),
    )(cot, df, far(x1), vectors, near(w), *map(far, away))


def attend_back_kernel(
    first_head, group, do_ref, rd_ref, o_ref, pq_ref, pk_ref, v_ref, s_ref, q_ref, k_ref, fq, fk,
    dproj_ref, sums_ref, fmap_ref, state, gq, gk,
):
    heads_here = state.shape[0]
    width = heads_here * HD
    base = first_head // 2
    steps = do_ref.shape[0] // CHUNK
    for ref in (state, gq, gk, sums_ref):
        ref[...] = jnp.zeros_like(ref)
    ones = block_ones(4 * HD)
    halves = jnp.concatenate([ones[0:128, 0:128], ones[0:128, 0:128]], 0)
    row = lax.broadcasted_iota(jnp.int32, (CHUNK, CHUNK), 0)
    col = lax.broadcasted_iota(jnp.int32, (CHUNK, CHUNK), 1)
    causal = row >= col
    below = row <= col
    lane = lanes((CHUNK, 128))
    low = lane < HD

    def body(index, carry):
        step = steps - 1 - index
        rows = block_rows(step, CHUNK)
        for start in range(0, heads_here // 2, group):
            pairs = range(start, start + group)
            heads = range(2 * start, 2 * (start + group))
            pair_cols = {pair: slice((base + pair) * 128, (base + pair + 1) * 128) for pair in pairs}
            head_cols = {head: slice((first_head + head) * 128, (first_head + head + 1) * 128) for head in heads}
            pq = {head: pq_ref[rows, head_cols[head]] for head in heads}
            pk = {head: pk_ref[rows, head_cols[head]] for head in heads}
            scores = {head: nt(pk[head], pq[head]) for head in heads}
            numer = {p: (do_ref[rows, pair_cols[p]].astype(F32) * rd_ref[rows, pair_cols[p]].astype(F32)).astype(BF16).astype(F32) for p in pairs}
            denom = {}
            for p in pairs:
                product = numer[p] * o_ref[rows, pair_cols[p]].astype(F32)
                coarse = product.astype(BF16)
                fine = (product - coarse.astype(F32)).astype(BF16)
                denom[p] = -nn(jnp.concatenate([coarse, fine], 1), halves)
            vx = {}
            for p in pairs:
                vx[2 * p], vx[2 * p + 1] = value_pair(v_ref[rows, pair_cols[p]])
            scores = {head: jnp.where(below, scores[head], 0.0).astype(BF16) for head in heads}
            dn = {}
            for p in pairs:
                for head, top, rest in ((2 * p, numer[p], swap_halves(denom[p])), (2 * p + 1, swap_halves(numer[p]), denom[p])):
                    rounded = rest.astype(BF16).astype(F32)
                    tail = jnp.where(lane == HD, rounded, jnp.where(lane == HD + 1, rest - rounded, 0.0))
                    dn[head] = jnp.where(low, top, tail).astype(BF16)
            later = {head: state[head].astype(BF16) for head in heads}
            ds = {head: nt(dn[head], vx[head]) for head in heads}
            dst = {head: nt(vx[head], dn[head]) for head in heads}
            far_q = {head: nt(dn[head], s_ref[step, first_head + head]) for head in heads}
            far_k = {head: nt(vx[head], later[head]) for head in heads}
            far_v = {head: nn(pk[head], later[head]) for head in heads}
            dv = {head: nn(scores[head], dn[head]) + far_v[head] for head in heads}
            more = {head: tn(pq[head], dn[head]) for head in heads}
            ds = {head: jnp.where(causal, ds[head], 0.0).astype(BF16) for head in heads}
            dst = {head: jnp.where(below, dst[head], 0.0).astype(BF16) for head in heads}
            dq = {head: nn(ds[head], pk[head]) + far_q[head] for head in heads}
            dk = {head: nn(dst[head], pq[head]) + far_k[head] for head in heads}
            for head in heads:
                state[head] += more[head]
            out = {}
            for p in pairs:
                out[2, p] = jnp.where(low, dv[2 * p], swap_halves(dv[2 * p + 1])).astype(BF16)
            grads, feats, inner = {}, {}, {}
            for p in pairs:
                both = slice((base + p) * 256, (base + p + 1) * 256)
                for part, (grad, feat_ref) in enumerate(((dq, pq_ref), (dk, pk_ref))):
                    grads[part, p] = jnp.concatenate([grad[2 * p], grad[2 * p + 1]], 1)
                    feats[part, p] = feat_ref[rows, both].astype(F32)
                    inner[part, p] = nn((grads[part, p] * feats[part, p]).astype(BF16), ones)
            logits = {key: (feats[key] * (grads[key] - inner[key])).astype(BF16) for key in inner}
            for p in pairs:
                for part, (rows_ref, maps, total) in enumerate(((q_ref, fq, gq), (k_ref, fk, gk))):
                    out[part, p] = nt(logits[part, p], maps[base + p]).astype(BF16)
                    total[p] += tn(rows_ref[rows, pair_cols[p]], logits[part, p])
            for (part, p), value in out.items():
                cols = slice(part * width + p * 128, part * width + (p + 1) * 128)
                dproj_ref[rows, cols] = value
                sums_ref[:, cols] += column_sums(value.astype(F32))
        return carry

    lax.fori_loop(0, steps, body, 0)
    first = lanes((HD, 2 * HD)) < HD
    for head in range(heads_here):
        r, c = (head % 2) * HD, (head % 2) * 2 * HD
        bq = gq[head // 2, r : r + HD, c : c + 2 * HD]
        bk = gk[head // 2, r : r + HD, c : c + 2 * HD]
        fmap_ref[head * HD : (head + 1) * HD, :] = jnp.where(first, bq - swap_halves(bq), swap_halves(bk) - bk)


def attend_back(first, heads, do, rd, o, pq, pk, v, s, q, k, fq, fk, group=2):
    count = v.shape[0]
    width = heads * HD
    return pl.pallas_call(
        functools.partial(attend_back_kernel, first, group),
        name="attend_back",
        in_specs=[VMEM] * 11,
        out_specs=[VMEM] * 3,
        out_shape=[array((count, 3 * width)), array((1, 3 * width), F32), array((width, 2 * HD), F32)],
        scratch_shapes=[
            pltpu.VMEM((heads, 128, 128), F32), pltpu.VMEM((heads // 2, 128, 256), F32), pltpu.VMEM((heads // 2, 128, 256), F32),
        ],
        compiler_params=limit(12),
        cost_estimate=cost(2 * count * heads * 128 * 128 * 14, 40 * count * width),
    )(do, *map(near, (rd, o, pq, pk, v, s, q, k)), fq, fk)


def slot_of(index):
    return 2 * index if index < 4 else 2 * index - 7


def outer_rows_kernel(first, me_ref, left_ref, right_ref, out_ref):
    rows = out_ref.shape[1]
    right = right_ref[...]
    for index in range(4):
        start = pl.multiple_of((me_ref[0] ^ slot_of(first + index)) * rows, 128)
        out_ref[index] = tn(left_ref[:, pl.ds(start, rows)], right).astype(BF16)


def outer_rows(me, first, left, right):
    count, wide = left.shape
    across = right.shape[1]
    return pl.pallas_call(
        functools.partial(outer_rows_kernel, first),
        name="outer_rows",
        in_specs=[SMEM, VMEM, VMEM],
        out_specs=VMEM,
        out_shape=array((4, wide // 8, across)),
        compiler_params=limit(10),
        cost_estimate=cost(0 if first else count * wide * across, 0),
    )(me, left, right)


def outer_cols_kernel(plan, away, inputs, brought, me_ref, *refs):
    ins, refs = list(refs[:inputs]), refs[inputs:]
    sources, (send_ref, keep_ref), refs = refs[:brought], refs[brought : brought + 2], refs[brought + 2 :]
    targets, turned, refs = refs[:brought], refs[brought], refs[brought + 1 :]
    bring = [pltpu.make_async_copy(*pair, refs[-1].at[at]) for at, pair in enumerate(zip(sources, targets))]
    copies = {}
    for at, index in enumerate(away):
        held = refs[at]
        copies[index] = pltpu.make_async_copy(ins[index], held, refs[len(away)].at[at])
        copies[index].start()
        ins[index] = held
    for copy in bring:
        copy.start()
    rows = send_ref.shape[1]
    at = 0

    def by_slot(value):
        for shard in range(8):
            slot = me_ref[0] ^ shard
            turned[(slot >> 1) + 4 * (slot & 1), :, : value.shape[1]] = value[shard * rows : (shard + 1) * rows]

    for left, right in plan:
        across = ins[right].shape[1]
        if left is None:
            by_slot(ins[right][...].astype(BF16))
            keep_ref[:, :, at : at + across] = turned[0:4, :, :across]
            send_ref[:, :, at : at + across] = turned[4:8, :, :across]
            at += across
            continue
        if left in copies:
            copies[left].wait()
        by_slot(ins[left][...].T)
        whole = turned[...].reshape(8 * rows, turned.shape[2])
        for start in range(0, across, TILE):
            value = nn(whole, ins[right][:, start : start + TILE]).astype(BF16)
            keep_ref[:, :, at : at + TILE] = value[: 4 * rows].reshape(4, rows, TILE)
            send_ref[:, :, at : at + TILE] = value[4 * rows :].reshape(4, rows, TILE)
            at += TILE
    for copy in bring:
        copy.wait()


def outer_cols(me, arrays, plan, away=(), bring=()):
    across = sum(arrays[right].shape[1] for _, right in plan)
    out = array((4, D // 8, across))
    send, keep, *brought = pl.pallas_call(
        functools.partial(outer_cols_kernel, plan, away, len(arrays), len(bring)),
        name="outer_cols",
        in_specs=[SMEM] + [ANY if index in away else VMEM for index in range(len(arrays))] + [ANY] * len(bring),
        out_specs=[VMEM] * (2 + len(bring)),
        out_shape=[out, out] + [pltpu.VMEM(value.shape, BF16) for value in bring],
        scratch_shapes=[pltpu.VMEM((8, D // 8, arrays[0].shape[0]), BF16)]
        + [pltpu.VMEM(arrays[index].shape, BF16) for index in away]
        + [pltpu.SemaphoreType.DMA((max(1, len(away)),)), pltpu.SemaphoreType.DMA((max(1, len(bring)),))],
        compiler_params=limit(11),
        cost_estimate=cost(0, 0),
    )(me, *[far(value) if index in away else value for index, value in enumerate(arrays)], *map(far, bring))
    return ((send, keep), brought) if bring else (send, keep)


def input_back_kernel(source, groups, me_ref, tok_ref, da_ref, vec_ref, *refs):
    parts, refs = refs[: len(groups)], refs[len(groups) :]
    count = len(source.arrays)
    out_ref, gain1_ref, bias1_ref, w_ref, sems = refs[count:]
    copies = source.copies(me_ref[0], refs[:count], w_ref, sems)
    for copy in copies:
        copy.start()
    for ref in (gain1_ref, bias1_ref):
        ref[...] = jnp.zeros_like(ref)
    for copy in copies:
        copy.wait()

    def body(index, carry):
        rows = [block_rows(2 * index + half, ROWS) for half in range(2)]
        grads = []
        for at in rows:
            grad = None
            for (first, heads), part_ref in zip(groups, parts):
                width = heads * HD
                for part in range(3):
                    cols = slice(part * D + first * HD, part * D + (first + heads) * HD)
                    more = nt(part_ref[at, part * width : (part + 1) * width], w_ref[:, cols])
                    grad = more if grad is None else grad + more
            grads.append(grad)
        for at, grad in zip(rows, grads):
            unit, scale = normalized(tok_ref[at, :].astype(F32))
            value = da_ref[at, :].astype(F32) + norm_back(grad, vec_ref[4:5, :D], unit, scale)
            out_ref[at, :] = value.astype(BF16)
            gain1_ref[...] += column_sums(grad * unit)
        bias1_ref[...] += column_sums(grads[0]) + column_sums(grads[1])
        return carry

    lax.fori_loop(0, tok_ref.shape[0] // (2 * ROWS), body, 0)


def input_back(me, groups, parts, tokens, da, vectors, source):
    count = tokens.shape[0]
    return pl.pallas_call(
        functools.partial(input_back_kernel, source, groups),
        name="input_back",
        in_specs=[SMEM] + [VMEM] * (3 + len(parts)) + source.specs(),
        out_specs=[VMEM] * 3,
        out_shape=[array((count, D)), array((1, D), F32), array((1, D), F32)],
        scratch_shapes=[pltpu.VMEM(source.shape, BF16), source.semaphores()],
        compiler_params=limit(14),
        cost_estimate=cost(2 * count * D * 3 * D, 14 * count * D + 6 * D * D),
    )(me, tokens, da, vectors, *parts, *source.arrays)


def narrow_kernel(source, base, me_ref, g_far, x1_far, vec_ref, *refs):
    if source is None:
        w_ref, out_ref, g_ref, x1_ref, row_sems = refs
        copies = []
    else:
        count = len(source.arrays)
        out_ref, w_ref, g_ref, x1_ref, row_sems, sems = refs[count:]
        copies = source.copies(me_ref[0], refs[:count], w_ref, sems)
    steps = out_ref.shape[0] // ROWS
    rows_here = pl.ds(base, out_ref.shape[0])
    enter = Rows([(g_far.at[rows_here, :], g_ref), (x1_far.at[rows_here, :], x1_ref)], row_sems)
    for copy in copies:
        copy.start()
    for step in range(steps):
        enter.start(step)
    for copy in copies:
        copy.wait()

    def body(step, carry):
        enter.wait(step)
        rows = block_rows(step, ROWS)
        out_ref[rows, :] = (x1_ref[rows, :].astype(F32) + (nn(g_ref[rows, :], w_ref[...]) + vec_ref[3:4, :D])).astype(BF16)
        return carry

    lax.fori_loop(0, steps, body, 0)


def narrow(me, base, count, g, x1, vectors, source):
    first = isinstance(source, Source)
    return pl.pallas_call(
        functools.partial(narrow_kernel, source if first else None, base),
        name="narrow",
        in_specs=[SMEM, ANY, ANY, VMEM] + (source.specs() if first else [VMEM]),
        out_specs=[VMEM] * 2 if first else VMEM,
        out_shape=[array((count, D)), array(source.shape)] if first else array((count, D)),
        scratch_shapes=[pltpu.VMEM((count, FF), BF16), pltpu.VMEM((count, D), BF16), row_semaphores(2, count)]
        + ([source.semaphores()] if first else []),
        compiler_params=limit(10),
        cost_estimate=cost(2 * count * D * FF, 14 * count * D + 8 * D * D),
    )(me, far(g), far(x1), vectors, *(source.arrays if first else [source]))


def fold_kernel(keep_ref, arrived_ref, *outs):
    for index, out in enumerate(outs):
        out[...] = keep_ref[index] + arrived_ref[index]


def fold(keep, arrived):
    slots, rows, across = keep.shape
    return pl.pallas_call(
        fold_kernel,
        name="fold",
        in_specs=[VMEM] * 2,
        out_specs=[VMEM] * slots,
        out_shape=[array((rows, across))] * slots,
        compiler_params=limit(8),
        cost_estimate=cost(keep.size, 6 * keep.size),
    )(keep, arrived)


def total_kernel(*refs):
    *values, out = refs
    result = values[0][...].astype(F32)
    for value in values[1:]:
        result = result + value[...].astype(F32)
    out[...] = result.astype(out.dtype)


def total(*values):
    return pl.pallas_call(
        total_kernel,
        name="total",
        in_specs=[VMEM] * len(values),
        out_specs=VMEM,
        out_shape=array(values[0].shape),
        compiler_params=limit(8),
        cost_estimate=cost(4 * values[0].size, 10 * values[0].size),
    )(*values)


def cross_kernel(keep_ref, arrived_ref, send_x, send_y, top, bottom):
    half = top.shape[1]
    for outs, rows in (((top, send_x, top, send_x), slice(0, half)), ((bottom, bottom, send_y, send_y), slice(half, 2 * half))):
        for slot, out in enumerate(outs):
            out[slot // 2 if outs[0] is outs[2] else slot % 2] = keep_ref[slot, rows, :] + arrived_ref[slot, rows, :]


def cross_over(keep, arrived):
    _, rows, across = keep.shape
    return pl.pallas_call(
        cross_kernel,
        name="cross_over",
        in_specs=[VMEM] * 2,
        out_specs=[VMEM] * 4,
        out_shape=[array((2, rows // 2, across))] * 4,
        compiler_params=limit(8),
        cost_estimate=cost(keep.size, 6 * keep.size),
    )(keep, arrived)


def turn_kernel(top, bottom, over_x, over_y, send_y, send_x, mine_top, mine_bottom):
    mine_top[...] = top[0] + over_x[0]
    send_y[...] = top[1] + over_x[1]
    mine_bottom[...] = bottom[0] + over_y[0]
    send_x[...] = bottom[1] + over_y[1]


def turn_over(top, bottom, over_x, over_y):
    _, half, across = top.shape
    return pl.pallas_call(
        turn_kernel,
        name="turn_over",
        in_specs=[VMEM] * 4,
        out_specs=[VMEM] * 4,
        out_shape=[array((half, across))] * 4,
        compiler_params=limit(8),
        cost_estimate=cost(4 * half * across, 24 * half * across),
    )(top, bottom, over_x, over_y)


def halve_kernel(side_ref, top, last_y, bottom, last_x, own_ref, other_ref):
    for side, one, two in ((0, top, last_y), (1, bottom, last_x)):
        value = one[...] + two[...]

        @pl.when(side_ref[0] == side)
        def _():
            own_ref[...] = value

        @pl.when(side_ref[0] != side)
        def _():
            other_ref[...] = value


def halve(side, top, last_y, bottom, last_x):
    return pl.pallas_call(
        halve_kernel,
        name="halve",
        in_specs=[SMEM] + [VMEM] * 4,
        out_specs=[VMEM] * 2,
        out_shape=[array(top.shape)] * 2,
        compiler_params=limit(8),
        cost_estimate=cost(2 * top.size, 12 * top.size),
    )(side, top, last_y, bottom, last_x)


def stack_kernel(top, last_y, bottom, last_x, out_ref):
    half = top.shape[0]
    out_ref[:half, :] = top[...] + last_y[...]
    out_ref[half:, :] = bottom[...] + last_x[...]


def stack(top, last_y, bottom, last_x):
    half, across = top.shape
    return pl.pallas_call(
        stack_kernel,
        name="stack",
        in_specs=[VMEM] * 4,
        out_specs=VMEM,
        out_shape=array((2 * half, across)),
        compiler_params=limit(8),
        cost_estimate=cost(2 * top.size, 12 * top.size),
    )(top, last_y, bottom, last_x)


def join_kernel(side_ref, own_ref, other_ref, out_ref):
    half = own_ref.shape[0]
    out_ref[block_rows(side_ref[0], half), :] = own_ref[...].astype(F32)
    out_ref[block_rows(1 - side_ref[0], half), :] = other_ref[...].astype(F32)


def join(side, own, other):
    half, across = own.shape
    return pl.pallas_call(
        join_kernel,
        name="join",
        in_specs=[SMEM] + [VMEM] * 2,
        out_specs=VMEM,
        out_shape=array((2 * half, across), F32),
        compiler_params=limit(8),
        cost_estimate=cost(half * across, 12 * half * across),
    )(side, own, other)


def write_lines(lines, outs):
    at = 0
    for out in outs:
        size = out.shape[0]
        for start in range(0, size, 128):
            count = min(128, size - start)
            out[pl.ds(start, count)] = lines[at : at + 1, :count].reshape(count)
            at += 1


def publish_kernel(groups, side_ref, own_ref, other_ref, one_ref, two_ref, qkvw_ref, outw_ref, fmap_ref, *outs):
    half = own_ref.shape[0]
    for side, ref in ((side_ref[0], own_ref), (1 - side_ref[0], other_ref)):
        rows = block_rows(side, half)
        outw_ref[rows, :] = ref[:, :D].astype(F32)
        first, heads = groups[0]
        width = heads * HD
        for part in range(3):
            value = ref[:, D + part * width : D + (part + 1) * width]
            qkvw_ref[rows, part * D + first * HD : part * D + first * HD + width] = value.astype(F32)
    last = one_ref[...].astype(F32) + two_ref[...].astype(F32)
    first, heads = groups[1]
    width = heads * HD
    for part in range(3):
        qkvw_ref[:, part * D + first * HD : part * D + first * HD + width] = last[:, part * width : (part + 1) * width]
    fmap_ref[...] = last[:, 3 * width : 3 * width + 2 * HD]
    write_lines(last[:, 3 * width + 2 * HD :], outs)


def publish(groups, side, own, other, one, two, sizes):
    rows = one.shape[0]
    return pl.pallas_call(
        functools.partial(publish_kernel, groups),
        name="publish",
        in_specs=[SMEM] + [VMEM] * 4,
        out_specs=[VMEM] * (3 + len(sizes)),
        out_shape=[array((rows, 3 * D), F32), array((rows, D), F32), array((rows, 2 * HD), F32)] + [array((size,), F32) for size in sizes],
        compiler_params=limit(8),
        cost_estimate=cost(rows * 3 * D * 4, rows * 3 * D * 12),
    )(side, own, other, one, two)


def line_count(sizes):
    return sum(-(-size // 128) for size in sizes)


def to_lines(vector, start, size):
    lines = []
    for at in range(0, size, 128):
        count = min(128, size - at)
        line = vector[:, start + at : start + at + count]
        if count < 128:
            line = jnp.concatenate([line, jnp.zeros((1, 128 - count), F32)], 1)
        lines.append(line)
    return lines


def pack_kernel(*refs):
    *vectors, fm_ref, w_ref, out_ref = refs
    width = w_ref.shape[1]
    out_ref[:, :width] = w_ref[...]
    out_ref[:, width : width + 128] = fm_ref[...]
    lines = []
    for vector in vectors:
        size = vector.shape[0]
        lines += to_lines(vector[...].astype(F32).reshape(1, size), 0, size)
    lines += [jnp.zeros((1, 128), F32)] * (w_ref.shape[0] - len(lines))
    out_ref[:, width + 128 :] = jnp.concatenate(lines, 0).astype(BF16)


def pack(w, fm, vectors):
    rows, width = w.shape
    return pl.pallas_call(
        pack_kernel,
        name="pack",
        in_specs=[VMEM] * (len(vectors) + 2),
        out_specs=VMEM,
        out_shape=array((rows, width + 256)),
        compiler_params=limit(56),
    )(*vectors, fm, w)


def small_grads_kernel(shards, *refs):
    *vectors, out_ref = refs
    rows = out_ref.shape[0] // shards
    for shard in range(shards):
        lines = []
        for vector in vectors:
            size = vector.shape[1] // shards
            lines += to_lines(vector[...], shard * size, size)
        lines += [jnp.zeros((1, 128), F32)] * (rows - len(lines))
        out_ref[shard * rows : (shard + 1) * rows, :] = jnp.concatenate(lines, 0)


def small_grads(shards, vectors):
    return pl.pallas_call(
        functools.partial(small_grads_kernel, shards),
        name="small_grads",
        in_specs=[VMEM] * len(vectors),
        out_specs=VMEM,
        out_shape=array((D, 128), F32),
        compiler_params=limit(8),
    )(*vectors)


def small_owned_kernel(lines_ref, *outs):
    write_lines(lines_ref[...], outs)


def small_owned(lines, sizes):
    return pl.pallas_call(
        small_owned_kernel,
        name="small_owned",
        in_specs=[VMEM],
        out_specs=[VMEM] * len(sizes),
        out_shape=[array((size,), F32) for size in sizes],
        compiler_params=limit(8),
    )(lines)


GROUPS = ((0, 8), (8, 4))


def after(value, *others):
    return lax.optimization_barrier((value, *others))[0]


def exchange(value, axis, mask):
    return lax.ppermute(value, axis, [(i, i ^ mask) for i in range(lax.axis_size(axis))])


class Gather:
    def __init__(self, shard):
        self.shard, self.rows = shard, shard.shape[0]
        self.hand = by_hand(self.rows)

    def start(self, *others):
        if not self.hand:
            self.full = lax.all_gather(self.shard, "fsdp", axis=0, tiled=True)
            return ()
        shard = after(self.shard, *others) if others else self.shard
        self.over_x, self.over_y = exchange(shard, "fsdp", 2), exchange(shard, "fsdp", 4)
        self.sibling = exchange(shard, "fsdp", 1)
        return self.over_x, self.over_y

    def relay(self, *others):
        if not self.hand:
            return ()
        half = self.rows // 2
        over_x, over_y, self.sibling = lax.optimization_barrier((self.over_x, self.over_y, self.sibling, *others))[:3]
        self.pieces = over_y[:half], over_x[half:]
        self.upper, self.lower = exchange(self.pieces[0], "fsdp", 2), exchange(self.pieces[1], "fsdp", 4)
        self.shared = [((3, 0), exchange(over_x, "fsdp", 1)), ((5, 0), exchange(over_y, "fsdp", 1))]
        return self.pieces

    def settled(self):
        return [value for _, value in self.shared] if self.hand else []

    def finish(self, *others):
        if not self.hand:
            return Source([(0, 0)], [self.full], self.rows, self.full.shape[0])
        half = self.rows // 2
        upper, lower = self.upper, self.lower
        if others:
            upper, lower = lax.optimization_barrier((upper, lower, *others))[:2]
        held = [((0, 0), self.shard), ((2, 0), self.over_x), ((4, 0), self.over_y), ((1, 0), self.sibling)] + self.shared
        held += [((6, 0), upper), ((6, half), lower)]
        held += [((7, 0), exchange(upper, "fsdp", 1)), ((7, half), exchange(lower, "fsdp", 1))]
        return Source([place for place, _ in held], [part for _, part in held], self.rows, 8 * self.rows)


def by_hand(rows):
    return lax.axis_size("fsdp") == 8 and lax.axis_size("dp") == 4 and rows % 32 == 0


class Scatter:
    def __init__(self, pair):
        send, self.keep = pair
        self.arrived = exchange(send, "fsdp", 1)

    def cross(self, *others):
        send_x, send_y, self.top, self.bottom = cross_over(self.keep, after(self.arrived, *others))
        self.over_x, self.over_y = exchange(send_x, "fsdp", 2), exchange(send_y, "fsdp", 4)
        return send_x, send_y

    def turn(self, *others):
        over_x, over_y = lax.optimization_barrier((self.over_x, self.over_y, *others))[:2]
        send_y, send_x, self.top, self.bottom = turn_over(self.top, self.bottom, over_x, over_y)
        self.last_y, self.last_x = exchange(send_y, "fsdp", 4), exchange(send_x, "fsdp", 2)
        return send_y, send_x

    def finish(self, *others):
        last_y, last_x = lax.optimization_barrier((self.last_y, self.last_x, *others))[:2]
        return self.top, last_y, self.bottom, last_x

    def straight(self, *others):
        self.mine, *away = fold(self.keep, after(self.arrived, *others))
        self.moved = [exchange(value, "fsdp", mask) for value, mask in zip(away, (2, 4, 6))]
        return away

    def arrive(self, *others):
        return total(self.mine, *lax.optimization_barrier((*self.moved, *others))[:3])


class Planes:
    def __init__(self, side, values):
        self.own, self.other = halve(side, *values)
        self.moved = exchange(self.other, "dp", 1)

    def mirror(self, *others):
        self.own = self.own + after(self.moved, *others)
        self.moved = exchange(self.own, "dp", 3)
        return self.own

    def back(self, *others):
        self.own = self.own + after(self.moved, *others)
        self.moved = exchange(self.own, "dp", 1)
        return self.own

    def finish(self, *others):
        return self.own, after(self.moved, *others)


def outer(left, right):
    return tn(left, right).astype(BF16)


def on_device(
    tokens, lengths, qkv_weight, qkv_bias, out_weight, out_bias, fc_weight, fc_bias, proj_weight, proj_bias,
    norm1_gain, norm1_bias, norm2_gain, norm2_bias, feature_map, cotangent,
):
    shards = lax.axis_size("fsdp")
    me = lax.axis_index("fsdp").astype(jnp.int32).reshape(1)
    plane = lax.axis_index("dp").astype(jnp.int32).reshape(1)
    side = (plane ^ (plane >> 1)) & 1
    qkv_weight, me, side = lax.optimization_barrier((qkv_weight, me, side))
    small = [qkv_bias, out_bias, fc_bias, proj_bias, norm1_gain, norm1_bias, norm2_gain, norm2_bias]
    first = Gather(pack(qkv_weight, feature_map, small))
    second = Gather(jnp.concatenate([fc_weight, out_weight], 1))
    third = Gather(proj_weight)
    first.start()
    second.start(*first.relay())
    first_source = first.finish()
    v, pq, pk, vectors, fq, fk, h1, q, k, v_far, pq_far, pk_far = project(
        me, lengths, tokens, first_source, [value.shape[0] for value in small]
    )
    second.relay(v)
    o, o_far, rd, s = attend(lengths, pq, pk, v)
    parts = second.finish(o)
    third.start(o)
    h2, g, slope, w_fc, g_far, x1 = widen(me, o, tokens, vectors, parts)
    g = after(g, *third.relay(g))
    hand = by_hand(qkv_weight.shape[0])
    summed = lambda share: lax.psum(share.astype(BF16), "dp").astype(F32)
    over = lambda value: lax.psum_scatter(value, "fsdp", scatter_dimension=0, tiled=True)
    if hand:
        send = after(outer_rows(me, 4, g, cotangent), *third.settled())
        keep = outer_rows(me, 0, after(g, send), cotangent)
        proj_scatter = Scatter((send, keep))
        third_source = third.finish(keep)
        slope = after(slope, *proj_scatter.cross(keep))
    else:
        third_source = third.finish()
    df, projb, fcb = slope_back(me, cotangent, slope, third_source)
    if hand:
        pair, (w_fc,) = outer_cols(me, [h2, df], [(0, 1)], (), (w_fc,))
        fc_scatter = Scatter(pair)
        df = after(df, *proj_scatter.turn(pair[0]))
    da, do, gain2, bias2, outb, *held = middle_back(
        cotangent, df, x1, vectors, w_fc, [rd, o_far, pq_far, pk_far, v_far, s, q, k]
    )
    if hand:
        proj_planes = Planes(side, proj_scatter.finish(do))
        do = after(do, proj_planes.other, *fc_scatter.cross(do))
    parts, sums, maps = [], [], []
    for index, (start, heads) in enumerate(GROUPS):
        dproj, sum_grad, fmap_grad = attend_back(start, heads, do, *held, fq, fk)
        parts.append(dproj)
        sums.append(sum_grad)
        maps.append(fmap_grad)
        if hand and index == 0:
            left = after(h1, proj_planes.mirror(dproj), *fc_scatter.turn(dproj))
            pair = outer_cols(me, [o_far, da, left, dproj], [(0, 1), (2, 3)], (0, 2))
            qkv_scatter = Scatter(pair)
            fc_planes = Planes(side, fc_scatter.finish(pair[0]))
            do = after(do, fc_planes.other)
    if hand:
        tokens = after(tokens, proj_planes.back(dproj), *qkv_scatter.cross(dproj), fc_planes.mirror(dproj))
    input_grad, gain1, bias1 = input_back(me, GROUPS, parts, tokens, da, vectors, first_source)
    spread = lambda values: jnp.concatenate([
        value[:, part * heads * HD : (part + 1) * heads * HD] for part in range(3) for (_, heads), value in zip(GROUPS, values)
    ], 1)
    ordered = spread(sums)
    small = [ordered[:, : 2 * D], ordered[:, 2 * D :], outb, fcb, projb, gain1, bias1, gain2, bias2]
    table = small_grads(shards, small)
    sizes = [value.shape[1] // shards for value in small]
    if hand:
        left = after(h1, *qkv_scatter.turn(table), fc_planes.back(table))
        pair = outer_cols(me, [left, dproj, jnp.concatenate(maps, 0), table], [(0, 1), (None, 2), (None, 3)], (0,))
        last_scatter = Scatter(pair)
        projw_grad = join(side, *proj_planes.finish(pair[0]))
        x1 = after(x1, pair[0], projw_grad)
    if hand:
        qkv_planes = Planes(side, qkv_scatter.finish(pair[0]))
        x1 = after(x1, qkv_planes.other)
    piece, w_proj = narrow(me, 0, ROWS, g_far, x1, vectors, third_source)
    pieces = [piece]
    for base in range(ROWS, tokens.shape[0], ROWS):
        if hand and base == ROWS:
            x1 = after(x1, *last_scatter.straight(piece))
        if hand and base == 2 * ROWS:
            fcw_grad = join(side, *fc_planes.finish(pieces[-1]))
            x1 = after(x1, fcw_grad, qkv_planes.mirror(pieces[-1]))
        if hand and base == 3 * ROWS:
            share = last_scatter.arrive(pieces[-1])
            x1 = after(x1, share)
        pieces.append(narrow(me, base, ROWS, g_far, x1, vectors, w_proj))
    block_out = jnp.concatenate(pieces, 0)
    if hand:
        qkv_planes.back(pieces[-1])
        share = share + after(exchange(share, "dp", 1), pieces[-1])
        qkvw_grad, outw_grad, fmap_grad, *vectors = publish(
            GROUPS, side, *qkv_planes.finish(), share, exchange(share, "dp", 3), sizes
        )
    else:
        vectors = small_owned(lax.psum(over(table), "dp"), sizes)
    qkb, vb, outb, fcb, projb, gain1, bias1, gain2, bias2 = vectors
    if not hand:
        projw_grad = summed(over(outer(g_far, cotangent)))
        fcw_grad, outw_grad = summed(over(outer(h2, df))), summed(over(outer(o_far, da)))
        qkvw_grad, fmap_grad = summed(over(outer(h1, spread(parts)))), summed(over(jnp.concatenate(maps, 0)))
    return (
        block_out, input_grad, qkvw_grad, qkb, vb, outw_grad, outb, fcw_grad, fcb,
        projw_grad, projb, gain1, bias1, gain2, bias2, fmap_grad,
    )


def solution(mesh):
    rows = P(("dp", "fsdp"), None)
    wide = P("fsdp", None)
    flat = P("fsdp")
    in_specs = (
        rows, P(("dp", "fsdp")), wide, flat, wide, flat, wide, flat, wide, flat, flat, flat, flat, flat, wide, rows,
    )
    out_specs = (rows, rows, wide, flat, flat, wide, flat, wide, flat, wide, flat, flat, flat, flat, flat, wide)
    return jax.shard_map(on_device, mesh=mesh, in_specs=in_specs, out_specs=out_specs, check_vma=False)
```

```python
import functools

import jax
import jax.numpy as jnp
from jax import lax
from jax.experimental import pallas as pl
from jax.experimental.pallas import tpu as pltpu
from jax.sharding import PartitionSpec as P

D = 768
HEADS = 12
HD = 64
PAIRS = HEADS // 2
FF = 3072
ROWS = 256
CHUNK = 256
TILE = 256
EPSILON = 1e-05
SAFE = 60.0
SCALE = 20
F32 = jnp.float32
BF16 = jnp.bfloat16
ROOT = 0.7978845608028654
CUBE = 0.044715
VMEM = pl.BlockSpec(memory_space=pltpu.VMEM)
SMEM = pl.BlockSpec(memory_space=pltpu.SMEM)
ANY = pl.BlockSpec(memory_space=pl.ANY)
VECTORS = (8, FF)
MAPS = (PAIRS, 128, 256)


def nn(left, right):
    return lax.dot_general(left, right, (((1,), (0,)), ((), ())), preferred_element_type=F32)


def nt(left, right):
    return lax.dot_general(left, right, (((1,), (1,)), ((), ())), preferred_element_type=F32)


def tn(left, right):
    return lax.dot_general(left, right, (((0,), (0,)), ((), ())), preferred_element_type=F32)


def limit(mib):
    return pltpu.CompilerParams(vmem_limit_bytes=mib * 1024 * 1024)


def cost(flops, size, trans=0):
    return pl.CostEstimate(flops=int(SCALE * flops), bytes_accessed=int(size), transcendentals=int(trans))


def array(shape, kind=BF16):
    return jax.ShapeDtypeStruct(shape, kind)


def near(value):
    return pltpu.with_memory_space_constraint(value, pltpu.VMEM)


def far(value):
    return pltpu.with_memory_space_constraint(value, pltpu.HBM)


def lanes(shape):
    return lax.broadcasted_iota(jnp.int32, shape, 1)


def block_rows(index, count):
    return pl.ds(pl.multiple_of(index * count, count), count)


def normalized(values):
    middle = jnp.mean(values, -1, keepdims=True)
    centred = values - middle
    spread = jnp.mean(centred * centred, -1, keepdims=True)
    scale = lax.rsqrt(spread + EPSILON)
    return centred * scale, scale


def norm_back(grad, gain, unit, scale):
    scaled = grad * gain
    first = jnp.mean(scaled, -1, keepdims=True)
    second = jnp.mean(scaled * unit, -1, keepdims=True)
    return (scaled - first - unit * second) * scale


def swap_halves(values):
    return pltpu.roll(values, 64, 1)


def block_ones(size):
    row = lax.broadcasted_iota(jnp.int32, (size, size), 0) // HD
    col = lax.broadcasted_iota(jnp.int32, (size, size), 1) // HD
    return jnp.where(row == col, 1.0, 0.0).astype(BF16)


def build_maps(map_ref, fq, fk):
    fq[...] = jnp.zeros_like(fq)
    fk[...] = jnp.zeros_like(fk)
    low = lanes((HD, 2 * HD)) < HD
    for head in range(HEADS):
        block = map_ref[head * HD : (head + 1) * HD, :].astype(F32)
        turned = swap_halves(block)
        row, col = (head % 2) * HD, (head % 2) * 2 * HD
        fq[head // 2, row : row + HD, col : col + 2 * HD] = jnp.where(low, block, -turned).astype(BF16)
        fk[head // 2, row : row + HD, col : col + 2 * HD] = jnp.where(low, turned, -block).astype(BF16)


class Source:
    def __init__(self, places, arrays, rows, total):
        self.places, self.arrays, self.rows = places, list(arrays), rows
        self.shape = (total, arrays[0].shape[1])

    def specs(self):
        return [ANY] * len(self.arrays)

    def semaphores(self):
        return pltpu.SemaphoreType.DMA((len(self.arrays),))

    def copies(self, me, refs, held, sems, first=0, count=None):
        made = []
        count = self.shape[1] - first if count is None else count
        cols = pl.ds(first, count)
        for at, ((slot, offset), ref) in enumerate(zip(self.places, refs)):
            start = 0 if len(self.places) == 1 else pl.multiple_of((me ^ slot) * self.rows + offset, 16)
            made.append(pltpu.make_async_copy(ref.at[:, cols], held.at[pl.ds(start, ref.shape[0]), cols], sems.at[at]))
        return made


class Rows:
    def __init__(self, pairs, sems):
        self.pairs, self.sems = pairs, sems

    def copies(self, step):
        rows = block_rows(step, ROWS)
        return [
            pltpu.make_async_copy(source.at[rows, :], target.at[rows, :], self.sems.at[at, step])
            for at, (source, target) in enumerate(self.pairs)
        ]

    def start(self, step):
        for copy in self.copies(step):
            copy.start()

    def wait(self, step):
        for copy in self.copies(step):
            copy.wait()


def row_semaphores(pairs, count):
    return pltpu.SemaphoreType.DMA((pairs, count // ROWS))


def read_vectors(table, rows, sizes, out):
    for shard in range(table.shape[0] // rows):
        line = shard * rows
        for row, size in enumerate(sizes):
            for at in range(0, size, 128):
                count = min(128, size - at)
                out[row : row + 1, shard * size + at : shard * size + at + count] = table[line : line + 1, :count].astype(F32)
                line += 1


def project_kernel(source, sizes, me_ref, len_ref, tok_ref, *refs):
    count = len(source.arrays)
    v_ref, pq_ref, pk_ref, vec_ref, fq, fk, *far_refs, w_ref, h_ref, q_ref, k_ref, side_sems, sems, row_sems = refs[count:]
    leave = Rows(list(zip((h_ref, q_ref, k_ref, v_ref, pq_ref, pk_ref), far_refs)), row_sems)
    steps = tok_ref.shape[0] // ROWS
    side = source.copies(me_ref[0], refs[:count], w_ref, side_sems, 3 * D)
    main = source.copies(me_ref[0], refs[:count], w_ref, sems, 0, 3 * D)
    for copy in side + main:
        copy.start()
    vec_ref[...] = jnp.zeros_like(vec_ref)
    ones = block_ones(4 * HD)
    for copy in side:
        copy.wait()
    read_vectors(w_ref.at[:, 3 * D + 128 :], source.rows, sizes, vec_ref)
    build_maps(w_ref.at[:, 3 * D : 3 * D + 128], fq, fk)

    def norm(step, carry):
        rows = block_rows(step, ROWS)
        unit, _ = normalized(tok_ref[rows, :].astype(F32))
        h_ref[rows, :] = (unit * vec_ref[4:5, :D] + vec_ref[5:6, :D]).astype(BF16)
        return carry

    lax.fori_loop(0, steps, norm, 0)
    for copy in main:
        copy.wait()

    def body(step, carry):
        rows = block_rows(step, ROWS)
        h = h_ref[rows, :]
        wide = [(nn(h, w_ref[:, p * D : (p + 1) * D]) + vec_ref[0:1, p * D : (p + 1) * D]).astype(BF16) for p in range(3)]
        for out, value in zip((q_ref, k_ref, v_ref), wide):
            out[rows, :] = value
        place = step * ROWS + lax.broadcasted_iota(jnp.int32, (ROWS, 1), 0)
        live = (place < len_ref[0]).astype(F32)
        largest = jnp.zeros((ROWS, 256), F32)
        for part, (maps, out) in enumerate(((fq, pq_ref), (fk, pk_ref))):
            u = [nn(wide[part][:, p * 128 : (p + 1) * 128], maps[p]) for p in range(PAIRS)]
            e = [jnp.exp(value) for value in u]
            total = [nn(value.astype(BF16), ones) for value in e]
            for p in range(PAIRS):
                largest = jnp.maximum(largest, u[p])
                share = e[p] * pl.reciprocal(total[p], approx=True)
                if part == 1:
                    share = share * live
                out[rows, p * 256 : (p + 1) * 256] = share.astype(BF16)

        @pl.when(jnp.logical_not(jnp.max(largest) <= SAFE))
        def _():
            for part, (maps, rows_ref, out) in enumerate(((fq, q_ref, pq_ref), (fk, k_ref, pk_ref))):
                for p in range(PAIRS):
                    u = nn(rows_ref[rows, p * 128 : (p + 1) * 128], maps[p])
                    for group in range(4):
                        piece = u[:, group * HD : (group + 1) * HD]
                        e = jnp.exp(piece - jnp.max(piece, -1, keepdims=True))
                        share = e / jnp.sum(e, -1, keepdims=True)
                        if part == 1:
                            share = share * live
                        out[rows, p * 256 + group * HD : p * 256 + (group + 1) * HD] = share.astype(BF16)

        leave.start(step)
        return carry

    lax.fori_loop(0, steps, body, 0)
    for step in range(steps):
        leave.wait(step)


def project(me, lengths, tokens, source, sizes):
    count = tokens.shape[0]
    return pl.pallas_call(
        functools.partial(project_kernel, source, sizes),
        name="project",
        in_specs=[SMEM, SMEM, VMEM] + source.specs(),
        out_specs=[VMEM] * 6 + [ANY] * 6,
        out_shape=[array((count, D)), array((count, 2 * D)), array((count, 2 * D)), array(VECTORS, F32), array(MAPS), array(MAPS)]
        + [pltpu.HBM((count, D), BF16)] * 4 + [pltpu.HBM((count, 2 * D), BF16)] * 2,
        scratch_shapes=[pltpu.VMEM(source.shape, BF16)] + [pltpu.VMEM((count, D), BF16)] * 3
        + [source.semaphores(), source.semaphores(), row_semaphores(6, count)],
        compiler_params=limit(17),
        cost_estimate=cost(0, 0),
    )(me, lengths, tokens, *source.arrays)


def value_pair(v_pair):
    low = lanes(v_pair.shape) < HD
    wide = v_pair.astype(F32)
    return (
        jnp.where(low, wide, 1.0).astype(BF16),
        jnp.where(low, swap_halves(wide), 1.0).astype(BF16),
    )


def attend_kernel(group, len_ref, pq_ref, pk_ref, v_ref, o_ref, o_far, rd_far, s_far, rd_ref, s_ref, state, row_sems, s_sems):
    leave = Rows([(o_ref, o_far), (rd_ref, rd_far)], row_sems)
    leave_state = lambda step: pltpu.make_async_copy(s_ref.at[step], s_far.at[step], s_sems.at[step])
    steps = v_ref.shape[0] // CHUNK
    state[...] = jnp.zeros_like(state)
    row = lax.broadcasted_iota(jnp.int32, (CHUNK, CHUNK), 0)
    col = lax.broadcasted_iota(jnp.int32, (CHUNK, CHUNK), 1)
    causal = row >= col
    low = lanes((CHUNK, 128)) < HD
    place = lax.broadcasted_iota(jnp.int32, (CHUNK, 128), 0)

    def body(step, carry):
        rows = block_rows(step, CHUNK)
        live = (step * CHUNK + place < len_ref[0]).astype(F32)
        for first in range(0, PAIRS, group):
            pairs = range(first, first + group)
            heads = range(2 * first, 2 * (first + group))
            cols = [slice(head * 128, (head + 1) * 128) for head in range(HEADS)]
            pq = {head: pq_ref[rows, cols[head]] for head in heads}
            pk = {head: pk_ref[rows, cols[head]] for head in heads}
            vx = {}
            for pair in pairs:
                vx[2 * pair], vx[2 * pair + 1] = value_pair(v_ref[rows, cols[pair]])
            scores = {head: nt(pq[head], pk[head]) for head in heads}
            prior = {head: state[head].astype(BF16) for head in heads}
            more = {head: tn(pk[head], vx[head]) for head in heads}
            far = {head: nn(pq[head], prior[head]) for head in heads}
            scores = {head: jnp.where(causal, scores[head], 0.0).astype(BF16) for head in heads}
            sums = {head: nn(scores[head], vx[head]) + far[head] for head in heads}
            for head in heads:
                s_ref[step, head] = prior[head]
                state[head] += more[head]
            for pair in pairs:
                one, two = sums[2 * pair], sums[2 * pair + 1]
                numer = jnp.where(low, one, swap_halves(two))
                denom = jnp.where(low, swap_halves(one), two)
                rd = live / denom
                rd_ref[rows, cols[pair]] = rd.astype(BF16)
                o_ref[rows, cols[pair]] = (numer * rd).astype(BF16)
        leave.start(step)
        leave_state(step).start()
        return carry

    lax.fori_loop(0, steps, body, 0)
    for step in range(steps):
        leave.wait(step)
        leave_state(step).wait()


def attend(lengths, pq, pk, v, group=3):
    count = v.shape[0]
    steps = count // CHUNK
    return pl.pallas_call(
        functools.partial(attend_kernel, group),
        name="attend",
        in_specs=[SMEM, VMEM, VMEM, VMEM],
        out_specs=[VMEM] + [ANY] * 3,
        out_shape=[array((count, D))] + [pltpu.HBM((count, D), BF16)] * 2 + [pltpu.HBM((steps, HEADS, 128, 128), BF16)],
        scratch_shapes=[
            pltpu.VMEM((count, D), BF16), pltpu.VMEM((steps, HEADS, 128, 128), BF16), pltpu.VMEM((HEADS, 128, 128), F32),
            row_semaphores(2, count), pltpu.SemaphoreType.DMA((steps,)),
        ],
        compiler_params=limit(10),
        cost_estimate=cost(2 * count * HEADS * 128 * 512, 20 * count * D),
    )(lengths, pq, pk, v)


def gelu_pair(f):
    low = f.astype(BF16)
    square = low * low
    bend = jnp.tanh(low * (BF16(ROOT) + BF16(ROOT * CUBE) * square))
    share = BF16(0.5) + BF16(0.5) * bend
    value = low * share
    slope = share + value * (BF16(1.0) - share) * (BF16(2 * ROOT) + BF16(6 * ROOT * CUBE) * square)
    return value, slope


def widen_kernel(source, me_ref, o_ref, tok_ref, vec_ref, *refs):
    count = len(source.arrays)
    h2_ref, g_ref, slope_ref, w_far, g_far, x1_far, w_ref, x1_ref, side_sems, sems, g_sems, x1_sems, w_sem = refs[count:]
    leave, leave_x1 = Rows([(g_ref, g_far)], g_sems), Rows([(x1_ref, x1_far)], x1_sems)
    steps = tok_ref.shape[0] // ROWS
    side = source.copies(me_ref[0], refs[:count], w_ref, side_sems, FF)
    main = source.copies(me_ref[0], refs[:count], w_ref, sems, 0, FF)
    for copy in side + main:
        copy.start()
    for copy in side:
        copy.wait()

    def middle(index, carry):
        rows = block_rows(index, 2 * ROWS)
        x1 = tok_ref[rows, :].astype(F32) + (nn(o_ref[rows, :], w_ref[:, FF:]) + vec_ref[1:2, :D])
        x1_ref[rows, :] = x1.astype(BF16)
        unit, _ = normalized(x1)
        h2_ref[rows, :] = (unit * vec_ref[6:7, :D] + vec_ref[7:8, :D]).astype(BF16)
        leave_x1.start(2 * index)
        leave_x1.start(2 * index + 1)
        return carry

    lax.fori_loop(0, steps // 2, middle, 0)
    for copy in main:
        copy.wait()
    leave_w = pltpu.make_async_copy(w_ref, w_far, w_sem)
    leave_w.start()

    def body(index, carry):
        rows = block_rows(index, 2 * ROWS)
        h2 = h2_ref[rows, :]
        for part in range(4):
            cols = slice(part * D, (part + 1) * D)
            g_ref[rows, cols], slope_ref[rows, cols] = gelu_pair(nn(h2, w_ref[:, cols]) + vec_ref[2:3, cols])
        leave.start(2 * index)
        leave.start(2 * index + 1)
        return carry

    lax.fori_loop(0, steps // 2, body, 0)
    for step in range(steps):
        leave_x1.wait(step)
        leave.wait(step)
    leave_w.wait()


def widen(me, o, tokens, vectors, source):
    count = tokens.shape[0]
    return pl.pallas_call(
        functools.partial(widen_kernel, source),
        name="widen",
        in_specs=[SMEM, VMEM, VMEM, VMEM] + source.specs(),
        out_specs=[VMEM] * 3 + [ANY] * 3,
        out_shape=[
            array((count, D)), array((count, FF)), array((count, FF)), pltpu.HBM(source.shape, BF16),
            pltpu.HBM((count, FF), BF16), pltpu.HBM((count, D), BF16),
        ],
        scratch_shapes=[
            pltpu.VMEM(source.shape, BF16), pltpu.VMEM((count, D), BF16), source.semaphores(), source.semaphores(),
            row_semaphores(1, count), row_semaphores(1, count), pltpu.SemaphoreType.DMA,
        ],
        compiler_params=limit(16),
        cost_estimate=cost(2 * count * D * 5 * D, 26 * count * D + 10 * D * D, count * FF),
    )(me, o, tokens, vectors, *source.arrays)


def column_sums(values):
    return jnp.sum(values, 0, keepdims=True)


def slope_back_kernel(source, me_ref, cot_ref, slope_ref, *refs):
    count = len(source.arrays)
    df_ref, projb_ref, fcb_ref, wp_ref, sems = refs[count:]
    copies = source.copies(me_ref[0], refs[:count], wp_ref, sems)
    for copy in copies:
        copy.start()
    projb_ref[...] = column_sums(cot_ref[...].astype(F32))
    fcb_ref[...] = jnp.zeros_like(fcb_ref)
    for copy in copies:
        copy.wait()

    def body(step, carry):
        rows = block_rows(step, 2 * ROWS)
        cot = cot_ref[rows, :]
        for part in range(4):
            cols = slice(part * D, (part + 1) * D)
            df = nt(cot, wp_ref[cols, :]).astype(BF16) * slope_ref[rows, cols]
            df_ref[rows, cols] = df
            fcb_ref[:, cols] += column_sums(df.astype(F32))
        return carry

    lax.fori_loop(0, cot_ref.shape[0] // (2 * ROWS), body, 0)


def slope_back(me, cot, slope, source):
    count = cot.shape[0]
    return pl.pallas_call(
        functools.partial(slope_back_kernel, source),
        name="slope_back",
        in_specs=[SMEM, VMEM, VMEM] + source.specs(),
        out_specs=[VMEM] * 3,
        out_shape=[array((count, FF)), array((1, D), F32), array((1, FF), F32)],
        scratch_shapes=[pltpu.VMEM(source.shape, BF16), source.semaphores()],
        compiler_params=limit(14),
        cost_estimate=cost(2 * count * D * 4 * D, 30 * count * D + 18 * D * D),
    )(me, cot, near(slope), *source.arrays)


def middle_back_kernel(
    ahead, cot_ref, df_ref, x1_far, vec_ref, w_ref, *refs
):
    away, refs = refs[:ahead], refs[ahead:]
    da_ref, do_ref, gain2_ref, bias2_ref, outb_ref, *held, x1_ref, row_sems, sems = refs
    enter = Rows([(x1_far, x1_ref)], row_sems)
    steps = cot_ref.shape[0] // ROWS
    for step in range(steps):
        enter.start(step)
    copies = [pltpu.make_async_copy(source, target, sems.at[at]) for at, (source, target) in enumerate(zip(away, held))]
    for copy in copies:
        copy.start()
    for ref in (gain2_ref, bias2_ref, outb_ref):
        ref[...] = jnp.zeros_like(ref)

    def body(index, carry):
        blocks = [2 * index, 2 * index + 1]
        rows = [block_rows(step, ROWS) for step in blocks]
        totals = [nt(df_ref[at, :], w_ref[:, :FF]) for at in rows]
        for step in blocks:
            enter.wait(step)
        das = []
        for at, total in zip(rows, totals):
            unit, scale = normalized(x1_ref[at, :].astype(F32))
            dx1 = cot_ref[at, :].astype(F32) + norm_back(total, vec_ref[6:7, :D], unit, scale)
            da = dx1.astype(BF16)
            das.append(da)
            da_ref[at, :] = da
            do_ref[at, :] = nt(da, w_ref[:, FF:]).astype(BF16)
            gain2_ref[...] += column_sums(total * unit)
        bias2_ref[...] += column_sums(totals[0]) + column_sums(totals[1])
        outb_ref[...] += column_sums(das[0].astype(F32)) + column_sums(das[1].astype(F32))
        return carry

    lax.fori_loop(0, steps // 2, body, 0)
    for copy in copies:
        copy.wait()


def middle_back(cot, df, x1, vectors, w, away):
    count = cot.shape[0]
    return pl.pallas_call(
        functools.partial(middle_back_kernel, len(away)),
        name="middle_back",
        in_specs=[VMEM] * 2 + [ANY] + [VMEM] * 2 + [ANY] * len(away),
        out_specs=[VMEM] * (5 + len(away)),
        out_shape=[array((count, D)), array((count, D))] + [array((1, D), F32)] * 3
        + [pltpu.VMEM(value.shape, BF16) for value in away],
        scratch_shapes=[pltpu.VMEM((count, D), BF16), row_semaphores(1, count), pltpu.SemaphoreType.DMA((len(away),))],
        compiler_params=limit(10),
        cost_estimate=cost(2 * count * D * 5 * D, 30 * count * D + 18 * D * D),
    )(cot, df, far(x1), vectors, near(w), *map(far, away))


def attend_back_kernel(
    first_head, group, do_ref, rd_ref, o_ref, pq_ref, pk_ref, v_ref, s_ref, q_ref, k_ref, fq, fk,
    dproj_ref, sums_ref, fmap_ref, state, gq, gk,
):
    heads_here = state.shape[0]
    width = heads_here * HD
    base = first_head // 2
    steps = do_ref.shape[0] // CHUNK
    for ref in (state, gq, gk, sums_ref):
        ref[...] = jnp.zeros_like(ref)
    ones = block_ones(4 * HD)
    halves = jnp.concatenate([ones[0:128, 0:128], ones[0:128, 0:128]], 0)
    row = lax.broadcasted_iota(jnp.int32, (CHUNK, CHUNK), 0)
    col = lax.broadcasted_iota(jnp.int32, (CHUNK, CHUNK), 1)
    causal = row >= col
    below = row <= col
    lane = lanes((CHUNK, 128))
    low = lane < HD

    def body(index, carry):
        step = steps - 1 - index
        rows = block_rows(step, CHUNK)
        for start in range(0, heads_here // 2, group):
            pairs = range(start, start + group)
            heads = range(2 * start, 2 * (start + group))
            pair_cols = {pair: slice((base + pair) * 128, (base + pair + 1) * 128) for pair in pairs}
            head_cols = {head: slice((first_head + head) * 128, (first_head + head + 1) * 128) for head in heads}
            pq = {head: pq_ref[rows, head_cols[head]] for head in heads}
            pk = {head: pk_ref[rows, head_cols[head]] for head in heads}
            scores = {head: nt(pk[head], pq[head]) for head in heads}
            numer = {p: (do_ref[rows, pair_cols[p]].astype(F32) * rd_ref[rows, pair_cols[p]].astype(F32)).astype(BF16).astype(F32) for p in pairs}
            denom = {}
            for p in pairs:
                product = numer[p] * o_ref[rows, pair_cols[p]].astype(F32)
                coarse = product.astype(BF16)
                fine = (product - coarse.astype(F32)).astype(BF16)
                denom[p] = -nn(jnp.concatenate([coarse, fine], 1), halves)
            vx = {}
            for p in pairs:
                vx[2 * p], vx[2 * p + 1] = value_pair(v_ref[rows, pair_cols[p]])
            scores = {head: jnp.where(below, scores[head], 0.0).astype(BF16) for head in heads}
            dn = {}
            for p in pairs:
                for head, top, rest in ((2 * p, numer[p], swap_halves(denom[p])), (2 * p + 1, swap_halves(numer[p]), denom[p])):
                    rounded = rest.astype(BF16).astype(F32)
                    tail = jnp.where(lane == HD, rounded, jnp.where(lane == HD + 1, rest - rounded, 0.0))
                    dn[head] = jnp.where(low, top, tail).astype(BF16)
            later = {head: state[head].astype(BF16) for head in heads}
            ds = {head: nt(dn[head], vx[head]) for head in heads}
            dst = {head: nt(vx[head], dn[head]) for head in heads}
            far_q = {head: nt(dn[head], s_ref[step, first_head + head]) for head in heads}
            far_k = {head: nt(vx[head], later[head]) for head in heads}
            far_v = {head: nn(pk[head], later[head]) for head in heads}
            dv = {head: nn(scores[head], dn[head]) + far_v[head] for head in heads}
            more = {head: tn(pq[head], dn[head]) for head in heads}
            ds = {head: jnp.where(causal, ds[head], 0.0).astype(BF16) for head in heads}
            dst = {head: jnp.where(below, dst[head], 0.0).astype(BF16) for head in heads}
            dq = {head: nn(ds[head], pk[head]) + far_q[head] for head in heads}
            dk = {head: nn(dst[head], pq[head]) + far_k[head] for head in heads}
            for head in heads:
                state[head] += more[head]
            out = {}
            for p in pairs:
                out[2, p] = jnp.where(low, dv[2 * p], swap_halves(dv[2 * p + 1])).astype(BF16)
            grads, feats, inner = {}, {}, {}
            for p in pairs:
                both = slice((base + p) * 256, (base + p + 1) * 256)
                for part, (grad, feat_ref) in enumerate(((dq, pq_ref), (dk, pk_ref))):
                    grads[part, p] = jnp.concatenate([grad[2 * p], grad[2 * p + 1]], 1)
                    feats[part, p] = feat_ref[rows, both].astype(F32)
                    inner[part, p] = nn((grads[part, p] * feats[part, p]).astype(BF16), ones)
            logits = {key: (feats[key] * (grads[key] - inner[key])).astype(BF16) for key in inner}
            for p in pairs:
                for part, (rows_ref, maps, total) in enumerate(((q_ref, fq, gq), (k_ref, fk, gk))):
                    out[part, p] = nt(logits[part, p], maps[base + p]).astype(BF16)
                    total[p] += tn(rows_ref[rows, pair_cols[p]], logits[part, p])
            for (part, p), value in out.items():
                cols = slice(part * width + p * 128, part * width + (p + 1) * 128)
                dproj_ref[rows, cols] = value
                sums_ref[:, cols] += column_sums(value.astype(F32))
        return carry

    lax.fori_loop(0, steps, body, 0)
    first = lanes((HD, 2 * HD)) < HD
    for head in range(heads_here):
        r, c = (head % 2) * HD, (head % 2) * 2 * HD
        bq = gq[head // 2, r : r + HD, c : c + 2 * HD]
        bk = gk[head // 2, r : r + HD, c : c + 2 * HD]
        fmap_ref[head * HD : (head + 1) * HD, :] = jnp.where(first, bq - swap_halves(bq), swap_halves(bk) - bk)


def attend_back(first, heads, do, rd, o, pq, pk, v, s, q, k, fq, fk, group=2):
    count = v.shape[0]
    width = heads * HD
    return pl.pallas_call(
        functools.partial(attend_back_kernel, first, group),
        name="attend_back",
        in_specs=[VMEM] * 11,
        out_specs=[VMEM] * 3,
        out_shape=[array((count, 3 * width)), array((1, 3 * width), F32), array((width, 2 * HD), F32)],
        scratch_shapes=[
            pltpu.VMEM((heads, 128, 128), F32), pltpu.VMEM((heads // 2, 128, 256), F32), pltpu.VMEM((heads // 2, 128, 256), F32),
        ],
        compiler_params=limit(12),
        cost_estimate=cost(2 * count * heads * 128 * 128 * 14, 40 * count * width),
    )(do, *map(near, (rd, o, pq, pk, v, s, q, k)), fq, fk)


def slot_of(index):
    return 2 * index if index < 4 else 2 * index - 7


def outer_rows_kernel(first, me_ref, left_ref, right_ref, out_ref):
    rows = out_ref.shape[1]
    right = right_ref[...]
    for index in range(4):
        start = pl.multiple_of((me_ref[0] ^ slot_of(first + index)) * rows, 128)
        out_ref[index] = tn(left_ref[:, pl.ds(start, rows)], right).astype(BF16)


def outer_rows(me, first, left, right):
    count, wide = left.shape
    across = right.shape[1]
    return pl.pallas_call(
        functools.partial(outer_rows_kernel, first),
        name="outer_rows",
        in_specs=[SMEM, VMEM, VMEM],
        out_specs=VMEM,
        out_shape=array((4, wide // 8, across)),
        compiler_params=limit(7),
        cost_estimate=cost(0 if first else count * wide * across, 0),
    )(me, left, right)


def outer_cols_kernel(plan, away, inputs, brought, me_ref, *refs):
    ins, refs = list(refs[:inputs]), refs[inputs:]
    sources, (send_ref, keep_ref), refs = refs[:brought], refs[brought : brought + 2], refs[brought + 2 :]
    targets, turned, refs = refs[:brought], refs[brought], refs[brought + 1 :]
    bring = [pltpu.make_async_copy(*pair, refs[-1].at[at]) for at, pair in enumerate(zip(sources, targets))]
    copies = {}
    for at, index in enumerate(away):
        held = refs[at]
        copies[index] = pltpu.make_async_copy(ins[index], held, refs[len(away)].at[at])
        copies[index].start()
        ins[index] = held
    for copy in bring:
        copy.start()
    rows = send_ref.shape[1]
    at = 0

    def by_slot(value):
        for shard in range(8):
            slot = me_ref[0] ^ shard
            turned[(slot >> 1) + 4 * (slot & 1), :, : value.shape[1]] = value[shard * rows : (shard + 1) * rows]

    for left, right in plan:
        across = ins[right].shape[1]
        if left is None:
            by_slot(ins[right][...].astype(BF16))
            keep_ref[:, :, at : at + across] = turned[0:4, :, :across]
            send_ref[:, :, at : at + across] = turned[4:8, :, :across]
            at += across
            continue
        if left in copies:
            copies[left].wait()
        by_slot(ins[left][...].T)
        whole = turned[...].reshape(8 * rows, turned.shape[2])
        for start in range(0, across, TILE):
            value = nn(whole, ins[right][:, start : start + TILE]).astype(BF16)
            keep_ref[:, :, at : at + TILE] = value[: 4 * rows].reshape(4, rows, TILE)
            send_ref[:, :, at : at + TILE] = value[4 * rows :].reshape(4, rows, TILE)
            at += TILE
    for copy in bring:
        copy.wait()


def outer_cols(me, arrays, plan, away=(), bring=()):
    across = sum(arrays[right].shape[1] for _, right in plan)
    out = array((4, D // 8, across))
    send, keep, *brought = pl.pallas_call(
        functools.partial(outer_cols_kernel, plan, away, len(arrays), len(bring)),
        name="outer_cols",
        in_specs=[SMEM] + [ANY if index in away else VMEM for index in range(len(arrays))] + [ANY] * len(bring),
        out_specs=[VMEM] * (2 + len(bring)),
        out_shape=[out, out] + [pltpu.VMEM(value.shape, BF16) for value in bring],
        scratch_shapes=[pltpu.VMEM((8, D // 8, arrays[0].shape[0]), BF16)]
        + [pltpu.VMEM(arrays[index].shape, BF16) for index in away]
        + [pltpu.SemaphoreType.DMA((max(1, len(away)),)), pltpu.SemaphoreType.DMA((max(1, len(bring)),))],
        compiler_params=limit(10),
        cost_estimate=cost(0, 0),
    )(me, *[far(value) if index in away else value for index, value in enumerate(arrays)], *map(far, bring))
    return ((send, keep), brought) if bring else (send, keep)


def input_back_kernel(source, groups, me_ref, tok_ref, da_ref, vec_ref, *refs):
    parts, refs = refs[: len(groups)], refs[len(groups) :]
    count = len(source.arrays)
    out_ref, gain1_ref, bias1_ref, w_ref, sems = refs[count:]
    copies = source.copies(me_ref[0], refs[:count], w_ref, sems)
    for copy in copies:
        copy.start()
    for ref in (gain1_ref, bias1_ref):
        ref[...] = jnp.zeros_like(ref)
    for copy in copies:
        copy.wait()

    def body(index, carry):
        rows = [block_rows(2 * index + half, ROWS) for half in range(2)]
        grads = []
        for at in rows:
            grad = None
            for (first, heads), part_ref in zip(groups, parts):
                width = heads * HD
                for part in range(3):
                    cols = slice(part * D + first * HD, part * D + (first + heads) * HD)
                    more = nt(part_ref[at, part * width : (part + 1) * width], w_ref[:, cols])
                    grad = more if grad is None else grad + more
            grads.append(grad)
        for at, grad in zip(rows, grads):
            unit, scale = normalized(tok_ref[at, :].astype(F32))
            value = da_ref[at, :].astype(F32) + norm_back(grad, vec_ref[4:5, :D], unit, scale)
            out_ref[at, :] = value.astype(BF16)
            gain1_ref[...] += column_sums(grad * unit)
        bias1_ref[...] += column_sums(grads[0]) + column_sums(grads[1])
        return carry

    lax.fori_loop(0, tok_ref.shape[0] // (2 * ROWS), body, 0)


def input_back(me, groups, parts, tokens, da, vectors, source):
    count = tokens.shape[0]
    return pl.pallas_call(
        functools.partial(input_back_kernel, source, groups),
        name="input_back",
        in_specs=[SMEM] + [VMEM] * (3 + len(parts)) + source.specs(),
        out_specs=[VMEM] * 3,
        out_shape=[array((count, D)), array((1, D), F32), array((1, D), F32)],
        scratch_shapes=[pltpu.VMEM(source.shape, BF16), source.semaphores()],
        compiler_params=limit(14),
        cost_estimate=cost(2 * count * D * 3 * D, 14 * count * D + 6 * D * D),
    )(me, tokens, da, vectors, *parts, *source.arrays)


def narrow_kernel(source, base, me_ref, g_far, x1_far, vec_ref, *refs):
    if source is None:
        w_ref, out_ref, g_ref, x1_ref, row_sems = refs
        copies = []
    else:
        count = len(source.arrays)
        out_ref, w_ref, g_ref, x1_ref, row_sems, sems = refs[count:]
        copies = source.copies(me_ref[0], refs[:count], w_ref, sems)
    steps = out_ref.shape[0] // ROWS
    rows_here = pl.ds(base, out_ref.shape[0])
    enter = Rows([(g_far.at[rows_here, :], g_ref), (x1_far.at[rows_here, :], x1_ref)], row_sems)
    for copy in copies:
        copy.start()
    for step in range(steps):
        enter.start(step)
    for copy in copies:
        copy.wait()

    def body(step, carry):
        enter.wait(step)
        rows = block_rows(step, ROWS)
        out_ref[rows, :] = (x1_ref[rows, :].astype(F32) + (nn(g_ref[rows, :], w_ref[...]) + vec_ref[3:4, :D])).astype(BF16)
        return carry

    lax.fori_loop(0, steps, body, 0)


def narrow(me, base, count, g, x1, vectors, source):
    first = isinstance(source, Source)
    return pl.pallas_call(
        functools.partial(narrow_kernel, source if first else None, base),
        name="narrow",
        in_specs=[SMEM, ANY, ANY, VMEM] + (source.specs() if first else [VMEM]),
        out_specs=[VMEM] * 2 if first else VMEM,
        out_shape=[array((count, D)), array(source.shape)] if first else array((count, D)),
        scratch_shapes=[pltpu.VMEM((count, FF), BF16), pltpu.VMEM((count, D), BF16), row_semaphores(2, count)]
        + ([source.semaphores()] if first else []),
        compiler_params=limit(10),
        cost_estimate=cost(2 * count * D * FF, 14 * count * D + 8 * D * D),
    )(me, far(g), far(x1), vectors, *(source.arrays if first else [source]))


def fold_kernel(keep_ref, arrived_ref, *outs):
    for index, out in enumerate(outs):
        out[...] = keep_ref[index] + arrived_ref[index]


def fold(keep, arrived):
    slots, rows, across = keep.shape
    return pl.pallas_call(
        fold_kernel,
        name="fold",
        in_specs=[VMEM] * 2,
        out_specs=[VMEM] * slots,
        out_shape=[array((rows, across))] * slots,
        compiler_params=limit(5),
        cost_estimate=cost(keep.size, 6 * keep.size),
    )(keep, arrived)


def total_kernel(*refs):
    *values, out = refs
    result = values[0][...].astype(F32)
    for value in values[1:]:
        result = result + value[...].astype(F32)
    out[...] = result.astype(out.dtype)


def total(*values):
    return pl.pallas_call(
        total_kernel,
        name="total",
        in_specs=[VMEM] * len(values),
        out_specs=VMEM,
        out_shape=array(values[0].shape),
        compiler_params=limit(5),
        cost_estimate=cost(4 * values[0].size, 10 * values[0].size),
    )(*values)


def cross_kernel(keep_ref, arrived_ref, send_x, send_y, top, bottom):
    half = top.shape[1]
    for outs, rows in (((top, send_x, top, send_x), slice(0, half)), ((bottom, bottom, send_y, send_y), slice(half, 2 * half))):
        for slot, out in enumerate(outs):
            out[slot // 2 if outs[0] is outs[2] else slot % 2] = keep_ref[slot, rows, :] + arrived_ref[slot, rows, :]


def cross_over(keep, arrived):
    _, rows, across = keep.shape
    return pl.pallas_call(
        cross_kernel,
        name="cross_over",
        in_specs=[VMEM] * 2,
        out_specs=[VMEM] * 4,
        out_shape=[array((2, rows // 2, across))] * 4,
        compiler_params=limit(6),
        cost_estimate=cost(keep.size, 6 * keep.size),
    )(keep, arrived)


def turn_kernel(top, bottom, over_x, over_y, send_y, send_x, mine_top, mine_bottom):
    mine_top[...] = top[0] + over_x[0]
    send_y[...] = top[1] + over_x[1]
    mine_bottom[...] = bottom[0] + over_y[0]
    send_x[...] = bottom[1] + over_y[1]


def turn_over(top, bottom, over_x, over_y):
    _, half, across = top.shape
    return pl.pallas_call(
        turn_kernel,
        name="turn_over",
        in_specs=[VMEM] * 4,
        out_specs=[VMEM] * 4,
        out_shape=[array((half, across))] * 4,
        compiler_params=limit(5),
        cost_estimate=cost(4 * half * across, 24 * half * across),
    )(top, bottom, over_x, over_y)


def halve_kernel(side_ref, top, last_y, bottom, last_x, own_ref, other_ref):
    for side, one, two in ((0, top, last_y), (1, bottom, last_x)):
        value = one[...] + two[...]

        @pl.when(side_ref[0] == side)
        def _():
            own_ref[...] = value

        @pl.when(side_ref[0] != side)
        def _():
            other_ref[...] = value


def halve(side, top, last_y, bottom, last_x):
    return pl.pallas_call(
        halve_kernel,
        name="halve",
        in_specs=[SMEM] + [VMEM] * 4,
        out_specs=[VMEM] * 2,
        out_shape=[array(top.shape)] * 2,
        compiler_params=limit(5),
        cost_estimate=cost(2 * top.size, 12 * top.size),
    )(side, top, last_y, bottom, last_x)


def stack_kernel(top, last_y, bottom, last_x, out_ref):
    half = top.shape[0]
    out_ref[:half, :] = top[...] + last_y[...]
    out_ref[half:, :] = bottom[...] + last_x[...]


def stack(top, last_y, bottom, last_x):
    half, across = top.shape
    return pl.pallas_call(
        stack_kernel,
        name="stack",
        in_specs=[VMEM] * 4,
        out_specs=VMEM,
        out_shape=array((2 * half, across)),
        compiler_params=limit(8),
        cost_estimate=cost(2 * top.size, 12 * top.size),
    )(top, last_y, bottom, last_x)


def join_kernel(side_ref, own_ref, other_ref, out_ref):
    half = own_ref.shape[0]
    out_ref[block_rows(side_ref[0], half), :] = own_ref[...].astype(F32)
    out_ref[block_rows(1 - side_ref[0], half), :] = other_ref[...].astype(F32)


def join(side, own, other):
    half, across = own.shape
    return pl.pallas_call(
        join_kernel,
        name="join",
        in_specs=[SMEM] + [VMEM] * 2,
        out_specs=VMEM,
        out_shape=array((2 * half, across), F32),
        compiler_params=limit(6),
        cost_estimate=cost(half * across, 12 * half * across),
    )(side, own, other)


def write_lines(lines, outs):
    at = 0
    for out in outs:
        size = out.shape[0]
        for start in range(0, size, 128):
            count = min(128, size - start)
            out[pl.ds(start, count)] = lines[at : at + 1, :count].reshape(count)
            at += 1


def publish_kernel(groups, side_ref, own_ref, other_ref, one_ref, two_ref, qkvw_ref, outw_ref, fmap_ref, *outs):
    half = own_ref.shape[0]
    for side, ref in ((side_ref[0], own_ref), (1 - side_ref[0], other_ref)):
        rows = block_rows(side, half)
        outw_ref[rows, :] = ref[:, :D].astype(F32)
        first, heads = groups[0]
        width = heads * HD
        for part in range(3):
            value = ref[:, D + part * width : D + (part + 1) * width]
            qkvw_ref[rows, part * D + first * HD : part * D + first * HD + width] = value.astype(F32)
    last = one_ref[...].astype(F32) + two_ref[...].astype(F32)
    first, heads = groups[1]
    width = heads * HD
    for part in range(3):
        qkvw_ref[:, part * D + first * HD : part * D + first * HD + width] = last[:, part * width : (part + 1) * width]
    fmap_ref[...] = last[:, 3 * width : 3 * width + 2 * HD]
    write_lines(last[:, 3 * width + 2 * HD :], outs)


def publish(groups, side, own, other, one, two, sizes):
    rows = one.shape[0]
    return pl.pallas_call(
        functools.partial(publish_kernel, groups),
        name="publish",
        in_specs=[SMEM] + [VMEM] * 4,
        out_specs=[VMEM] * (3 + len(sizes)),
        out_shape=[array((rows, 3 * D), F32), array((rows, D), F32), array((rows, 2 * HD), F32)] + [array((size,), F32) for size in sizes],
        compiler_params=limit(8),
        cost_estimate=cost(rows * 3 * D * 4, rows * 3 * D * 12),
    )(side, own, other, one, two)


def line_count(sizes):
    return sum(-(-size // 128) for size in sizes)


def to_lines(vector, start, size):
    lines = []
    for at in range(0, size, 128):
        count = min(128, size - at)
        line = vector[:, start + at : start + at + count]
        if count < 128:
            line = jnp.concatenate([line, jnp.zeros((1, 128 - count), F32)], 1)
        lines.append(line)
    return lines


def pack_kernel(*refs):
    *vectors, fm_ref, w_ref, out_ref = refs
    width = w_ref.shape[1]
    out_ref[:, :width] = w_ref[...]
    out_ref[:, width : width + 128] = fm_ref[...]
    lines = []
    for vector in vectors:
        size = vector.shape[0]
        lines += to_lines(vector[...].astype(F32).reshape(1, size), 0, size)
    lines += [jnp.zeros((1, 128), F32)] * (w_ref.shape[0] - len(lines))
    out_ref[:, width + 128 :] = jnp.concatenate(lines, 0).astype(BF16)


def pack(w, fm, vectors):
    rows, width = w.shape
    return pl.pallas_call(
        pack_kernel,
        name="pack",
        in_specs=[VMEM] * (len(vectors) + 2),
        out_specs=VMEM,
        out_shape=array((rows, width + 256)),
        compiler_params=limit(56),
    )(*vectors, fm, w)


def small_grads_kernel(shards, *refs):
    *vectors, out_ref = refs
    rows = out_ref.shape[0] // shards
    for shard in range(shards):
        lines = []
        for vector in vectors:
            size = vector.shape[1] // shards
            lines += to_lines(vector[...], shard * size, size)
        lines += [jnp.zeros((1, 128), F32)] * (rows - len(lines))
        out_ref[shard * rows : (shard + 1) * rows, :] = jnp.concatenate(lines, 0)


def small_grads(shards, vectors):
    return pl.pallas_call(
        functools.partial(small_grads_kernel, shards),
        name="small_grads",
        in_specs=[VMEM] * len(vectors),
        out_specs=VMEM,
        out_shape=array((D, 128), F32),
        compiler_params=limit(8),
    )(*vectors)


def small_owned_kernel(lines_ref, *outs):
    write_lines(lines_ref[...], outs)


def small_owned(lines, sizes):
    return pl.pallas_call(
        small_owned_kernel,
        name="small_owned",
        in_specs=[VMEM],
        out_specs=[VMEM] * len(sizes),
        out_shape=[array((size,), F32) for size in sizes],
        compiler_params=limit(8),
    )(lines)


GROUPS = ((0, 8), (8, 4))


def after(value, *others):
    return lax.optimization_barrier((value, *others))[0]


def exchange(value, axis, mask):
    return lax.ppermute(value, axis, [(i, i ^ mask) for i in range(lax.axis_size(axis))])


class Gather:
    def __init__(self, shard):
        self.shard, self.rows = shard, shard.shape[0]
        self.hand = by_hand(self.rows)

    def start(self, *others):
        if not self.hand:
            self.full = lax.all_gather(self.shard, "fsdp", axis=0, tiled=True)
            return ()
        shard = after(self.shard, *others) if others else self.shard
        self.over_x, self.over_y = exchange(shard, "fsdp", 2), exchange(shard, "fsdp", 4)
        self.sibling = exchange(shard, "fsdp", 1)
        return self.over_x, self.over_y

    def relay(self, *others):
        if not self.hand:
            return ()
        half = self.rows // 2
        over_x, over_y, self.sibling = lax.optimization_barrier((self.over_x, self.over_y, self.sibling, *others))[:3]
        self.pieces = over_y[:half], over_x[half:]
        self.upper, self.lower = exchange(self.pieces[0], "fsdp", 2), exchange(self.pieces[1], "fsdp", 4)
        self.shared = [((3, 0), exchange(over_x, "fsdp", 1)), ((5, 0), exchange(over_y, "fsdp", 1))]
        return self.pieces

    def settled(self):
        return [value for _, value in self.shared] if self.hand else []

    def finish(self, *others):
        if not self.hand:
            return Source([(0, 0)], [self.full], self.rows, self.full.shape[0])
        half = self.rows // 2
        upper, lower = self.upper, self.lower
        if others:
            upper, lower = lax.optimization_barrier((upper, lower, *others))[:2]
        held = [((0, 0), self.shard), ((2, 0), self.over_x), ((4, 0), self.over_y), ((1, 0), self.sibling)] + self.shared
        held += [((6, 0), upper), ((6, half), lower)]
        held += [((7, 0), exchange(upper, "fsdp", 1)), ((7, half), exchange(lower, "fsdp", 1))]
        return Source([place for place, _ in held], [part for _, part in held], self.rows, 8 * self.rows)


def by_hand(rows):
    return lax.axis_size("fsdp") == 8 and lax.axis_size("dp") == 4 and rows % 32 == 0


class Scatter:
    def __init__(self, pair):
        send, self.keep = pair
        self.arrived = exchange(send, "fsdp", 1)

    def cross(self, *others):
        send_x, send_y, self.top, self.bottom = cross_over(self.keep, after(self.arrived, *others))
        self.over_x, self.over_y = exchange(send_x, "fsdp", 2), exchange(send_y, "fsdp", 4)
        return send_x, send_y

    def turn(self, *others):
        over_x, over_y = lax.optimization_barrier((self.over_x, self.over_y, *others))[:2]
        send_y, send_x, self.top, self.bottom = turn_over(self.top, self.bottom, over_x, over_y)
        self.last_y, self.last_x = exchange(send_y, "fsdp", 4), exchange(send_x, "fsdp", 2)
        return send_y, send_x

    def finish(self, *others):
        last_y, last_x = lax.optimization_barrier((self.last_y, self.last_x, *others))[:2]
        return self.top, last_y, self.bottom, last_x

    def straight(self, *others):
        self.mine, *away = fold(self.keep, after(self.arrived, *others))
        self.moved = [exchange(value, "fsdp", mask) for value, mask in zip(away, (2, 4, 6))]
        return away

    def arrive(self, *others):
        return total(self.mine, *lax.optimization_barrier((*self.moved, *others))[:3])


class Planes:
    def __init__(self, side, values):
        self.own, self.other = halve(side, *values)
        self.moved = exchange(self.other, "dp", 1)

    def mirror(self, *others):
        self.own = self.own + after(self.moved, *others)
        self.moved = exchange(self.own, "dp", 3)
        return self.own

    def back(self, *others):
        self.own = self.own + after(self.moved, *others)
        self.moved = exchange(self.own, "dp", 1)
        return self.own

    def finish(self, *others):
        return self.own, after(self.moved, *others)


def outer(left, right):
    return tn(left, right).astype(BF16)


def on_device(
    tokens, lengths, qkv_weight, qkv_bias, out_weight, out_bias, fc_weight, fc_bias, proj_weight, proj_bias,
    norm1_gain, norm1_bias, norm2_gain, norm2_bias, feature_map, cotangent,
):
    shards = lax.axis_size("fsdp")
    me = lax.axis_index("fsdp").astype(jnp.int32).reshape(1)
    plane = lax.axis_index("dp").astype(jnp.int32).reshape(1)
    side = (plane ^ (plane >> 1)) & 1
    qkv_weight, me, side = lax.optimization_barrier((qkv_weight, me, side))
    small = [qkv_bias, out_bias, fc_bias, proj_bias, norm1_gain, norm1_bias, norm2_gain, norm2_bias]
    first = Gather(pack(qkv_weight, feature_map, small))
    second = Gather(jnp.concatenate([fc_weight, out_weight], 1))
    third = Gather(proj_weight)
    first.start()
    second.start(*first.relay())
    first_source = first.finish()
    v, pq, pk, vectors, fq, fk, h1, q, k, v_far, pq_far, pk_far = project(
        me, lengths, tokens, first_source, [value.shape[0] for value in small]
    )
    second.relay(v)
    o, o_far, rd, s = attend(lengths, pq, pk, v)
    parts = second.finish(o)
    third.start(o)
    h2, g, slope, w_fc, g_far, x1 = widen(me, o, tokens, vectors, parts)
    g = after(g, *third.relay(g))
    hand = by_hand(qkv_weight.shape[0])
    summed = lambda share: lax.psum(share.astype(BF16), "dp").astype(F32)
    over = lambda value: lax.psum_scatter(value, "fsdp", scatter_dimension=0, tiled=True)
    if hand:
        send = after(outer_rows(me, 4, g, cotangent), *third.settled())
        keep = outer_rows(me, 0, after(g, send), cotangent)
        proj_scatter = Scatter((send, keep))
        third_source = third.finish(keep)
        slope = after(slope, *proj_scatter.cross(keep))
    else:
        third_source = third.finish()
    df, projb, fcb = slope_back(me, cotangent, slope, third_source)
    if hand:
        pair, (w_fc,) = outer_cols(me, [h2, df], [(0, 1)], (), (w_fc,))
        fc_scatter = Scatter(pair)
        df = after(df, *proj_scatter.turn(pair[0]))
    da, do, gain2, bias2, outb, *held, h1_near = middle_back(
        cotangent, df, x1, vectors, w_fc, [rd, o_far, pq_far, pk_far, v_far, s, q, k, h1]
    )
    if hand:
        proj_planes = Planes(side, proj_scatter.finish(do))
        do = after(do, proj_planes.other, *fc_scatter.cross(do))
    parts, sums, maps = [], [], []
    for index, (start, heads) in enumerate(GROUPS):
        dproj, sum_grad, fmap_grad = attend_back(start, heads, do, *held, fq, fk)
        parts.append(dproj)
        sums.append(sum_grad)
        maps.append(fmap_grad)
        if hand and index == 0:
            left = after(h1_near, proj_planes.mirror(dproj), *fc_scatter.turn(dproj))
            pair = outer_cols(me, [held[1], da, left, dproj], [(0, 1), (2, 3)])
            qkv_scatter = Scatter(pair)
            fc_planes = Planes(side, fc_scatter.finish(pair[0]))
            do = after(do, fc_planes.other)
    if hand:
        tokens = after(tokens, proj_planes.back(dproj), *qkv_scatter.cross(dproj), fc_planes.mirror(dproj))
    input_grad, gain1, bias1 = input_back(me, GROUPS, parts, tokens, da, vectors, first_source)
    spread = lambda values: jnp.concatenate([
        value[:, part * heads * HD : (part + 1) * heads * HD] for part in range(3) for (_, heads), value in zip(GROUPS, values)
    ], 1)
    ordered = spread(sums)
    small = [ordered[:, : 2 * D], ordered[:, 2 * D :], outb, fcb, projb, gain1, bias1, gain2, bias2]
    table = small_grads(shards, small)
    sizes = [value.shape[1] // shards for value in small]
    if hand:
        left = after(h1_near, *qkv_scatter.turn(table), fc_planes.back(table))
        pair = outer_cols(me, [left, dproj, jnp.concatenate(maps, 0), table], [(0, 1), (None, 2), (None, 3)])
        last_scatter = Scatter(pair)
        projw_grad = join(side, *proj_planes.finish(pair[0]))
        x1 = after(x1, pair[0], projw_grad)
    if hand:
        qkv_planes = Planes(side, qkv_scatter.finish(pair[0]))
        x1 = after(x1, qkv_planes.other)
    piece, w_proj = narrow(me, 0, ROWS, g_far, x1, vectors, third_source)
    pieces = [piece]
    for base in range(ROWS, tokens.shape[0], ROWS):
        if hand and base == ROWS:
            x1 = after(x1, *last_scatter.straight(piece))
        if hand and base == 2 * ROWS:
            fcw_grad = join(side, *fc_planes.finish(pieces[-1]))
            x1 = after(x1, fcw_grad, qkv_planes.mirror(pieces[-1]))
        if hand and base == 3 * ROWS:
            share = last_scatter.arrive(pieces[-1])
            x1 = after(x1, share)
        pieces.append(narrow(me, base, ROWS, g_far, x1, vectors, w_proj))
    block_out = jnp.concatenate(pieces, 0)
    if hand:
        qkv_planes.back(pieces[-1])
        share = share + after(exchange(share, "dp", 1), pieces[-1])
        qkvw_grad, outw_grad, fmap_grad, *vectors = publish(
            GROUPS, side, *qkv_planes.finish(), share, exchange(share, "dp", 3), sizes
        )
    else:
        vectors = small_owned(lax.psum(over(table), "dp"), sizes)
    qkb, vb, outb, fcb, projb, gain1, bias1, gain2, bias2 = vectors
    if not hand:
        projw_grad = summed(over(outer(g_far, cotangent)))
        fcw_grad, outw_grad = summed(over(outer(h2, df))), summed(over(outer(o_far, da)))
        qkvw_grad, fmap_grad = summed(over(outer(h1, spread(parts)))), summed(over(jnp.concatenate(maps, 0)))
    return (
        block_out, input_grad, qkvw_grad, qkb, vb, outw_grad, outb, fcw_grad, fcb,
        projw_grad, projb, gain1, bias1, gain2, bias2, fmap_grad,
    )


def solution(mesh):
    rows = P(("dp", "fsdp"), None)
    wide = P("fsdp", None)
    flat = P("fsdp")
    in_specs = (
        rows, P(("dp", "fsdp")), wide, flat, wide, flat, wide, flat, wide, flat, flat, flat, flat, flat, wide, rows,
    )
    out_specs = (rows, rows, wide, flat, flat, wide, flat, wide, flat, wide, flat, flat, flat, flat, flat, wide)
    return jax.shard_map(on_device, mesh=mesh, in_specs=in_specs, out_specs=out_specs, check_vma=False)
```
